32 devices in a mesh: groups: 2 (over x), dom: 16 (over z, y, core).
Axes of the slice: x: 2, y: 2, z: 4, core: 2. Of those that a mesh axis runs over, the one named last changes fastest.
Arguments:
- grid_latent: bfloat16 [32768, 512], P(('groups', 'dom')), parts along dimension 0, may hold values from -6 to 6
- mesh_latent: bfloat16 [16384, 512], P(('groups', 'dom')), parts along dimension 0, may hold values from -6 to 6
- encoder_weight: bfloat16 [512, 512], replicated, may hold values from -0.25 to 0.25
- processor_weights: bfloat16 [2, 512, 512], replicated, may hold values from -0.25 to 0.25
- decoder_weight: bfloat16 [512, 512], replicated, may hold values from -0.25 to 0.25
- cotangent: bfloat16 [32768, 512], P(('groups', 'dom')), parts along dimension 0, may hold values from -6 to 6
- grid_halo_rows: int32 [16, 2, 64], P('dom'), may hold values from 0 to 1023
- encoder_neighbours: int32 [8192, 4], P('dom'), may hold values from 0 to 1151
- halo_rows: int32 [16, 2, 64], P('dom'), may hold values from 0 to 511
- far_sources: int32 [16, 16, 4], P('dom'), may hold values from 0 to 511, as said below
- mesh_neighbours: int32 [8192, 8], P('dom'), may hold values from 0 to 703, as said below
- decoder_neighbours: int32 [16384, 3], P('dom'), may hold values from 0 to 639
Outputs:
- output: bfloat16 [32768, 512], P(('groups', 'dom')), parts along dimension 0
- grid_grad: bfloat16 [32768, 512], P(('groups', 'dom')), parts along dimension 0
- mesh_grad: bfloat16 [16384, 512], P(('groups', 'dom')), parts along dimension 0
The draws below stay inside these ranges and needn't reach their ends.
There are 2 independent parts, one for each index of `groups`. The reference program is written for one: setup_inputs(seed, part) draws one part's arguments, and reference() takes and returns one part's arrays. A program takes and returns all parts, laid end to end along the dimension named above; an argument that names none is the same for every part. Nothing has to cross between parts.
Inputs may be any that keep to these rules, and one draw needn't show every extreme that they name: `far_sources`: slots j at or beyond the number of mesh nodes that p sends to r hold 0; every partition sends at least one mesh node to every partition; in every draw some partition sends 4 to every partition and some partition receives 4 from every partition. `mesh_neighbours`: the first 6 entries of a row are below 640; the last 2 are at least 640 and name only filled slots.
All inputs are finite; a program needn't handle non-finite values.
Results may differ from the reference program's by a relative error of at most 0.012.
Values may be sent and summed in bfloat16 or wider, within the bound.
No kernel may reach another device: no remote copies, remote signals or barrier semaphores. Data moves between devices by JAX's collectives and lax.ppermute only.
A program may use at most 64 MiB of HBM per device.

```python
import jax
import jax.numpy as jnp

D = 512
G_DEV = 1024
M_DEV = 512
GHALO = 64
HALO = 64
FAR_CAP = 4
ENC_DEG = 4
DEC_DEG = 3
NBRS = 8
FAR_EDGES = 2
LAYERS = 2
GRID = 16384
MESH = 8192
N_DOM = 16


def far_counts(key):
    key = jax.random.fold_in(key, 505)
    first, second, third = jax.random.split(key, 3)
    counts = jax.random.randint(first, (N_DOM, N_DOM), 1, FAR_CAP + 1)
    full_column = jax.random.randint(second, (), 0, N_DOM)
    full_row = jax.random.randint(third, (), 0, N_DOM)
    places = jnp.arange(N_DOM, dtype=jnp.int32)
    counts = jnp.where(places[None, :] == full_column, FAR_CAP, counts)
    counts = jnp.where(places[:, None] == full_row, FAR_CAP, counts)
    return counts.astype(jnp.int32)


def draw_far_sources(key, part):
    counts = far_counts(key)
    key = jax.random.fold_in(key, 7)
    picked = jax.random.randint(key, (N_DOM, N_DOM, FAR_CAP), 0, M_DEV)
    live = jnp.arange(FAR_CAP, dtype=jnp.int32)[None, None, :] < counts[:, :, None]
    return jnp.where(live, picked, 0).astype(jnp.int32)


def draw_mesh_neighbours(key, part):
    counts = far_counts(key)
    key = jax.random.fold_in(key, 8)
    first, second, third = jax.random.split(key, 3)
    local = jax.random.randint(first, (MESH, NBRS - FAR_EDGES), 0, M_DEV + 2 * HALO)
    senders = jax.random.randint(second, (MESH, FAR_EDGES), 0, N_DOM)
    owner = (jnp.arange(MESH, dtype=jnp.int32) // M_DEV)[:, None]
    available = counts[senders, owner]
    slot = jax.random.randint(third, (MESH, FAR_EDGES), 0, 1048576) % available
    far_entry = M_DEV + 2 * HALO + senders * FAR_CAP + slot
    return jnp.concatenate([local, far_entry], axis=1).astype(jnp.int32)


def with_ends(drawn, stream_key, low, top_value):
    dims = drawn.shape
    index_at = [jax.random.randint(jax.random.fold_in(stream_key, axis), (), 0, dims[axis]) for axis in range(len(dims))]
    drawn = drawn.at[tuple(index_at)].set(low)
    longest = dims.index(max(dims))
    index_at[longest] = (index_at[longest] + 1) % dims[longest]
    return drawn.at[tuple(index_at)].set(top_value)


def level_of(own_key, shape, cuts, least, largest):
    level, own = 1.0, jax.random.fold_in(own_key, 6)
    for position, blocks in cuts:
        steps = jnp.exp(jax.random.uniform(jax.random.fold_in(own, position), (blocks,), jnp.float32, least / len(cuts), largest / len(cuts)))
        level = level * jnp.repeat(steps, shape[position] // blocks).reshape([-1 if axis == position else 1 for axis in range(len(shape))])
    return level


def gaussian(stream_key, shape, spread, reach, cuts=(), kind=jnp.bfloat16):
    drawn = spread * jax.random.normal(stream_key, shape, jnp.float32)
    if cuts:
        drawn = drawn * level_of(stream_key, shape, cuts, -0.22, 0.18)
    return jnp.clip(drawn, -reach, reach).astype(kind)


def setup_inputs(seed: int = 0, part: int = 0) -> dict:
    splits = jax.random.split(jax.random.key(seed), 13)
    own_keys = jax.random.split(jax.random.fold_in(splits[12], part), 13)
    return {
        "grid_latent": gaussian(own_keys[0], (GRID, D), 1.0, 6.0, ((0, 16),)),
        "mesh_latent": gaussian(own_keys[1], (MESH, D), 1.0, 6.0, ((0, 16),)),
        "encoder_weight": gaussian(splits[2], (D, D), D ** -0.5, 0.25),
        "processor_weights": gaussian(splits[3], (LAYERS, D, D), D ** -0.5, 0.25),
        "decoder_weight": gaussian(splits[4], (D, D), D ** -0.5, 0.25),
        "cotangent": gaussian(own_keys[5], (GRID, D), 1.0, 6.0, ((0, 16),)),
        "grid_halo_rows": with_ends(jax.random.randint(splits[6], (N_DOM, 2, GHALO), 0, G_DEV), jax.random.fold_in(splits[6], 1), 0, G_DEV - 1).astype(jnp.int32),
        "encoder_neighbours": with_ends(jax.random.randint(splits[7], (MESH, ENC_DEG), 0, G_DEV + 2 * GHALO), jax.random.fold_in(splits[7], 1), 0, (G_DEV + 2 * GHALO) - 1).astype(jnp.int32),
        "halo_rows": with_ends(jax.random.randint(splits[8], (N_DOM, 2, HALO), 0, M_DEV), jax.random.fold_in(splits[8], 1), 0, M_DEV - 1).astype(jnp.int32),
        "far_sources": draw_far_sources(jax.random.fold_in(splits[12], 71), part),
        "mesh_neighbours": draw_mesh_neighbours(jax.random.fold_in(splits[12], 71), part),
        "decoder_neighbours": with_ends(jax.random.randint(splits[11], (GRID, DEC_DEG), 0, M_DEV + 2 * HALO), jax.random.fold_in(splits[11], 1), 0, (M_DEV + 2 * HALO) - 1).astype(jnp.int32),
    }


def silu_grad(value):
    sigma = jax.nn.sigmoid(value)
    return sigma * (1.0 + value * (1.0 - sigma))

def resolve(entry, rows_per_part, source_count, rim_size, lists):
    owner = (jnp.arange(entry.shape[0], dtype=jnp.int32) // rows_per_part)[:, None]
    left_part = (owner - 1) % N_DOM
    right_part = (owner + 1) % N_DOM
    from_left = left_part * source_count + lists[left_part, 1, jnp.clip(entry - source_count, 0, rim_size - 1)]
    from_right = right_part * source_count + lists[right_part, 0, jnp.clip(entry - source_count - rim_size, 0, rim_size - 1)]
    nodes = jnp.where(entry < source_count, owner * source_count + entry, jnp.where(entry < source_count + rim_size, from_left, from_right))
    return (owner, nodes.astype(jnp.int32))

def reference(grid_latent, mesh_latent, encoder_weight, processor_weights, decoder_weight, cotangent, grid_halo_rows, encoder_neighbours, halo_rows, far_sources, mesh_neighbours, decoder_neighbours):
    _, encoder_nodes = resolve(encoder_neighbours, M_DEV, G_DEV, GHALO, grid_halo_rows)
    _, decoder_nodes = resolve(decoder_neighbours, G_DEV, M_DEV, HALO, halo_rows)
    owner, near_nodes = resolve(mesh_neighbours, M_DEV, M_DEV, HALO, halo_rows)
    far_entry = jnp.maximum(mesh_neighbours - M_DEV - 2 * HALO, 0)
    far_part = jnp.minimum(far_entry // FAR_CAP, N_DOM - 1)
    far_slot = far_entry % FAR_CAP
    far_nodes = far_part * M_DEV + far_sources[far_part, owner, far_slot]
    sources = jnp.where(mesh_neighbours < M_DEV + 2 * HALO, near_nodes, far_nodes).astype(jnp.int32)
    pre_encoder = jnp.dot(grid_latent, encoder_weight, preferred_element_type=jnp.float32)
    grid_message = jax.nn.silu(pre_encoder).astype(jnp.bfloat16)
    encoder_sum = jnp.zeros((MESH, D), jnp.float32)
    for slot in range(ENC_DEG):
        encoder_sum = encoder_sum + grid_message[encoder_nodes[:, slot]].astype(jnp.float32)
    hidden = (mesh_latent.astype(jnp.float32) + encoder_sum).astype(jnp.bfloat16)
    pre_layers = []
    for layer in range(LAYERS):
        pre_layer = jnp.dot(hidden, processor_weights[layer], preferred_element_type=jnp.float32)
        message = jax.nn.silu(pre_layer).astype(jnp.bfloat16)
        gathered = jnp.zeros((MESH, D), jnp.float32)
        for slot in range(NBRS):
            gathered = gathered + message[sources[:, slot]].astype(jnp.float32)
        hidden = (hidden.astype(jnp.float32) + gathered * (1.0 / NBRS)).astype(jnp.bfloat16)
        pre_layers.append(pre_layer)
    pre_decoder = jnp.dot(hidden, decoder_weight, preferred_element_type=jnp.float32)
    decoder_message = jax.nn.silu(pre_decoder).astype(jnp.bfloat16)
    decoder_sum = jnp.zeros((GRID, D), jnp.float32)
    for slot in range(DEC_DEG):
        decoder_sum = decoder_sum + decoder_message[decoder_nodes[:, slot]].astype(jnp.float32)
    output = (grid_latent.astype(jnp.float32) + decoder_sum).astype(jnp.bfloat16)
    cot_float = cotangent.astype(jnp.float32)
    back_decoder = jnp.zeros((MESH, D), jnp.float32)
    for slot in range(DEC_DEG):
        back_decoder = back_decoder + jax.ops.segment_sum(cot_float, decoder_nodes[:, slot], num_segments=MESH)
    decoder_grad = (back_decoder * silu_grad(pre_decoder)).astype(jnp.bfloat16)
    mesh_grad = jnp.dot(decoder_grad, decoder_weight.T, preferred_element_type=jnp.float32).astype(jnp.bfloat16)
    for layer in reversed(range(LAYERS)):
        grad_float = mesh_grad.astype(jnp.float32)
        message_grad = jnp.zeros((MESH, D), jnp.float32)
        for slot in range(NBRS):
            message_grad = message_grad + jax.ops.segment_sum(grad_float, sources[:, slot], num_segments=MESH)
        message_grad = message_grad * (1.0 / NBRS)
        layer_grad = (message_grad * silu_grad(pre_layers[layer])).astype(jnp.bfloat16)
        mesh_grad = (grad_float + jnp.dot(layer_grad, processor_weights[layer].T, preferred_element_type=jnp.float32)).astype(jnp.bfloat16)
    grad_float = mesh_grad.astype(jnp.float32)
    back_encoder = jnp.zeros((GRID, D), jnp.float32)
    for slot in range(ENC_DEG):
        back_encoder = back_encoder + jax.ops.segment_sum(grad_float, encoder_nodes[:, slot], num_segments=GRID)
    encoder_grad = (back_encoder * silu_grad(pre_encoder)).astype(jnp.bfloat16)
    grid_grad = (cot_float + jnp.dot(encoder_grad, encoder_weight.T, preferred_element_type=jnp.float32)).astype(jnp.bfloat16)
    return (output, grid_grad, mesh_grad)
```

```python
import jax
import jax.numpy as jnp
from jax import lax
from jax.sharding import PartitionSpec as P


def exchange(pair):
    peers = lax.axis_size("dom")
    odd = lax.axis_index("dom") % 2 == 1
    inner = [(i, i ^ 1) for i in range(peers)]
    outer = [(i, (i + 1) % peers if i % 2 else (i - 1) % peers) for i in range(peers)]
    to_left, to_right = pair[0], pair[1]
    far_side = lax.ppermute(jnp.where(odd, to_right, to_left), "dom", outer)
    near_side = lax.ppermute(jnp.where(odd, to_left, to_right), "dom", inner)
    from_left = jnp.where(odd, near_side, far_side)
    from_right = jnp.where(odd, far_side, near_side)
    return jnp.concatenate([from_left, from_right], axis=0)


def far_exchange(blocks):
    if blocks.shape[0] > 32:
        return lax.all_to_all(blocks, "dom", split_axis=0, concat_axis=0, tiled=True)
    everything = lax.all_gather(blocks, "dom")
    return lax.dynamic_index_in_dim(everything, lax.axis_index("dom"), axis=1, keepdims=False)


def silu_grad(value):
    sigma = jax.nn.sigmoid(value)
    return sigma * (1.0 + value * (1.0 - sigma))


def block_sum(targets, values, count):
    block_rows = min(count, 512)
    starts = jnp.arange(count // block_rows, dtype=jnp.int32) * block_rows

    def one_block(start):
        wanted = start + jnp.arange(block_rows, dtype=jnp.int32)
        onehot = (wanted[:, None] == targets[None, :]).astype(values.dtype)
        return jnp.dot(onehot, values, preferred_element_type=jnp.float32)

    return lax.map(one_block, starts).reshape(count, values.shape[1])


def edge_counts(entries, columns):
    wanted = jnp.arange(columns, dtype=jnp.int32)
    return jnp.sum((entries[:, :, None] == wanted[None, None, :]).astype(jnp.int32), axis=1).astype(
        jnp.bfloat16
    )


def spread_back(counts, values):
    return lax.dot_general(
        counts, values, (((0,), (0,)), ((), ())), preferred_element_type=jnp.float32
    )


def on_device(
    grid_latent,
    mesh_latent,
    encoder_weight,
    processor_weights,
    decoder_weight,
    cotangent,
    grid_halo_rows,
    encoder_neighbours,
    halo_rows,
    far_sources,
    mesh_neighbours,
    decoder_neighbours,
):
    devices = lax.axis_size("dom")
    grid_rows, feature_width = grid_latent.shape
    mesh_rows = mesh_latent.shape[0]
    grid_rim_size = grid_halo_rows.shape[2]
    mesh_rim_size = halo_rows.shape[2]
    far_slots = far_sources.shape[2]
    degree = mesh_neighbours.shape[1]
    layer_count = processor_weights.shape[0]
    inverse_degree = 1.0 / degree
    grid_lists = grid_halo_rows[0].reshape(-1)
    rim_lists = halo_rows[0].reshape(-1)
    far_lists = far_sources[0].reshape(-1)
    near_columns = mesh_rows + 2 * mesh_rim_size
    pre_encoder = jnp.dot(grid_latent, encoder_weight, preferred_element_type=jnp.float32)
    grid_message = jax.nn.silu(pre_encoder).astype(jnp.bfloat16)
    grid_out = jnp.take(grid_message, grid_lists, axis=0).reshape(2, grid_rim_size, feature_width)
    grid_in = exchange(grid_out)
    encoder_counts = edge_counts(encoder_neighbours, grid_rows + 2 * grid_rim_size)
    grid_extended = jnp.concatenate([grid_message, grid_in], axis=0)
    encoder_sum = jnp.dot(encoder_counts, grid_extended, preferred_element_type=jnp.float32)
    hidden = (mesh_latent.astype(jnp.float32) + encoder_sum).astype(jnp.bfloat16)
    mesh_counts = edge_counts(mesh_neighbours, near_columns + devices * far_slots)
    pre_layers = []
    for layer in range(layer_count):
        weight = processor_weights[layer]
        pre_layer = jnp.dot(hidden, weight, preferred_element_type=jnp.float32)
        message = jax.nn.silu(pre_layer).astype(jnp.bfloat16)
        rim_out = jnp.take(message, rim_lists, axis=0).reshape(2, mesh_rim_size, feature_width)
        far_out = jnp.take(message, far_lists, axis=0).reshape(devices, far_slots, feature_width)
        rim_in = exchange(rim_out)
        far_in = far_exchange(far_out)
        remote = jnp.concatenate([rim_in, far_in.reshape(-1, feature_width)], axis=0)
        extended = jnp.concatenate([message, remote], axis=0)
        gathered = jnp.dot(mesh_counts, extended, preferred_element_type=jnp.float32)
        hidden = (hidden.astype(jnp.float32) + gathered * inverse_degree).astype(jnp.bfloat16)
        pre_layers.append(pre_layer)
    pre_decoder = jnp.dot(hidden, decoder_weight, preferred_element_type=jnp.float32)
    decoder_message = jax.nn.silu(pre_decoder).astype(jnp.bfloat16)
    decoder_out = jnp.take(decoder_message, rim_lists, axis=0).reshape(
        2, mesh_rim_size, feature_width
    )
    decoder_in = exchange(decoder_out)
    decoder_counts = edge_counts(decoder_neighbours, near_columns)
    mesh_extended = jnp.concatenate([decoder_message, decoder_in], axis=0)
    decoder_sum = jnp.dot(decoder_counts, mesh_extended, preferred_element_type=jnp.float32)
    output = (grid_latent.astype(jnp.float32) + decoder_sum).astype(jnp.bfloat16)
    decoder_spread = spread_back(decoder_counts, cotangent)
    decoder_returning = jnp.stack(
        [
            decoder_spread[mesh_rows : mesh_rows + mesh_rim_size],
            decoder_spread[mesh_rows + mesh_rim_size :],
        ]
    )
    decoder_returned = exchange(decoder_returning.astype(jnp.bfloat16))
    back_decoder = decoder_spread[:mesh_rows] + block_sum(
        rim_lists, decoder_returned, mesh_rows
    )
    decoder_grad = (back_decoder * silu_grad(pre_decoder)).astype(jnp.bfloat16)
    mesh_grad = jnp.dot(decoder_grad, decoder_weight.T, preferred_element_type=jnp.float32).astype(
        jnp.bfloat16
    )
    for layer in reversed(range(layer_count)):
        spread = spread_back(mesh_counts, mesh_grad)
        returning = jnp.stack(
            [
                spread[mesh_rows : mesh_rows + mesh_rim_size],
                spread[mesh_rows + mesh_rim_size : near_columns],
            ]
        )
        returned = exchange(returning.astype(jnp.bfloat16))
        far_returning = spread[near_columns:].reshape(devices, far_slots, feature_width)
        far_returned = far_exchange(far_returning.astype(jnp.bfloat16))
        message_grad = spread[:mesh_rows] + block_sum(rim_lists, returned, mesh_rows)
        message_grad = (
            message_grad + block_sum(far_lists, far_returned.reshape(-1, feature_width), mesh_rows)
        ) * inverse_degree
        layer_grad = (message_grad * silu_grad(pre_layers[layer])).astype(jnp.bfloat16)
        mesh_grad = (
            mesh_grad.astype(jnp.float32)
            + jnp.dot(layer_grad, processor_weights[layer].T, preferred_element_type=jnp.float32)
        ).astype(jnp.bfloat16)
    encoder_spread = spread_back(encoder_counts, mesh_grad)
    grid_returning = jnp.stack(
        [
            encoder_spread[grid_rows : grid_rows + grid_rim_size],
            encoder_spread[grid_rows + grid_rim_size :],
        ]
    )
    grid_returned = exchange(grid_returning.astype(jnp.bfloat16))
    back_encoder = encoder_spread[:grid_rows] + block_sum(
        grid_lists, grid_returned, grid_rows
    )
    encoder_grad = (back_encoder * silu_grad(pre_encoder)).astype(jnp.bfloat16)
    grid_grad = (
        cotangent.astype(jnp.float32)
        + jnp.dot(encoder_grad, encoder_weight.T, preferred_element_type=jnp.float32)
    ).astype(jnp.bfloat16)
    return (output, grid_grad, mesh_grad)


def solution(mesh):
    in_specs = (
        P(("groups", "dom"), None),
        P(("groups", "dom"), None),
        P(),
        P(),
        P(),
        P(("groups", "dom"), None),
        P("dom", None, None),
        P("dom", None),
        P("dom", None, None),
        P("dom", None, None),
        P("dom", None),
        P("dom", None),
    )
    out_specs = (P(("groups", "dom"), None), P(("groups", "dom"), None), P(("groups", "dom"), None))
    return jax.shard_map(
        on_device, mesh=mesh, in_specs=in_specs, out_specs=out_specs, check_vma=False
    )
```

```python
import jax
import jax.numpy as jnp
from jax import lax
from jax.sharding import PartitionSpec as P


def exchange(pair):
    peers = lax.axis_size("dom")
    odd = lax.axis_index("dom") % 2 == 1
    inner = [(i, i ^ 1) for i in range(peers)]
    outer = [[i, (i + 1) % peers] for i in range(1, peers, 2)]
    to_left, to_right = pair[0], pair[1]
    both = lax.all_gather(jnp.where(odd, to_right, to_left), "dom", axis_index_groups=outer)
    far_side = jnp.where(odd, both[1], both[0])
    near_side = lax.ppermute(jnp.where(odd, to_left, to_right), "dom", inner)
    from_left = jnp.where(odd, near_side, far_side)
    from_right = jnp.where(odd, far_side, near_side)
    return jnp.concatenate([from_left, from_right], axis=0)


def far_exchange(blocks):
    return lax.all_to_all(blocks, "dom", split_axis=0, concat_axis=0, tiled=True)


def silu_grad(value):
    sigma = jax.nn.sigmoid(value)
    return sigma * (1.0 + value * (1.0 - sigma))


def block_sum(targets, values, count):
    block_rows = min(count, 512)
    starts = jnp.arange(count // block_rows, dtype=jnp.int32) * block_rows

    def one_block(start):
        wanted = start + jnp.arange(block_rows, dtype=jnp.int32)
        onehot = (wanted[:, None] == targets[None, :]).astype(values.dtype)
        return jnp.dot(onehot, values, preferred_element_type=jnp.float32)

    return lax.map(one_block, starts).reshape(count, values.shape[1])


def edge_counts(entries, columns):
    wanted = jnp.arange(columns, dtype=jnp.int32)
    return jnp.sum((entries[:, :, None] == wanted[None, None, :]).astype(jnp.int32), axis=1).astype(
        jnp.bfloat16
    )


def spread_back(counts, values):
    return lax.dot_general(
        counts, values, (((0,), (0,)), ((), ())), preferred_element_type=jnp.float32
    )


def on_device(
    grid_latent,
    mesh_latent,
    encoder_weight,
    processor_weights,
    decoder_weight,
    cotangent,
    grid_halo_rows,
    encoder_neighbours,
    halo_rows,
    far_sources,
    mesh_neighbours,
    decoder_neighbours,
):
    devices = lax.axis_size("dom")
    grid_rows, feature_width = grid_latent.shape
    mesh_rows = mesh_latent.shape[0]
    grid_rim_size = grid_halo_rows.shape[2]
    mesh_rim_size = halo_rows.shape[2]
    far_slots = far_sources.shape[2]
    degree = mesh_neighbours.shape[1]
    layer_count = processor_weights.shape[0]
    inverse_degree = 1.0 / degree
    grid_lists = grid_halo_rows[0].reshape(-1)
    rim_lists = halo_rows[0].reshape(-1)
    far_lists = far_sources[0].reshape(-1)
    near_columns = mesh_rows + 2 * mesh_rim_size
    pre_encoder = jnp.dot(grid_latent, encoder_weight, preferred_element_type=jnp.float32)
    grid_message = jax.nn.silu(pre_encoder).astype(jnp.bfloat16)
    grid_out = jnp.take(grid_message, grid_lists, axis=0).reshape(2, grid_rim_size, feature_width)
    grid_in = exchange(grid_out)
    encoder_counts = edge_counts(encoder_neighbours, grid_rows + 2 * grid_rim_size)
    grid_extended = jnp.concatenate([grid_message, grid_in], axis=0)
    encoder_sum = jnp.dot(encoder_counts, grid_extended, preferred_element_type=jnp.float32)
    hidden = (mesh_latent.astype(jnp.float32) + encoder_sum).astype(jnp.bfloat16)
    mesh_counts = edge_counts(mesh_neighbours, near_columns + devices * far_slots)
    pre_layers = []
    for layer in range(layer_count):
        weight = processor_weights[layer]
        pre_layer = jnp.dot(hidden, weight, preferred_element_type=jnp.float32)
        message = jax.nn.silu(pre_layer).astype(jnp.bfloat16)
        rim_out = jnp.take(message, rim_lists, axis=0).reshape(2, mesh_rim_size, feature_width)
        far_out = jnp.take(message, far_lists, axis=0).reshape(devices, far_slots, feature_width)
        rim_in = exchange(rim_out)
        far_in = far_exchange(far_out)
        remote = jnp.concatenate([rim_in, far_in.reshape(-1, feature_width)], axis=0)
        extended = jnp.concatenate([message, remote], axis=0)
        gathered = jnp.dot(mesh_counts, extended, preferred_element_type=jnp.float32)
        hidden = (hidden.astype(jnp.float32) + gathered * inverse_degree).astype(jnp.bfloat16)
        pre_layers.append(pre_layer)
    pre_decoder = jnp.dot(hidden, decoder_weight, preferred_element_type=jnp.float32)
    decoder_message = jax.nn.silu(pre_decoder).astype(jnp.bfloat16)
    decoder_out = jnp.take(decoder_message, rim_lists, axis=0).reshape(
        2, mesh_rim_size, feature_width
    )
    decoder_in = exchange(decoder_out)
    decoder_counts = edge_counts(decoder_neighbours, near_columns)
    mesh_extended = jnp.concatenate([decoder_message, decoder_in], axis=0)
    decoder_sum = jnp.dot(decoder_counts, mesh_extended, preferred_element_type=jnp.float32)
    output = (grid_latent.astype(jnp.float32) + decoder_sum).astype(jnp.bfloat16)
    decoder_spread = spread_back(decoder_counts, cotangent)
    decoder_returning = jnp.stack(
        [
            decoder_spread[mesh_rows : mesh_rows + mesh_rim_size],
            decoder_spread[mesh_rows + mesh_rim_size :],
        ]
    )
    decoder_returned = exchange(decoder_returning.astype(jnp.bfloat16))
    back_decoder = decoder_spread[:mesh_rows] + block_sum(
        rim_lists, decoder_returned, mesh_rows
    )
    decoder_grad = (back_decoder * silu_grad(pre_decoder)).astype(jnp.bfloat16)
    mesh_grad = jnp.dot(decoder_grad, decoder_weight.T, preferred_element_type=jnp.float32).astype(
        jnp.bfloat16
    )
    for layer in reversed(range(layer_count)):
        spread = spread_back(mesh_counts, mesh_grad)
        returning = jnp.stack(
            [
                spread[mesh_rows : mesh_rows + mesh_rim_size],
                spread[mesh_rows + mesh_rim_size : near_columns],
            ]
        )
        returned = exchange(returning.astype(jnp.bfloat16))
        far_returning = spread[near_columns:].reshape(devices, far_slots, feature_width)
        far_returned = far_exchange(far_returning.astype(jnp.bfloat16))
        message_grad = spread[:mesh_rows] + block_sum(rim_lists, returned, mesh_rows)
        message_grad = (
            message_grad + block_sum(far_lists, far_returned.reshape(-1, feature_width), mesh_rows)
        ) * inverse_degree
        layer_grad = (message_grad * silu_grad(pre_layers[layer])).astype(jnp.bfloat16)
        mesh_grad = (
            mesh_grad.astype(jnp.float32)
            + jnp.dot(layer_grad, processor_weights[layer].T, preferred_element_type=jnp.float32)
        ).astype(jnp.bfloat16)
    encoder_spread = spread_back(encoder_counts, mesh_grad)
    grid_returning = jnp.stack(
        [
            encoder_spread[grid_rows : grid_rows + grid_rim_size],
            encoder_spread[grid_rows + grid_rim_size :],
        ]
    )
    grid_returned = exchange(grid_returning.astype(jnp.bfloat16))
    back_encoder = encoder_spread[:grid_rows] + block_sum(
        grid_lists, grid_returned, grid_rows
    )
    encoder_grad = (back_encoder * silu_grad(pre_encoder)).astype(jnp.bfloat16)
    grid_grad = (
        cotangent.astype(jnp.float32)
        + jnp.dot(encoder_grad, encoder_weight.T, preferred_element_type=jnp.float32)
    ).astype(jnp.bfloat16)
    return (output, grid_grad, mesh_grad)


def solution(mesh):
    in_specs = (
        P(("groups", "dom"), None),
        P(("groups", "dom"), None),
        P(),
        P(),
        P(),
        P(("groups", "dom"), None),
        P("dom", None, None),
        P("dom", None),
        P("dom", None, None),
        P("dom", None, None),
        P("dom", None),
        P("dom", None),
    )
    out_specs = (P(("groups", "dom"), None), P(("groups", "dom"), None), P(("groups", "dom"), None))
    return jax.shard_map(
        on_device, mesh=mesh, in_specs=in_specs, out_specs=out_specs, check_vma=False
    )
```

```python
import functools

import jax
import jax.numpy as jnp
from jax import lax
from jax.experimental import pallas as pl
from jax.experimental.pallas import tpu as pltpu
from jax.sharding import PartitionSpec as P

BF = jnp.bfloat16
F32 = jnp.float32
VMEM_LIMIT = 24 * 1024 * 1024


def mm(a, b):
    return jnp.dot(a, b, preferred_element_type=F32)


def mm_t(a, b):
    return lax.dot_general(a, b, (((1,), (1,)), ((), ())), preferred_element_type=F32)


def silu_pair(value):
    sigma = 1.0 / (1.0 + jnp.exp(-value))
    message = value * sigma
    return message, sigma + message * (1.0 - sigma)


def pick(rows, wanted):
    places = lax.broadcasted_iota(jnp.int32, (rows, wanted.shape[1]), 0)
    return (places == wanted).astype(F32).astype(BF)


def counts(entries, first, columns):
    rows, degree = entries.shape
    places = lax.broadcasted_iota(jnp.int32, (rows, columns), 1) + first
    total = jnp.zeros((rows, columns), F32)
    for k in range(degree):
        total = total + (places == entries[:, k : k + 1]).astype(F32)
    return total.astype(BF)


def call(body, out_shapes, flops, *args, scratch=()):
    shapes = [jax.ShapeDtypeStruct(s, t) for s, t in out_shapes]
    size = sum(a.size * a.dtype.itemsize for a in args)
    size += sum(s.size * s.dtype.itemsize for s in shapes)
    return pl.pallas_call(
        body,
        out_shape=shapes,
        in_specs=[pl.BlockSpec(memory_space=pltpu.VMEM) for _ in args],
        out_specs=[pl.BlockSpec(memory_space=pltpu.VMEM) for _ in shapes],
        scratch_shapes=list(scratch),
        compiler_params=pltpu.CompilerParams(vmem_limit_bytes=VMEM_LIMIT),
        cost_estimate=pl.CostEstimate(flops=flops, bytes_accessed=size, transcendentals=0),
    )(*args)


def grid_send(latent, lists, outer, inner):
    half = outer.shape[0]
    chosen = pick(latent.shape[0], lists[...]).T
    rows = mm(chosen, latent[...]).astype(BF)
    outer[...] = rows[:half]
    inner[...] = rows[half:]


def encoder_local(latent, weight, mesh, entries, lists, near, rim, rim_t, slope, chosen, chosen_t):
    grid_rows = latent.shape[0]
    message, gradient = silu_pair(mm(latent[...], weight[...]))
    slope[...] = gradient.astype(BF)
    own = counts(entries[...], 0, grid_rows)
    near[...] = mesh[...].astype(F32) + mm(own, message.astype(BF))
    side = counts(entries[...], grid_rows, rim.shape[1])
    rim[...] = side
    rim_t[...] = side.T
    selected = pick(mesh.shape[0], lists[...])
    chosen[...] = selected
    chosen_t[...] = selected.T


def split_far(far, rows, scratch):
    scratch[...] = rows
    for peer in range(far.shape[0]):
        far[peer] = scratch[peer * far.shape[1] : (peer + 1) * far.shape[1]].astype(BF)


def first_hidden(near, rim, outer_in, inner_in, encoder, weight, chosen_t, hidden, message, slope, outer, inner, far, scratch):
    half = outer_in.shape[0]
    arrived = jnp.concatenate([outer_in[...], inner_in[...]], axis=0)
    far_message = silu_pair(mm(arrived, encoder[...]))[0].astype(BF)
    state = (near[...] + mm(rim[...], far_message)).astype(BF)
    hidden[...] = state
    value, gradient = silu_pair(mm(state, weight[...]))
    value = value.astype(BF)
    message[...] = value
    slope[...] = gradient
    slots = far.shape[0] * far.shape[1]
    rows = mm(chosen_t[...], value)
    outer[...] = rows[:half].astype(BF)
    inner[...] = rows[half : 2 * half].astype(BF)
    split_far(far, rows[2 * half : 2 * half + slots], scratch)


def mesh_tables(entries, own, rim, far, back_t):
    rows = own.shape[0]
    width = rim.shape[1]
    own[...] = counts(entries[...], 0, rows)
    side = counts(entries[...], rows, width)
    distant = counts(entries[...], rows + width, back_t.shape[0] - width)
    rim[...] = side
    far[...] = distant[:, : far.shape[1]]
    back_t[:width] = side.T
    back_t[width:] = distant.T


def decoder_back(entries, cotangent, own, rim, near, outer, inner):
    rows = near.shape[0]
    half = outer.shape[0]
    mine = counts(entries[...], 0, rows)
    side = counts(entries[...], rows, 2 * half)
    own[...] = mine
    rim[...] = side
    grads = cotangent[...]
    near[...] = mm(mine.T, grads)
    back = mm(side.T, grads).astype(BF)
    outer[...] = back[:half]
    inner[...] = back[half:]


def layer_local(hidden, own, message, near, *, scale):
    near[...] = hidden[...].astype(F32) + scale * mm(own[...], message[...])


def join(near, rim, far, outer_in, inner_in, far_in, scale):
    arrived = jnp.concatenate([outer_in, inner_in], axis=0)
    total = mm(rim[...], arrived) + mm(far[...], far_in[...])
    return (near[...] + scale * total).astype(BF)


def next_hidden(near, rim, far_counts, outer_in, inner_in, far_in, weight, chosen_t, outer_extra, inner_extra,
                hidden, message, slope, outer, inner, far, scratch, *, scale):
    half = outer_in.shape[0]
    state = join(near, rim, far_counts, outer_in[...], inner_in[...], far_in, scale)
    hidden[...] = state
    value, gradient = silu_pair(mm(state, weight[...]))
    value = value.astype(BF)
    message[...] = value
    slope[...] = gradient
    slots = far.shape[0] * far.shape[1]
    rows = mm(chosen_t[...], value)
    outer[:half] = rows[:half].astype(BF)
    inner[:half] = rows[half : 2 * half].astype(BF)
    outer[half:] = outer_extra[...]
    inner[half:] = inner_extra[...]
    split_far(far, rows[2 * half : 2 * half + slots], scratch)


def turn(near, rim, far_counts, outer_in, inner_in, far_in, weight, chosen, chosen_t, back_t, back_near,
         message, grad, outer, inner, far, scratch, *, scale):
    half = outer_in.shape[0] // 2
    state = join(near, rim, far_counts, outer_in[:half], inner_in[:half], far_in, scale)
    value, gradient = silu_pair(mm(state, weight[...]))
    value = value.astype(BF)
    message[...] = value
    returned = jnp.concatenate([outer_in[half:], inner_in[half:]], axis=0)
    back = back_near[...] + mm(chosen[:, : 2 * half], returned)
    change = mm_t((back * gradient).astype(BF), weight[...]).astype(BF)
    grad[...] = change
    slots = far.shape[0] * far.shape[1]
    rows = mm(back_t[...], change)
    outer[:half] = rows[:half].astype(BF)
    inner[:half] = rows[half : 2 * half].astype(BF)
    split_far(far, rows[2 * half : 2 * half + slots], scratch)
    rim_rows = mm(chosen_t[: 2 * half], value).astype(BF)
    outer[half:] = rim_rows[:half]
    inner[half:] = rim_rows[half:]


def back_local(own, grad, near):
    near[...] = lax.dot_general(
        own[...], grad[...], (((0,), (0,)), ((), ())), preferred_element_type=F32
    )


def layer_back(near, chosen, returned, far_in, slope, weight, grad, scale):
    width = returned.shape[0]
    total = near[...] + mm(chosen[:, :width], returned)
    total = total + mm(chosen[:, width : width + far_in.shape[0]], far_in[...])
    change = (total * scale * slope[...]).astype(BF)
    return (grad[...].astype(F32) + mm_t(change, weight[...])).astype(BF)


def middle_back(near, chosen, outer_in, inner_in, far_in, slope, weight, grad, back_t,
                new_grad, outer, inner, far, scratch, *, scale):
    half = outer.shape[0]
    returned = jnp.concatenate([outer_in[:half], inner_in[:half]], axis=0)
    change = layer_back(near, chosen, returned, far_in, slope, weight, grad, scale)
    new_grad[...] = change
    slots = far.shape[0] * far.shape[1]
    rows = mm(back_t[...], change)
    outer[...] = rows[:half].astype(BF)
    inner[...] = rows[half : 2 * half].astype(BF)
    split_far(far, rows[2 * half : 2 * half + slots], scratch)


def last_back(near, chosen, outer_in, inner_in, far_in, slope, weight, grad, grid_rim_t,
              new_grad, outer, inner, *, scale):
    half = outer.shape[0]
    returned = jnp.concatenate([outer_in[...], inner_in[...]], axis=0)
    change = layer_back(near, chosen, returned, far_in, slope, weight, grad, scale)
    new_grad[...] = change
    rows = mm(grid_rim_t[...], change).astype(BF)
    outer[...] = rows[:half]
    inner[...] = rows[half:]


def decode(latent, own, rim, message, outer_in, inner_in, output):
    half = outer_in.shape[0] // 2
    arrived = jnp.concatenate([outer_in[half:], inner_in[half:]], axis=0)
    total = mm(own[...], message[...]) + mm(rim[...], arrived)
    output[...] = (latent[...].astype(F32) + total).astype(BF)


def grid_local(entries, grad, near):
    own = counts(entries[...], 0, near.shape[0])
    near[...] = lax.dot_general(own, grad[...], (((0,), (0,)), ((), ())), preferred_element_type=F32)


def grid_back(near, lists, outer_in, inner_in, slope, weight, cotangent, output):
    returned = jnp.concatenate([outer_in[...], inner_in[...]], axis=0)
    total = near[...] + mm(pick(near.shape[0], lists[...]), returned)
    change = (total * slope[...].astype(F32)).astype(BF)
    output[...] = (cotangent[...].astype(F32) + mm_t(change, weight[...])).astype(BF)


def swap(outer, inner):
    peers = lax.axis_size("dom")
    across = [(i, (i + 1) % peers if i % 2 else (i - 1) % peers) for i in range(peers)]
    within = [(i, i ^ 1) for i in range(peers)]
    return lax.ppermute(outer, "dom", across), lax.ppermute(inner, "dom", within)


def spread(blocks):
    out = lax.all_to_all(blocks, "dom", split_axis=0, concat_axis=0, tiled=True)
    return out.reshape(-1, blocks.shape[2])


def on_device(
    grid_latent,
    mesh_latent,
    encoder_weight,
    processor_weights,
    decoder_weight,
    cotangent,
    grid_halo_rows,
    encoder_neighbours,
    halo_rows,
    far_sources,
    mesh_neighbours,
    decoder_neighbours,
):
    devices = lax.axis_size("dom")
    grid_rows, width = grid_latent.shape
    mesh_rows = mesh_latent.shape[0]
    ghalo = grid_halo_rows.shape[2]
    halo = halo_rows.shape[2]
    cap = far_sources.shape[2]
    slots = devices * cap
    padded = -(-slots // 128) * 128
    scale = 1.0 / mesh_neighbours.shape[1]
    odd = lax.axis_index("dom") % 2 == 1

    def in_order(lists):
        return jnp.where(odd, lists[0, ::-1], lists[0]).reshape(1, -1)

    def remap(entries, rows, size):
        swapped = jnp.where(entries < rows + size, entries + size, entries - size)
        near = (entries < rows) | (entries >= rows + 2 * size)
        return jnp.where(near | jnp.logical_not(odd), entries, swapped)

    def square(rows, depth):
        return 2 * rows * depth * width

    grid_lists = in_order(grid_halo_rows)
    outer, inner = call(
        grid_send, [((ghalo, width), BF)] * 2, square(2 * ghalo, grid_rows), grid_latent, grid_lists
    )
    outer_in, inner_in = swap(outer, inner)

    mesh_lists = jnp.concatenate(
        [in_order(halo_rows), far_sources[0].reshape(1, -1), jnp.full((1, padded - slots), -1, jnp.int32)], axis=1
    )
    listed = 2 * halo + padded
    encoder_entries = remap(encoder_neighbours, grid_rows, ghalo)
    near, grid_rim, grid_rim_t, grid_slope, chosen, chosen_t = call(
        encoder_local,
        [
            ((mesh_rows, width), F32),
            ((mesh_rows, 2 * ghalo), BF),
            ((2 * ghalo, mesh_rows), BF),
            ((grid_rows, width), BF),
            ((mesh_rows, listed), BF),
            ((listed, mesh_rows), BF),
        ],
        square(grid_rows, width) + square(mesh_rows, grid_rows),
        grid_latent, encoder_weight, mesh_latent, encoder_entries, mesh_lists,
    )

    far_shape = ((devices, cap, width), BF)
    state_shape = ((mesh_rows, width), BF)
    total_shape = ((mesh_rows, width), F32)
    rim_shape = ((halo, width), BF)
    wide_shape = ((2 * halo, width), BF)
    staging = [pltpu.VMEM((slots, width), F32)]
    step_flops = 3 * square(mesh_rows, width)
    hidden, message, slope_0, outer, inner, far = call(
        first_hidden,
        [state_shape, state_shape, total_shape, rim_shape, rim_shape, far_shape],
        step_flops,
        near, grid_rim, outer_in, inner_in, encoder_weight, processor_weights[0], chosen_t,
        scratch=staging,
    )
    outer_in, inner_in = swap(outer, inner)
    far_in = spread(far)

    mesh_entries = remap(mesh_neighbours, mesh_rows, halo)
    own, rim, far_counts, back_t = call(
        mesh_tables,
        [
            ((mesh_rows, mesh_rows), BF),
            ((mesh_rows, 2 * halo), BF),
            ((mesh_rows, slots), BF),
            ((listed, mesh_rows), BF),
        ],
        10 * mesh_rows * listed,
        mesh_entries,
    )
    local = functools.partial(layer_local, scale=scale)
    (near,) = call(local, [total_shape], square(mesh_rows, mesh_rows), hidden, own, message)
    decoder_entries = remap(decoder_neighbours, mesh_rows, halo)
    grid_own, decoder_rim, decoder_near, outer_back, inner_back = call(
        decoder_back,
        [
            ((grid_rows, mesh_rows), BF),
            ((grid_rows, 2 * halo), BF),
            total_shape,
            rim_shape,
            rim_shape,
        ],
        2 * square(grid_rows, mesh_rows),
        decoder_entries, cotangent,
    )
    hidden, message, slope_1, outer, inner, far = call(
        functools.partial(next_hidden, scale=scale),
        [state_shape, state_shape, total_shape, wide_shape, wide_shape, far_shape],
        step_flops,
        near, rim, far_counts, outer_in, inner_in, far_in, processor_weights[1], chosen_t, outer_back, inner_back,
        scratch=staging,
    )
    outer_in, inner_in = swap(outer, inner)
    far_in = spread(far)
    (near,) = call(local, [total_shape], square(mesh_rows, mesh_rows), hidden, own, message)
    message, grad, outer, inner, far = call(
        functools.partial(turn, scale=scale),
        [state_shape, state_shape, wide_shape, wide_shape, far_shape],
        2 * step_flops,
        near, rim, far_counts, outer_in, inner_in, far_in, decoder_weight, chosen, chosen_t, back_t, decoder_near,
        scratch=staging,
    )
    outer_in, inner_in = swap(outer, inner)
    far_in = spread(far)
    (near,) = call(back_local, [total_shape], square(mesh_rows, mesh_rows), own, grad)
    outer_decoder, inner_decoder = outer_in, inner_in
    grad, outer, inner, far = call(
        functools.partial(middle_back, scale=scale),
        [state_shape, rim_shape, rim_shape, far_shape],
        step_flops,
        near, chosen, outer_in, inner_in, far_in, slope_1, processor_weights[1], grad, back_t,
        scratch=staging,
    )
    outer_in, inner_in = swap(outer, inner)
    far_in = spread(far)
    (near,) = call(back_local, [total_shape], square(mesh_rows, mesh_rows), own, grad)
    (output,) = call(
        decode,
        [((grid_rows, width), BF)],
        square(grid_rows, mesh_rows),
        grid_latent, grid_own, decoder_rim, message, outer_decoder, inner_decoder,
    )
    mesh_grad, outer, inner = call(
        functools.partial(last_back, scale=scale),
        [state_shape, ((ghalo, width), BF), ((ghalo, width), BF)],
        step_flops,
        near, chosen, outer_in, inner_in, far_in, slope_0, processor_weights[0], grad, grid_rim_t,
    )
    outer_in, inner_in = swap(outer, inner)
    (near,) = call(
        grid_local, [((grid_rows, width), F32)], square(mesh_rows, grid_rows), encoder_entries, mesh_grad
    )
    (grid_grad,) = call(
        grid_back,
        [((grid_rows, width), BF)],
        square(grid_rows, width),
        near, grid_lists, outer_in, inner_in, grid_slope, encoder_weight, cotangent,
    )
    return (output, grid_grad, mesh_grad)


def solution(mesh):
    in_specs = (
        P(("groups", "dom"), None),
        P(("groups", "dom"), None),
        P(),
        P(),
        P(),
        P(("groups", "dom"), None),
        P("dom", None, None),
        P("dom", None),
        P("dom", None, None),
        P("dom", None, None),
        P("dom", None),
        P("dom", None),
    )
    out_specs = (P(("groups", "dom"), None), P(("groups", "dom"), None), P(("groups", "dom"), None))
    return jax.shard_map(
        on_device, mesh=mesh, in_specs=in_specs, out_specs=out_specs, check_vma=False
    )
```

```python
import functools

import jax
import jax.numpy as jnp
from jax import lax
from jax.experimental import pallas as pl
from jax.experimental.pallas import tpu as pltpu
from jax.sharding import PartitionSpec as P

BF = jnp.bfloat16
F32 = jnp.float32
VMEM_LIMIT = 24 * 1024 * 1024
PLANE = 4
STAGED = 16


def mm(a, b):
    return jnp.dot(a, b, preferred_element_type=F32)


def mm_t(a, b):
    return lax.dot_general(a, b, (((1,), (1,)), ((), ())), preferred_element_type=F32)


def t_mm(a, b):
    return lax.dot_general(a, b, (((0,), (0,)), ((), ())), preferred_element_type=F32)


def silu_pair(value):
    sigma = 0.5 + 0.5 * jnp.tanh(0.5 * value)
    message = value * sigma
    return message, sigma + message * (1.0 - sigma)


def pick(rows, wanted):
    places = lax.broadcasted_iota(jnp.int32, (rows, wanted.shape[1]), 0)
    return (places == wanted).astype(F32).astype(BF)


def counts_t(columns, first, entries):
    degree, rows = entries.shape
    places = lax.broadcasted_iota(jnp.int32, (columns, rows), 0) + first
    total = jnp.zeros((columns, rows), F32)
    for k in range(degree):
        total = total + (places == entries[k : k + 1]).astype(F32)
    return total.astype(BF)


def side_swap(entries, rows, size, me):
    swapped = jnp.where(entries < rows + size, entries + size, entries - size)
    rim = (entries >= rows) & (entries < rows + 2 * size)
    return jnp.where(rim & (me % 2 == 1), swapped, entries)


def pair_order(lists, me):
    left, right = lists[0, 0:1], lists[0, 1:2]
    odd = me % 2
    return left + odd * (right - left), right + odd * (left - right)


def by_stage(x, devices):
    return (x % PLANE) * (devices // PLANE) + x // PLANE


def call(body, out_shapes, flops, *args, scalars=0):
    shapes = [jax.ShapeDtypeStruct(s, t) for s, t in out_shapes]
    size = sum(a.size * a.dtype.itemsize for a in args)
    size += sum(s.size * s.dtype.itemsize for s in shapes)
    specs = [pl.BlockSpec(memory_space=pltpu.SMEM) for _ in range(scalars)]
    specs += [pl.BlockSpec(memory_space=pltpu.VMEM) for _ in args[scalars:]]
    return pl.pallas_call(
        body,
        out_shape=shapes,
        in_specs=specs,
        out_specs=[pl.BlockSpec(memory_space=pltpu.VMEM) for _ in shapes],
        compiler_params=pltpu.CompilerParams(vmem_limit_bytes=VMEM_LIMIT),
        cost_estimate=pl.CostEstimate(flops=flops, bytes_accessed=size, transcendentals=0),
    )(*args)


def grid_send(me, latent, lists, outer, inner):
    wanted_outer, wanted_inner = pair_order(lists, me[0])
    values = latent[...]
    outer[...] = t_mm(pick(latent.shape[0], wanted_outer), values).astype(BF)
    inner[...] = t_mm(pick(latent.shape[0], wanted_inner), values).astype(BF)


def encoder_local(me, latent, weight, mesh, entries, near, own_t, rim_t, slope, *, size):
    rows = latent.shape[0]
    message, gradient = silu_pair(mm(latent[...], weight[...]))
    slope[...] = gradient.astype(BF)
    columns = side_swap(entries[...], rows, size, me[0])
    own = counts_t(rows, 0, columns)
    own_t[...] = own
    rim_t[...] = counts_t(2 * size, rows, columns)
    near[...] = mesh[...].astype(F32) + t_mm(own, message.astype(BF))


def list_tables(me, lists, far_lists, send, receive, *, rows):
    size = lists.shape[2]
    cap, devices = far_lists.shape
    outer, inner = pair_order(lists, me[0])
    rim = [pick(rows, outer), pick(rows, inner)]
    for k in range(2):
        send[:, k * size : (k + 1) * size] = rim[k]
        receive[:, k * size : (k + 1) * size] = rim[k]
    partner = lax.broadcasted_iota(jnp.int32, (devices, devices * cap), 0)
    place = lax.broadcasted_iota(jnp.int32, (devices, devices * cap), 1)
    if devices == STAGED:
        x = partner ^ me[0]
        send_place, receive_place = by_stage(x, devices) * cap, x * cap
    else:
        send_place, receive_place = partner * cap, partner * cap
    send_far = jnp.zeros((rows, devices * cap), F32)
    receive_far = jnp.zeros((rows, devices * cap), F32)
    for j in range(cap):
        chosen = pick(rows, far_lists[j : j + 1])
        send_far += mm(chosen, (place == send_place + j).astype(F32).astype(BF))
        receive_far += mm(chosen, (place == receive_place + j).astype(F32).astype(BF))
    send[:, 2 * size :] = send_far.astype(BF)
    receive[:, 2 * size :] = receive_far.astype(BF)


def mesh_tables(me, entries, own_t, forth_t, back_t, *, size, devices):
    rows = own_t.shape[0]
    slots = forth_t.shape[0] - 2 * size
    cap = slots // devices
    columns = side_swap(entries[...], rows, size, me[0])
    own_t[...] = counts_t(rows, 0, columns)
    rim = counts_t(2 * size, rows, columns)
    forth_t[: 2 * size] = rim
    back_t[: 2 * size] = rim
    far = jnp.maximum(columns - rows - 2 * size, 0)
    partner, slot = far // cap, far % cap
    if devices == STAGED:
        partner = partner ^ me[0]
        send_place, receive_place = by_stage(partner, devices) * cap + slot, partner * cap + slot
    else:
        send_place, receive_place = far, far
    is_far = columns >= rows + 2 * size
    forth_t[2 * size :] = counts_t(slots, 0, jnp.where(is_far, receive_place, -1))
    back_t[2 * size :] = counts_t(slots, 0, jnp.where(is_far, send_place, -1))


def decoder_back(me, entries, cotangent, own_t, rim_t, near, outer, inner):
    rows = near.shape[0]
    size = outer.shape[0]
    columns = side_swap(entries[...], rows, size, me[0])
    own = counts_t(rows, 0, columns)
    side = counts_t(2 * size, rows, columns)
    own_t[...] = own
    rim_t[...] = side
    grads = cotangent[...]
    near[...] = mm(own, grads)
    back = mm(side, grads).astype(BF)
    outer[...] = back[:size]
    inner[...] = back[size:]


def emit(outs, rows, size, extra=None):
    outer, inner = outs[:2]
    rows = rows.astype(BF)
    outer[:size] = rows[:size]
    inner[:size] = rows[size : 2 * size]
    used = size
    if extra is not None:
        outer[size:] = extra[0]
        inner[size : 2 * size] = extra[1]
        used = 2 * size
    far = rows[2 * size :]
    if len(outs) == 3:
        outs[2][...] = far
        return
    block = far.shape[0] // PLANE
    inner[used:] = far[block : 2 * block]
    outs[2][...] = far[:block]
    for k in range(2, PLANE):
        outs[k + 1][...] = far[k * block : (k + 1) * block]


def arrived(ins, size):
    return jnp.concatenate([ins[0][:size], ins[1][:size]] + [ref[...] for ref in ins[2:]], axis=0)


def shuffle(own, first, second, third, *outs):
    block = own.shape[0]
    parts = [own[...], first[first.shape[0] - block :], second[...], third[...]]
    rows = jnp.concatenate(parts, axis=0)
    count = rows.shape[0]
    cap = count // (PLANE * len(outs))
    target = lax.broadcasted_iota(jnp.int32, (count, count), 0)
    source = lax.broadcasted_iota(jnp.int32, (count, count), 1)
    place, slot = target // cap, target % cap
    wanted = ((place % PLANE) * len(outs) + place // PLANE) * cap + slot
    moved = mm((source == wanted).astype(F32).astype(BF), rows).astype(BF)
    for m, out in enumerate(outs):
        out[...] = moved[m * PLANE * cap : (m + 1) * PLANE * cap]


def layer_local(hidden, own_t, message, near, *, scale):
    near[...] = hidden[...].astype(F32) + scale * t_mm(own_t[...], message[...])


def back_local(own_t, grad, near):
    near[...] = mm(own_t[...], grad[...])


def first_hidden(near, rim_t, outer_in, inner_in, encoder, weight, send, hidden, message, slope, *outs):
    size = outs[0].shape[0]
    incoming = silu_pair(mm(arrived([outer_in, inner_in], outer_in.shape[0]), encoder[...]))[0].astype(BF)
    state = (near[...] + t_mm(rim_t[...], incoming)).astype(BF)
    hidden[...] = state
    value, gradient = silu_pair(mm(state, weight[0]))
    value = value.astype(BF)
    message[...] = value
    slope[...] = gradient
    emit(outs, t_mm(send[...], value), size)


def next_hidden(near, forth_t, weight, send, outer_extra, inner_extra, *refs, ins, layer, scale):
    size = outer_extra.shape[0]
    rows = arrived(refs[:ins], size)
    hidden, message, slope = refs[ins : ins + 3]
    state = (near[...] + scale * t_mm(forth_t[...], rows)).astype(BF)
    hidden[...] = state
    value, gradient = silu_pair(mm(state, weight[layer]))
    value = value.astype(BF)
    message[...] = value
    slope[...] = gradient
    emit(refs[ins + 3 :], t_mm(send[...], value), size, (outer_extra[...], inner_extra[...]))


def turn(near, forth_t, weight, send, receive, back_t, back_near, *refs, ins, scale):
    size = refs[0].shape[0] // 2
    rows = arrived(refs[:ins], size)
    message, grad = refs[ins : ins + 2]
    state = (near[...] + scale * t_mm(forth_t[...], rows)).astype(BF)
    value, gradient = silu_pair(mm(state, weight[...]))
    value = value.astype(BF)
    message[...] = value
    returned = jnp.concatenate([refs[0][size : 2 * size], refs[1][size : 2 * size]], axis=0)
    back = back_near[...] + mm(receive[:, : 2 * size], returned)
    change = mm_t((back * gradient).astype(BF), weight[...]).astype(BF)
    grad[...] = change
    rim = t_mm(send[:, : 2 * size], value).astype(BF)
    emit(refs[ins + 2 :], mm(back_t[...], change), size, (rim[:size], rim[size:]))


def layer_back(near, receive, rows, slope, weight, grad, scale):
    total = near[...] + mm(receive[...], rows)
    change = (total * scale * slope[...]).astype(BF)
    return (grad[...].astype(F32) + mm_t(change, weight)).astype(BF)


def middle_back(near, receive, slope, weight, grad, back_t, *refs, ins, layer, scale):
    size = refs[ins + 1].shape[0]
    rows = arrived(refs[:ins], size)
    change = layer_back(near, receive, rows, slope, weight[layer], grad, scale)
    refs[ins][...] = change
    emit(refs[ins + 1 :], mm(back_t[...], change), size)


def last_back(near, receive, slope, weight, grad, grid_rim_t, *refs, ins, scale):
    new_grad, outer, inner = refs[ins:]
    rows = arrived(refs[:ins], refs[0].shape[0])
    change = layer_back(near, receive, rows, slope, weight[0], grad, scale)
    new_grad[...] = change
    back = mm(grid_rim_t[...], change).astype(BF)
    outer[...] = back[: outer.shape[0]]
    inner[...] = back[outer.shape[0] :]


def decode(latent, own_t, rim_t, message, outer_in, inner_in, output):
    size = outer_in.shape[0] // 2
    incoming = jnp.concatenate([outer_in[size:], inner_in[size : 2 * size]], axis=0)
    total = t_mm(own_t[...], message[...]) + t_mm(rim_t[...], incoming)
    output[...] = (latent[...].astype(F32) + total).astype(BF)


def grid_back(me, near, lists, outer_in, inner_in, slope, weight, cotangent, output):
    outer, inner = pair_order(lists, me[0])
    rows = near.shape[0]
    total = near[...] + mm(pick(rows, outer), outer_in[...]) + mm(pick(rows, inner), inner_in[...])
    change = (total * slope[...].astype(F32)).astype(BF)
    output[...] = (cotangent[...].astype(F32) + mm_t(change, weight[...])).astype(BF)


def toggle(value, bits):
    peers = lax.axis_size("dom")
    return lax.ppermute(value, "dom", [(i, i ^ bits) for i in range(peers)])


def across(value):
    peers = lax.axis_size("dom")
    pairs = [(i, (i + 1) % peers if i % 2 else (i - 1) % peers) for i in range(peers)]
    return lax.ppermute(value, "dom", pairs)


def exchange(outs, cap):
    width = outs[0].shape[1]
    if len(outs) == 3:
        outer, inner, far = outs
        peers = lax.axis_size("dom")
        blocks = far.reshape(peers, cap, width)
        blocks = lax.all_to_all(blocks, "dom", split_axis=0, concat_axis=0, tiled=True)
        return [across(outer), toggle(inner, 1), blocks.reshape(-1, width)]
    outer, inner, own, second, third = outs
    third_in = toggle(third, 3)
    second_in = toggle(second, 2)
    inner_in = toggle(inner, 1)
    outer_in = across(outer)
    columns = STAGED // PLANE
    blocks = call(
        shuffle,
        [((PLANE * cap, width), BF)] * columns,
        2 * (STAGED * cap) ** 2 * width,
        own, inner_in, second_in, third_in,
    )
    moved = [toggle(blocks[m], m * PLANE) for m in reversed(range(1, columns))]
    return [outer_in, inner_in, blocks[0]] + moved[::-1]


def on_device(
    grid_latent,
    mesh_latent,
    encoder_weight,
    processor_weights,
    decoder_weight,
    cotangent,
    grid_halo_rows,
    encoder_neighbours,
    halo_rows,
    far_sources,
    mesh_neighbours,
    decoder_neighbours,
):
    devices = lax.axis_size("dom")
    grid_rows, width = grid_latent.shape
    mesh_rows = mesh_latent.shape[0]
    ghalo = grid_halo_rows.shape[2]
    halo = halo_rows.shape[2]
    cap = far_sources.shape[2]
    slots = devices * cap
    listed = 2 * halo + slots
    scale = 1.0 / mesh_neighbours.shape[1]
    me = lax.axis_index("dom").astype(jnp.int32).reshape(1)

    def square(rows, depth):
        return 2 * rows * depth * width

    def sends(per_side):
        if devices != STAGED:
            return [((per_side, width), BF)] * 2 + [((slots, width), BF)]
        block = slots // PLANE
        return [((per_side, width), BF), ((per_side + block, width), BF)] + [((block, width), BF)] * (PLANE - 1)

    state = ((mesh_rows, width), BF)
    total = ((mesh_rows, width), F32)
    step = 3 * square(mesh_rows, width)

    outer, inner = call(
        grid_send, [((ghalo, width), BF)] * 2, square(2 * ghalo, grid_rows), me, grid_latent, grid_halo_rows,
        scalars=1,
    )
    outer_in, inner_in = across(outer), toggle(inner, 1)

    near, grid_own_t, grid_rim_t, grid_slope = call(
        functools.partial(encoder_local, size=ghalo),
        [total, ((grid_rows, mesh_rows), BF), ((2 * ghalo, mesh_rows), BF), ((grid_rows, width), BF)],
        square(grid_rows, width) + square(mesh_rows, grid_rows),
        me, grid_latent, encoder_weight, mesh_latent, encoder_neighbours.T,
        scalars=1,
    )
    send, receive = call(
        functools.partial(list_tables, rows=mesh_rows),
        [((mesh_rows, listed), BF)] * 2,
        16 * mesh_rows * listed,
        me, halo_rows, far_sources[0].T,
        scalars=1,
    )

    hidden, message, slope_0, *outs = call(
        first_hidden,
        [state, state, total] + sends(halo),
        step,
        near, grid_rim_t, outer_in, inner_in, encoder_weight, processor_weights, send,
    )
    ins = exchange(outs, cap)

    own_t, forth_t, back_t = call(
        functools.partial(mesh_tables, size=halo, devices=devices),
        [((mesh_rows, mesh_rows), BF)] + [((listed, mesh_rows), BF)] * 2,
        30 * mesh_rows * listed,
        me, mesh_neighbours.T,
        scalars=1,
    )
    local = functools.partial(layer_local, scale=scale)
    (near,) = call(local, [total], square(mesh_rows, mesh_rows), hidden, own_t, message)
    decoder_own_t, decoder_rim_t, decoder_near, outer_back, inner_back = call(
        decoder_back,
        [((mesh_rows, grid_rows), BF), ((2 * halo, grid_rows), BF), total, ((halo, width), BF), ((halo, width), BF)],
        square(grid_rows, mesh_rows),
        me, decoder_neighbours.T, cotangent,
        scalars=1,
    )

    hidden, message, slope_1, *outs = call(
        functools.partial(next_hidden, ins=len(ins), layer=1, scale=scale),
        [state, state, total] + sends(2 * halo),
        step,
        near, forth_t, processor_weights, send, outer_back, inner_back, *ins,
    )
    ins = exchange(outs, cap)
    (near,) = call(local, [total], square(mesh_rows, mesh_rows), hidden, own_t, message)

    message, grad, *outs = call(
        functools.partial(turn, ins=len(ins), scale=scale),
        [state, state] + sends(2 * halo),
        2 * step,
        near, forth_t, decoder_weight, send, receive, back_t, decoder_near, *ins,
    )
    ins = exchange(outs, cap)
    outer_decoder, inner_decoder = ins[:2]
    (near,) = call(back_local, [total], square(mesh_rows, mesh_rows), own_t, grad)

    grad, *outs = call(
        functools.partial(middle_back, ins=len(ins), layer=1, scale=scale),
        [state] + sends(halo),
        step,
        near, receive, slope_1, processor_weights, grad, back_t, *ins,
    )
    ins = exchange(outs, cap)
    (near,) = call(back_local, [total], square(mesh_rows, mesh_rows), own_t, grad)
    (output,) = call(
        decode,
        [((grid_rows, width), BF)],
        square(grid_rows, mesh_rows),
        grid_latent, decoder_own_t, decoder_rim_t, message, outer_decoder, inner_decoder,
    )

    mesh_grad, outer, inner = call(
        functools.partial(last_back, ins=len(ins), scale=scale),
        [state, ((ghalo, width), BF), ((ghalo, width), BF)],
        step,
        near, receive, slope_0, processor_weights, grad, grid_rim_t, *ins,
    )
    outer_in, inner_in = across(outer), toggle(inner, 1)
    (near,) = call(
        back_local, [((grid_rows, width), F32)], square(mesh_rows, grid_rows), grid_own_t, mesh_grad
    )
    (grid_grad,) = call(
        grid_back,
        [((grid_rows, width), BF)],
        square(grid_rows, width),
        me, near, grid_halo_rows, outer_in, inner_in, grid_slope, encoder_weight, cotangent,
        scalars=1,
    )
    return (output, grid_grad, mesh_grad)


def solution(mesh):
    in_specs = (
        P(("groups", "dom"), None),
        P(("groups", "dom"), None),
        P(),
        P(),
        P(),
        P(("groups", "dom"), None),
        P("dom", None, None),
        P("dom", None),
        P("dom", None, None),
        P("dom", None, None),
        P("dom", None),
        P("dom", None),
    )
    out_specs = (P(("groups", "dom"), None), P(("groups", "dom"), None), P(("groups", "dom"), None))
    return jax.shard_map(
        on_device, mesh=mesh, in_specs=in_specs, out_specs=out_specs, check_vma=False
    )
```

```python
import functools

import jax
import jax.numpy as jnp
from jax import lax
from jax.experimental import pallas as pl
from jax.experimental.pallas import tpu as pltpu
from jax.sharding import PartitionSpec as P

BF = jnp.bfloat16
F32 = jnp.float32
VMEM_LIMIT = 24 * 1024 * 1024
PLANE = 4
STAGED = 16
CHUNKS = 4


def mm(a, b):
    return jnp.dot(a, b, preferred_element_type=F32)


def mm_t(a, b):
    return lax.dot_general(a, b, (((1,), (1,)), ((), ())), preferred_element_type=F32)


def t_mm(a, b):
    return lax.dot_general(a, b, (((0,), (0,)), ((), ())), preferred_element_type=F32)


def silu_pair(value):
    sigma = 0.5 + 0.5 * jnp.tanh(0.5 * value)
    message = value * sigma
    return message, sigma + message * (1.0 - sigma)


def pick(rows, wanted):
    places = lax.broadcasted_iota(jnp.int32, (rows, wanted.shape[1]), 0)
    return (places == wanted).astype(F32).astype(BF)


def counts_t(columns, first, entries):
    degree, rows = entries.shape
    places = lax.broadcasted_iota(jnp.int32, (columns, rows), 0) + first
    total = jnp.zeros((columns, rows), F32)
    for k in range(degree):
        total = total + (places == entries[k : k + 1]).astype(F32)
    return total.astype(BF)


def side_swap(entries, rows, size, me):
    swapped = jnp.where(entries < rows + size, entries + size, entries - size)
    rim = (entries >= rows) & (entries < rows + 2 * size)
    return jnp.where(rim & (me % 2 == 1), swapped, entries)


def pair_order(lists, me):
    left, right = lists[0, 0:1], lists[0, 1:2]
    odd = me % 2
    return left + odd * (right - left), right + odd * (left - right)


def by_stage(x, devices):
    return (x % PLANE) * (devices // PLANE) + x // PLANE


def call(body, out_shapes, flops, *args, scalars=0, hbm=0, free=0, hbm_out=0, scratch=()):
    shapes = [jax.ShapeDtypeStruct(s, t) for s, t in out_shapes]
    size = sum(a.size * a.dtype.itemsize for a in args)
    size += sum(s.size * s.dtype.itemsize for s in shapes)
    places = [pltpu.SMEM] * scalars + [pltpu.HBM] * hbm + [pltpu.VMEM] * (len(args) - scalars - hbm - free)
    places += [pl.ANY] * free
    out_places = [pltpu.HBM] * hbm_out + [pltpu.VMEM] * (len(shapes) - hbm_out)
    return pl.pallas_call(
        body,
        out_shape=shapes,
        in_specs=[pl.BlockSpec(memory_space=place) for place in places],
        out_specs=[pl.BlockSpec(memory_space=place) for place in out_places],
        scratch_shapes=list(scratch),
        compiler_params=pltpu.CompilerParams(vmem_limit_bytes=VMEM_LIMIT),
        cost_estimate=pl.CostEstimate(flops=flops, bytes_accessed=size, transcendentals=0),
    )(*args)


def copies_of(arrays):
    return [pltpu.VMEM(a.shape, a.dtype) for a in arrays]


def fetch(sources, targets, sems):
    copies = [pltpu.make_async_copy(s, t, sems.at[i]) for i, (s, t) in enumerate(zip(sources, targets))]
    for copy in copies:
        copy.start()
    return copies


def row_chunks(rows):
    step = rows // CHUNKS
    return [pl.ds(i * step, step) for i in range(CHUNKS)]


def grid_send(me, latent, lists, outer, inner, values, wanted, sems):
    parts = row_chunks(latent.shape[0])
    sources = [lists] + [latent.at[part] for part in parts]
    copies = fetch(sources, [wanted] + [values.at[part] for part in parts], sems)
    copies[0].wait()
    wanted_outer, wanted_inner = pair_order(wanted, me[0])
    step = latent.shape[0] // CHUNKS
    outer_rows = inner_rows = 0.0
    for i, part in enumerate(parts):
        copies[i + 1].wait()
        chunk = values[part]
        outer_rows += t_mm(pick(step, wanted_outer - i * step), chunk)
        inner_rows += t_mm(pick(step, wanted_inner - i * step), chunk)
    outer[...] = outer_rows.astype(BF)
    inner[...] = inner_rows.astype(BF)


def encoder_local(me, entries, mesh_entries, lists, far_lists, weight, latent, mesh,
                  near, grid_own_t, grid_rim_t, slope, send, receive, own_t, forth_t, back_t,
                  entries_v, mesh_entries_v, lists_v, far_lists_v, weight_v, latent_v, mesh_v, sems, *, size):
    sources = [entries, mesh_entries, lists, far_lists, weight, latent, mesh]
    targets = [entries_v, mesh_entries_v, lists_v, far_lists_v, weight_v, latent_v, mesh_v]
    copies = fetch(sources, targets, sems)
    rows = latent.shape[0]
    copies[0].wait()
    columns = side_swap(entries_v[...], rows, size, me[0])
    own = counts_t(rows, 0, columns)
    grid_own_t[...] = own
    grid_rim_t[...] = counts_t(2 * size, rows, columns)
    copies[1].wait()
    mesh_tables(me, mesh_entries_v, own_t, forth_t, back_t, lists.shape[2], far_lists.shape[1])
    copies[2].wait()
    copies[3].wait()
    list_tables(me, lists_v, far_lists_v, send, receive)
    copies[4].wait()
    copies[5].wait()
    message, gradient = silu_pair(mm(latent_v[...], weight_v[...]))
    slope[...] = gradient.astype(BF)
    copies[6].wait()
    near[...] = mesh_v[...].astype(F32) + t_mm(own, message.astype(BF))


def list_tables(me, lists, far_lists, send, receive):
    rows = send.shape[0]
    size = lists.shape[2]
    cap, devices = far_lists.shape
    outer, inner = pair_order(lists, me[0])
    rim = [pick(rows, outer), pick(rows, inner)]
    for k in range(2):
        send[:, k * size : (k + 1) * size] = rim[k]
        receive[:, k * size : (k + 1) * size] = rim[k]
    partner = lax.broadcasted_iota(jnp.int32, (devices, devices * cap), 0)
    place = lax.broadcasted_iota(jnp.int32, (devices, devices * cap), 1)
    if devices == STAGED:
        x = partner ^ me[0]
        send_place, receive_place = by_stage(x, devices) * cap, x * cap
    else:
        send_place, receive_place = partner * cap, partner * cap
    send_far = jnp.zeros((rows, devices * cap), F32)
    receive_far = jnp.zeros((rows, devices * cap), F32)
    for j in range(cap):
        chosen = pick(rows, far_lists[j : j + 1])
        send_far += mm(chosen, (place == send_place + j).astype(F32).astype(BF))
        receive_far += mm(chosen, (place == receive_place + j).astype(F32).astype(BF))
    send[:, 2 * size :] = send_far.astype(BF)
    receive[:, 2 * size :] = receive_far.astype(BF)


def mesh_tables(me, entries, own_t, forth_t, back_t, size, devices):
    rows = own_t.shape[0]
    slots = forth_t.shape[0] - 2 * size
    cap = slots // devices
    columns = side_swap(entries[...], rows, size, me[0])
    own_t[...] = counts_t(rows, 0, columns)
    rim = counts_t(2 * size, rows, columns)
    forth_t[: 2 * size] = rim
    back_t[: 2 * size] = rim
    far = jnp.maximum(columns - rows - 2 * size, 0)
    partner, slot = far // cap, far % cap
    if devices == STAGED:
        partner = partner ^ me[0]
        send_place, receive_place = by_stage(partner, devices) * cap + slot, partner * cap + slot
    else:
        send_place, receive_place = far, far
    is_far = columns >= rows + 2 * size
    forth_t[2 * size :] = counts_t(slots, 0, jnp.where(is_far, receive_place, -1))
    back_t[2 * size :] = counts_t(slots, 0, jnp.where(is_far, send_place, -1))


def decoder_back(me, entries, cotangent, own_t, rim_t, near, outer, inner):
    rows = near.shape[0]
    size = outer.shape[0]
    columns = side_swap(entries[...], rows, size, me[0])
    own = counts_t(rows, 0, columns)
    side = counts_t(2 * size, rows, columns)
    own_t[...] = own
    rim_t[...] = side
    grads = cotangent[...]
    near[...] = mm(own, grads)
    back = mm(side, grads).astype(BF)
    outer[...] = back[:size]
    inner[...] = back[size:]


def emit(outs, rows, size, extra=None):
    inner = outs[0]
    rows = rows.astype(BF)
    inner[:size] = rows[:size]
    used = size
    if extra is not None:
        inner[size : 2 * size] = extra
        used = 2 * size
    far = rows[size:]
    if len(outs) == 2:
        outs[1][...] = far
        return
    block = far.shape[0] // PLANE
    inner[used:] = far[block : 2 * block]
    outs[1][...] = far[:block]
    for k in range(2, PLANE):
        outs[k][...] = far[k * block : (k + 1) * block]


def outer_forth(send, message, *refs, size):
    outer = refs[-1]
    outer[:size] = t_mm(send[:, :size], message[...]).astype(BF)
    if len(refs) == 2:
        outer[size:] = refs[0][...]


def outer_back(back_t, grad, *refs, size):
    outer = refs[-1]
    outer[:size] = mm(back_t[:size], grad[...]).astype(BF)
    if len(refs) == 3:
        send, message = refs[:2]
        outer[size:] = t_mm(send[:, :size], message[...]).astype(BF)


def arrived(ins, size):
    far = list(ins[2:3]) + list(ins[3:])[::-1]
    return jnp.concatenate([ins[0][:size], ins[1][:size]] + [ref[...] for ref in far], axis=0)


def shuffle(own, third, second, first, _after, *outs):
    block = own.shape[0]
    parts = [own[...], first[first.shape[0] - block :], second[...], third[...]]
    rows = jnp.concatenate(parts, axis=0)
    count = rows.shape[0]
    cap = count // (PLANE * len(outs))
    target = lax.broadcasted_iota(jnp.int32, (count, count), 0)
    source = lax.broadcasted_iota(jnp.int32, (count, count), 1)
    place, slot = target // cap, target % cap
    wanted = ((place % PLANE) * len(outs) + place // PLANE) * cap + slot
    moved = mm((source == wanted).astype(F32).astype(BF), rows).astype(BF)
    for m, out in enumerate(outs):
        out[...] = moved[m * PLANE * cap : (m + 1) * PLANE * cap]


def layer_local(hidden, own_t, message, near, *, scale):
    near[...] = hidden[...].astype(F32) + scale * t_mm(own_t[...], message[...])


def back_local(own_t, grad, near):
    near[...] = mm(own_t[...], grad[...])


def first_hidden(near, rim_t, outer_in, inner_in, encoder, weight, send, hidden, message, slope, *outs, size):
    incoming = silu_pair(mm(arrived([outer_in, inner_in], outer_in.shape[0]), encoder[...]))[0].astype(BF)
    state = (near[...] + t_mm(rim_t[...], incoming)).astype(BF)
    hidden[...] = state
    value, gradient = silu_pair(mm(state, weight[0]))
    value = value.astype(BF)
    message[...] = value
    slope[...] = gradient
    emit(outs, t_mm(send[:, size:], value), size)


def next_hidden(near, forth_t, weight, send, inner_extra, *refs, ins, layer, scale, size):
    rows = arrived(refs[:ins], size)
    hidden, message, slope = refs[ins : ins + 3]
    state = (near[...] + scale * t_mm(forth_t[...], rows)).astype(BF)
    hidden[...] = state
    value, gradient = silu_pair(mm(state, weight[layer]))
    value = value.astype(BF)
    message[...] = value
    slope[...] = gradient
    emit(refs[ins + 3 :], t_mm(send[:, size:], value), size, inner_extra[...])


def turn(near, forth_t, weight, send, receive, back_t, back_near, *refs, ins, scale, size):
    rows = arrived(refs[:ins], size)
    message, grad = refs[ins : ins + 2]
    state = (near[...] + scale * t_mm(forth_t[...], rows)).astype(BF)
    value, gradient = silu_pair(mm(state, weight[...]))
    value = value.astype(BF)
    message[...] = value
    returned = jnp.concatenate([refs[0][size : 2 * size], refs[1][size : 2 * size]], axis=0)
    back = back_near[...] + mm(receive[:, : 2 * size], returned)
    change = mm_t((back * gradient).astype(BF), weight[...]).astype(BF)
    grad[...] = change
    rim = t_mm(send[:, size : 2 * size], value).astype(BF)
    emit(refs[ins + 2 :], mm(back_t[size:], change), size, rim)


def layer_back(near, receive, rows, slope, weight, grad, scale):
    total = near[...] + mm(receive[...], rows)
    change = (total * scale * slope[...]).astype(BF)
    return (grad[...].astype(F32) + mm_t(change, weight)).astype(BF)


def middle_back(near, receive, slope, weight, grad, back_t, *refs, ins, layer, scale, size):
    rows = arrived(refs[:ins], size)
    change = layer_back(near, receive, rows, slope, weight[layer], grad, scale)
    refs[ins][...] = change
    emit(refs[ins + 1 :], mm(back_t[size:], change), size)


def last_back(near, receive, slope, weight, grad, grid_rim_t, *refs, ins, scale):
    new_grad, outer, inner = refs[ins:]
    rows = arrived(refs[:ins], refs[0].shape[0])
    change = layer_back(near, receive, rows, slope, weight[0], grad, scale)
    new_grad[...] = change
    back = mm(grid_rim_t[...], change).astype(BF)
    outer[...] = back[: outer.shape[0]]
    inner[...] = back[outer.shape[0] :]


def decode(latent, own_t, rim_t, message, outer_in, inner_in, output):
    size = outer_in.shape[0] // 2
    incoming = jnp.concatenate([outer_in[size:], inner_in[size : 2 * size]], axis=0)
    total = t_mm(own_t[...], message[...]) + t_mm(rim_t[...], incoming)
    output[...] = (latent[...].astype(F32) + total).astype(BF)


def grid_local(me, own_t, grad, lists, slope, weight, cotangent, base, table, slope_rows):
    rows = own_t.shape[0]
    size = lists.shape[2]
    for k, wanted in enumerate(pair_order(lists, me[0])):
        table[:, k * size : (k + 1) * size] = pick(rows, wanted)
    slope_rows[...] = t_mm(table[...], slope[...])
    change = (mm(own_t[...], grad[...]) * slope[...].astype(F32)).astype(BF)
    base[...] = cotangent[...].astype(F32) + mm_t(change, weight[...])


def grid_back(base, table, slope_rows, weight, outer_in, inner_in, output, staging, sems):
    returned = jnp.concatenate([outer_in[...], inner_in[...]], axis=0).astype(F32)
    change = mm_t((returned * slope_rows[...]).astype(BF), weight[...]).astype(BF)
    copies = []
    for i, part in enumerate(row_chunks(base.shape[0])):
        staging[part] = (base[part] + mm(table[part], change)).astype(BF)
        copies.append(pltpu.make_async_copy(staging.at[part], output.at[part], sems.at[i]))
        copies[-1].start()
    for copy in copies:
        copy.wait()


def toggle(value, bits):
    peers = lax.axis_size("dom")
    return lax.ppermute(value, "dom", [(i, i ^ bits) for i in range(peers)])


def across(value):
    peers = lax.axis_size("dom")
    pairs = [(i, (i + 1) % peers if i % 2 else (i - 1) % peers) for i in range(peers)]
    return lax.ppermute(value, "dom", pairs)


def exchange(outer, outs, cap, after):
    width = outer.shape[1]
    if len(outs) == 2:
        inner, far = outs
        peers = lax.axis_size("dom")
        blocks = far.reshape(peers, cap, width)
        blocks = lax.all_to_all(blocks, "dom", split_axis=0, concat_axis=0, tiled=True)
        return [across(outer), toggle(inner, 1), blocks.reshape(-1, width)]
    inner, own, second, third = outs
    outer_in = across(outer)
    inner_in = toggle(inner, 1)
    second_in = toggle(second, 2)
    third_in = toggle(third, 3)
    columns = STAGED // PLANE
    blocks = call(
        shuffle,
        [((PLANE * cap, width), BF)] * columns,
        2 * (STAGED * cap) ** 2 * width,
        own, third_in, second_in, inner_in, after,
        free=1,
    )
    moved = [toggle(blocks[m], m * PLANE) for m in reversed(range(1, columns))]
    return [outer_in, inner_in, blocks[0]] + moved


def on_device(
    grid_latent,
    mesh_latent,
    encoder_weight,
    processor_weights,
    decoder_weight,
    cotangent,
    grid_halo_rows,
    encoder_neighbours,
    halo_rows,
    far_sources,
    mesh_neighbours,
    decoder_neighbours,
):
    devices = lax.axis_size("dom")
    grid_rows, width = grid_latent.shape
    mesh_rows = mesh_latent.shape[0]
    ghalo = grid_halo_rows.shape[2]
    halo = halo_rows.shape[2]
    cap = far_sources.shape[2]
    slots = devices * cap
    listed = 2 * halo + slots
    scale = 1.0 / mesh_neighbours.shape[1]
    me = lax.axis_index("dom").astype(jnp.int32).reshape(1)

    def square(rows, depth):
        return 2 * rows * depth * width

    def sends(per_side):
        if devices != STAGED:
            return [((per_side, width), BF), ((slots, width), BF)]
        block = slots // PLANE
        return [((per_side + block, width), BF)] + [((block, width), BF)] * (PLANE - 1)

    state = ((mesh_rows, width), BF)
    total = ((mesh_rows, width), F32)
    rim = ((halo, width), BF)
    wide = ((2 * halo, width), BF)
    grid_rim = ((ghalo, width), BF)
    step = 3 * square(mesh_rows, width)
    rim_flops = square(halo, mesh_rows)
    forth = functools.partial(outer_forth, size=halo)
    back = functools.partial(outer_back, size=halo)

    outer, inner = call(
        grid_send,
        [grid_rim, grid_rim],
        square(2 * ghalo, grid_rows),
        me, grid_latent, grid_halo_rows,
        scalars=1, hbm=2,
        scratch=copies_of([grid_latent, grid_halo_rows]) + [pltpu.SemaphoreType.DMA((CHUNKS + 1,))],
    )
    outer_in, inner_in = across(outer), toggle(inner, 1)

    sources = [
        encoder_neighbours.T, mesh_neighbours.T, halo_rows, far_sources[0].T, encoder_weight, grid_latent, mesh_latent,
    ]
    near, grid_own_t, grid_rim_t, grid_slope, send, receive, own_t, forth_t, back_t = call(
        functools.partial(encoder_local, size=ghalo),
        [
            total,
            ((grid_rows, mesh_rows), BF),
            ((2 * ghalo, mesh_rows), BF),
            ((grid_rows, width), BF),
            ((mesh_rows, listed), BF),
            ((mesh_rows, listed), BF),
            ((mesh_rows, mesh_rows), BF),
            ((listed, mesh_rows), BF),
            ((listed, mesh_rows), BF),
        ],
        4 * square(grid_rows, width),
        me, *sources,
        scalars=1, hbm=len(sources),
        scratch=copies_of(sources) + [pltpu.SemaphoreType.DMA((len(sources),))],
    )

    hidden, message, slope_0, *outs = call(
        functools.partial(first_hidden, size=halo),
        [state, state, total] + sends(halo),
        step,
        near, grid_rim_t, outer_in, inner_in, encoder_weight, processor_weights, send,
    )
    (outer,) = call(forth, [rim], rim_flops, send, message)
    local = functools.partial(layer_local, scale=scale)
    (near,) = call(local, [total], 5 * square(mesh_rows, mesh_rows), hidden, own_t, message)
    decoder_own_t, decoder_rim_t, decoder_near, outer_extra, inner_extra = call(
        decoder_back,
        [((mesh_rows, grid_rows), BF), ((2 * halo, grid_rows), BF), total, rim, rim],
        square(grid_rows, mesh_rows),
        me, decoder_neighbours.T, cotangent,
        scalars=1,
    )
    ins = exchange(outer, outs, cap, decoder_near)

    hidden, message, slope_1, *outs = call(
        functools.partial(next_hidden, ins=len(ins), layer=1, scale=scale, size=halo),
        [state, state, total] + sends(2 * halo),
        step,
        near, forth_t, processor_weights, send, inner_extra, *ins,
    )
    (outer,) = call(forth, [wide], rim_flops, send, message, outer_extra)
    (near,) = call(local, [total], 5 * square(mesh_rows, mesh_rows), hidden, own_t, message)
    ins = exchange(outer, outs, cap, near)

    message, grad, *outs = call(
        functools.partial(turn, ins=len(ins), scale=scale, size=halo),
        [state, state] + sends(2 * halo),
        2 * step,
        near, forth_t, decoder_weight, send, receive, back_t, decoder_near, *ins,
    )
    (outer,) = call(back, [wide], rim_flops, back_t, grad, send, message)
    (near,) = call(back_local, [total], 5 * square(mesh_rows, mesh_rows), own_t, grad)
    ins = exchange(outer, outs, cap, near)
    outer_decoder, inner_decoder = ins[:2]

    grad, *outs = call(
        functools.partial(middle_back, ins=len(ins), layer=1, scale=scale, size=halo),
        [state] + sends(halo),
        step,
        near, receive, slope_1, processor_weights, grad, back_t, *ins,
    )
    (outer,) = call(back, [rim], rim_flops, back_t, grad)
    (near,) = call(back_local, [total], square(mesh_rows, mesh_rows), own_t, grad)
    ins = exchange(outer, outs, cap, near)
    (output,) = call(
        decode,
        [((grid_rows, width), BF)],
        square(grid_rows, mesh_rows),
        grid_latent, decoder_own_t, decoder_rim_t, message, outer_decoder, inner_decoder,
    )

    mesh_grad, outer, inner = call(
        functools.partial(last_back, ins=len(ins), scale=scale),
        [state, grid_rim, grid_rim],
        step,
        near, receive, slope_0, processor_weights, grad, grid_rim_t, *ins,
    )
    outer_in, inner_in = across(outer), toggle(inner, 1)
    base, table, slope_rows = call(
        grid_local,
        [((grid_rows, width), F32), ((grid_rows, 2 * ghalo), BF), ((2 * ghalo, width), F32)],
        square(mesh_rows, grid_rows) + square(grid_rows, width),
        me, grid_own_t, mesh_grad, grid_halo_rows, grid_slope, encoder_weight, cotangent,
        scalars=1,
    )
    (grid_grad,) = call(
        grid_back,
        [((grid_rows, width), BF)],
        square(grid_rows, 4 * ghalo),
        base, table, slope_rows, encoder_weight, outer_in, inner_in,
        hbm_out=1,
        scratch=[pltpu.VMEM((grid_rows, width), BF), pltpu.SemaphoreType.DMA((CHUNKS,))],
    )
    return (output, grid_grad, mesh_grad)


def solution(mesh):
    in_specs = (
        P(("groups", "dom"), None),
        P(("groups", "dom"), None),
        P(),
        P(),
        P(),
        P(("groups", "dom"), None),
        P("dom", None, None),
        P("dom", None),
        P("dom", None, None),
        P("dom", None, None),
        P("dom", None),
        P("dom", None),
    )
    out_specs = (P(("groups", "dom"), None), P(("groups", "dom"), None), P(("groups", "dom"), None))
    return jax.shard_map(
        on_device, mesh=mesh, in_specs=in_specs, out_specs=out_specs, check_vma=False
    )
```

```python
import functools

import jax
import jax.numpy as jnp
from jax import lax
from jax.experimental import pallas as pl
from jax.experimental.pallas import tpu as pltpu
from jax.sharding import PartitionSpec as P

BF = jnp.bfloat16
F32 = jnp.float32
VMEM_LIMIT = 24 * 1024 * 1024
PLANE = 4
STAGED = 16
CHUNKS = 4


def mm(a, b):
    return jnp.dot(a, b, preferred_element_type=F32)


def mm_t(a, b):
    return lax.dot_general(a, b, (((1,), (1,)), ((), ())), preferred_element_type=F32)


def t_mm(a, b):
    return lax.dot_general(a, b, (((0,), (0,)), ((), ())), preferred_element_type=F32)


def silu_pair(value):
    sigma = 0.5 + 0.5 * jnp.tanh(0.5 * value)
    message = value * sigma
    return message, sigma + message * (1.0 - sigma)


def pick(rows, wanted):
    places = lax.broadcasted_iota(jnp.int32, (rows, wanted.shape[1]), 0)
    return (places == wanted).astype(F32).astype(BF)


def counts_t(columns, first, entries):
    degree, rows = entries.shape
    places = lax.broadcasted_iota(jnp.int32, (columns, rows), 0) + first
    total = jnp.zeros((columns, rows), F32)
    for k in range(degree):
        total = total + (places == entries[k : k + 1]).astype(F32)
    return total.astype(BF)


def side_swap(entries, rows, size, me):
    swapped = jnp.where(entries < rows + size, entries + size, entries - size)
    rim = (entries >= rows) & (entries < rows + 2 * size)
    return jnp.where(rim & (me % 2 == 1), swapped, entries)


def pair_order(lists, me):
    left, right = lists[0, 0:1], lists[0, 1:2]
    odd = me % 2
    return left + odd * (right - left), right + odd * (left - right)


def by_stage(x, devices):
    return (x % PLANE) * (devices // PLANE) + x // PLANE


def call(body, out_shapes, flops, *args, scalars=0, hbm=0, free=0, hbm_out=0, scratch=(), limit=VMEM_LIMIT):
    shapes = [jax.ShapeDtypeStruct(s, t) for s, t in out_shapes]
    size = sum(a.size * a.dtype.itemsize for a in args)
    size += sum(s.size * s.dtype.itemsize for s in shapes)
    size *= hbm == 0
    places = [pltpu.SMEM] * scalars + [pltpu.HBM] * hbm + [pltpu.VMEM] * (len(args) - scalars - hbm - free)
    places += [pl.ANY] * free
    out_places = [pltpu.HBM] * hbm_out + [pltpu.VMEM] * (len(shapes) - hbm_out)
    kept = len(args) - free
    inner = body if free == 0 else lambda *refs: body(*refs[:kept], *refs[len(args) :])
    return pl.pallas_call(
        inner,
        out_shape=shapes,
        in_specs=[pl.BlockSpec(memory_space=place) for place in places],
        out_specs=[pl.BlockSpec(memory_space=place) for place in out_places],
        scratch_shapes=list(scratch),
        compiler_params=pltpu.CompilerParams(vmem_limit_bytes=limit),
        cost_estimate=pl.CostEstimate(flops=flops, bytes_accessed=size, transcendentals=0),
    )(*args)


def copies_of(arrays):
    return [pltpu.VMEM(a.shape, a.dtype) for a in arrays]


def fetch(sources, targets, sems):
    copies = [pltpu.make_async_copy(s, t, sems.at[i]) for i, (s, t) in enumerate(zip(sources, targets))]
    for copy in copies:
        copy.start()
    return copies


def row_chunks(rows):
    step = rows // CHUNKS
    return [pl.ds(i * step, step) for i in range(CHUNKS)]


def grid_send(me, latent, lists, outer, inner, values, wanted, sems):
    parts = row_chunks(latent.shape[0])
    sources = [lists] + [latent.at[part] for part in parts]
    copies = fetch(sources, [wanted] + [values.at[part] for part in parts], sems)
    copies[0].wait()
    wanted_outer, wanted_inner = pair_order(wanted, me[0])
    step = latent.shape[0] // CHUNKS
    outer_rows = inner_rows = 0.0
    for i, part in enumerate(parts):
        copies[i + 1].wait()
        chunk = values[part]
        outer_rows += t_mm(pick(step, wanted_outer - i * step), chunk)
        inner_rows += t_mm(pick(step, wanted_inner - i * step), chunk)
    outer[...] = outer_rows.astype(BF)
    inner[...] = inner_rows.astype(BF)


def encoder_local(me, entries, lists, far_lists, weight, latent, mesh,
                  near, grid_own_t, grid_rim_t, slope, send, receive, *, size):
    rows = latent.shape[0]
    columns = side_swap(entries[...], rows, size, me[0])
    own = counts_t(rows, 0, columns)
    grid_own_t[...] = own
    grid_rim_t[...] = counts_t(2 * size, rows, columns)
    list_tables(me, lists, far_lists, send, receive)
    message, gradient = silu_pair(mm(latent[...], weight[...]))
    slope[...] = gradient.astype(BF)
    near[...] = mesh[...].astype(F32) + t_mm(own, message.astype(BF))


def list_tables(me, lists, far_lists, send, receive):
    rows = send.shape[0]
    size = lists.shape[2]
    cap, devices = far_lists.shape
    outer, inner = pair_order(lists, me[0])
    rim = [pick(rows, outer), pick(rows, inner)]
    for k in range(2):
        send[:, k * size : (k + 1) * size] = rim[k]
        receive[:, k * size : (k + 1) * size] = rim[k]
    partner = lax.broadcasted_iota(jnp.int32, (devices, devices * cap), 0)
    place = lax.broadcasted_iota(jnp.int32, (devices, devices * cap), 1)
    if devices == STAGED:
        x = partner ^ me[0]
        send_place, receive_place = by_stage(x, devices) * cap, x * cap
    else:
        send_place, receive_place = partner * cap, partner * cap
    send_far = jnp.zeros((rows, devices * cap), F32)
    receive_far = jnp.zeros((rows, devices * cap), F32)
    for j in range(cap):
        chosen = pick(rows, far_lists[j : j + 1])
        send_far += mm(chosen, (place == send_place + j).astype(F32).astype(BF))
        receive_far += mm(chosen, (place == receive_place + j).astype(F32).astype(BF))
    send[:, 2 * size :] = send_far.astype(BF)
    receive[:, 2 * size :] = receive_far.astype(BF)


def mesh_tables(me, entries, own_t, forth_t, back_t, *, size, devices):
    rows = own_t.shape[0]
    slots = forth_t.shape[0] - 2 * size
    cap = slots // devices
    columns = side_swap(entries[...], rows, size, me[0])
    own_t[...] = counts_t(rows, 0, columns)
    rim = counts_t(2 * size, rows, columns)
    forth_t[: 2 * size] = rim
    back_t[: 2 * size] = rim
    far = jnp.maximum(columns - rows - 2 * size, 0)
    partner, slot = far // cap, far % cap
    if devices == STAGED:
        partner = partner ^ me[0]
        send_place, receive_place = by_stage(partner, devices) * cap + slot, partner * cap + slot
    else:
        send_place, receive_place = far, far
    is_far = columns >= rows + 2 * size
    forth_t[2 * size :] = counts_t(slots, 0, jnp.where(is_far, receive_place, -1))
    back_t[2 * size :] = counts_t(slots, 0, jnp.where(is_far, send_place, -1))


def decoder_back(me, entries, cotangent, own_t, rim_t, near, outer, inner):
    rows = near.shape[0]
    size = outer.shape[0]
    columns = side_swap(entries[...], rows, size, me[0])
    own = counts_t(rows, 0, columns)
    side = counts_t(2 * size, rows, columns)
    own_t[...] = own
    rim_t[...] = side
    grads = cotangent[...]
    near[...] = mm(own, grads)
    back = mm(side, grads).astype(BF)
    outer[...] = back[:size]
    inner[...] = back[size:]


def emit(outs, rows, size, extra=None):
    inner = outs[0]
    rows = rows.astype(BF)
    inner[:size] = rows[:size]
    used = size
    if extra is not None:
        inner[size : 2 * size] = extra
        used = 2 * size
    far = rows[size:]
    if len(outs) == 2:
        outs[1][...] = far
        return
    block = far.shape[0] // PLANE
    inner[used:] = far[block : 2 * block]
    outs[1][...] = far[:block]
    for k in range(2, PLANE):
        outs[k][...] = far[k * block : (k + 1) * block]


def outer_forth(send, message, *refs, size):
    outer = refs[-1]
    outer[:size] = t_mm(send[:, :size], message[...]).astype(BF)
    if len(refs) == 2:
        outer[size:] = refs[0][...]


def outer_back(back_t, grad, *refs, size):
    outer = refs[-1]
    outer[:size] = mm(back_t[:size], grad[...]).astype(BF)
    if len(refs) == 3:
        send, message = refs[:2]
        outer[size:] = t_mm(send[:, :size], message[...]).astype(BF)


def arrived(ins, size):
    far = list(ins[2:3]) + list(ins[3:])[::-1]
    return jnp.concatenate([ins[0][:size], ins[1][:size]] + [ref[...] for ref in far], axis=0)


def shuffle(own, third, second, first, *outs):
    block = own.shape[0]
    parts = [own[...], first[first.shape[0] - block :], second[...], third[...]]
    rows = jnp.concatenate(parts, axis=0)
    count = rows.shape[0]
    cap = count // (PLANE * len(outs))
    target = lax.broadcasted_iota(jnp.int32, (count, count), 0)
    source = lax.broadcasted_iota(jnp.int32, (count, count), 1)
    place, slot = target // cap, target % cap
    wanted = ((place % PLANE) * len(outs) + place // PLANE) * cap + slot
    moved = mm((source == wanted).astype(F32).astype(BF), rows).astype(BF)
    for m, out in enumerate(outs):
        out[...] = moved[m * PLANE * cap : (m + 1) * PLANE * cap]


def layer_local(hidden, own_t, message, near, *, scale):
    near[...] = hidden[...].astype(F32) + scale * t_mm(own_t[...], message[...])


def back_local(own_t, grad, near):
    near[...] = mm(own_t[...], grad[...])


def first_hidden(near, rim_t, outer_in, inner_in, encoder, weight, send, hidden, message, slope, *outs, size):
    incoming = silu_pair(mm(arrived([outer_in, inner_in], outer_in.shape[0]), encoder[...]))[0].astype(BF)
    state = (near[...] + t_mm(rim_t[...], incoming)).astype(BF)
    hidden[...] = state
    value, gradient = silu_pair(mm(state, weight[0]))
    value = value.astype(BF)
    message[...] = value
    slope[...] = gradient
    emit(outs, t_mm(send[:, size:], value), size)


def next_hidden(near, forth_t, weight, send, inner_extra, *refs, ins, layer, scale, size):
    rows = arrived(refs[:ins], size)
    hidden, message, slope = refs[ins : ins + 3]
    state = (near[...] + scale * t_mm(forth_t[...], rows)).astype(BF)
    hidden[...] = state
    value, gradient = silu_pair(mm(state, weight[layer]))
    value = value.astype(BF)
    message[...] = value
    slope[...] = gradient
    emit(refs[ins + 3 :], t_mm(send[:, size:], value), size, inner_extra[...])


def turn(near, forth_t, weight, send, receive, back_t, back_near, *refs, ins, scale, size):
    rows = arrived(refs[:ins], size)
    message, grad = refs[ins : ins + 2]
    state = (near[...] + scale * t_mm(forth_t[...], rows)).astype(BF)
    value, gradient = silu_pair(mm(state, weight[...]))
    value = value.astype(BF)
    message[...] = value
    returned = jnp.concatenate([refs[0][size : 2 * size], refs[1][size : 2 * size]], axis=0)
    back = back_near[...] + mm(receive[:, : 2 * size], returned)
    change = mm_t((back * gradient).astype(BF), weight[...]).astype(BF)
    grad[...] = change
    rim = t_mm(send[:, size : 2 * size], value).astype(BF)
    emit(refs[ins + 2 :], mm(back_t[size:], change), size, rim)


def layer_back(near, receive, rows, slope, weight, grad, scale):
    total = near[...] + mm(receive[...], rows)
    change = (total * scale * slope[...]).astype(BF)
    return (grad[...].astype(F32) + mm_t(change, weight)).astype(BF)


def middle_back(near, receive, slope, weight, grad, back_t, *refs, ins, layer, scale, size):
    rows = arrived(refs[:ins], size)
    change = layer_back(near, receive, rows, slope, weight[layer], grad, scale)
    refs[ins][...] = change
    emit(refs[ins + 1 :], mm(back_t[size:], change), size)


def last_back(near, receive, slope, weight, grad, grid_rim_t, *refs, ins, scale):
    new_grad, outer, inner = refs[ins:]
    rows = arrived(refs[:ins], refs[0].shape[0])
    change = layer_back(near, receive, rows, slope, weight[0], grad, scale)
    new_grad[...] = change
    back = mm(grid_rim_t[...], change).astype(BF)
    outer[...] = back[: outer.shape[0]]
    inner[...] = back[outer.shape[0] :]


def decode(latent, own_t, rim_t, message, outer_in, inner_in, output):
    size = outer_in.shape[0] // 2
    incoming = jnp.concatenate([outer_in[size:], inner_in[size : 2 * size]], axis=0)
    total = t_mm(own_t[...], message[...]) + t_mm(rim_t[...], incoming)
    output[...] = (latent[...].astype(F32) + total).astype(BF)


def grid_local(me, own_t, grad, lists, slope, weight, cotangent, base, table, slope_rows, mesh_grad):
    mesh_grad[...] = grad[...]
    rows = own_t.shape[0]
    size = lists.shape[2]
    for k, wanted in enumerate(pair_order(lists, me[0])):
        table[:, k * size : (k + 1) * size] = pick(rows, wanted)
    slope_rows[...] = t_mm(table[...], slope[...])
    change = (mm(own_t[...], grad[...]) * slope[...].astype(F32)).astype(BF)
    base[...] = cotangent[...].astype(F32) + mm_t(change, weight[...])


def grid_back(base, table, slope_rows, weight, outer_in, inner_in, output, staging, sems):
    returned = jnp.concatenate([outer_in[...], inner_in[...]], axis=0).astype(F32)
    change = mm_t((returned * slope_rows[...]).astype(BF), weight[...]).astype(BF)
    copies = []
    for i, part in enumerate(row_chunks(base.shape[0])):
        staging[part] = (base[part] + mm(table[part], change)).astype(BF)
        copies.append(pltpu.make_async_copy(staging.at[part], output.at[part], sems.at[i]))
        copies[-1].start()
    for copy in copies:
        copy.wait()


def toggle(value, bits):
    peers = lax.axis_size("dom")
    return lax.ppermute(value, "dom", [(i, i ^ bits) for i in range(peers)])


def across(value):
    peers = lax.axis_size("dom")
    pairs = [(i, (i + 1) % peers if i % 2 else (i - 1) % peers) for i in range(peers)]
    return lax.ppermute(value, "dom", pairs)


def exchange(outer, outs, cap):
    width = outer.shape[1]
    if len(outs) == 2:
        inner, far = outs
        peers = lax.axis_size("dom")
        blocks = far.reshape(peers, cap, width)
        blocks = lax.all_to_all(blocks, "dom", split_axis=0, concat_axis=0, tiled=True)
        return [across(outer), toggle(inner, 1), blocks.reshape(-1, width)]
    inner, own, second, third = outs
    outer_in = across(outer)
    inner_in = toggle(inner, 1)
    second_in = toggle(second, 2)
    third_in = toggle(third, 3)
    columns = STAGED // PLANE
    blocks = call(
        shuffle,
        [((PLANE * cap, width), BF)] * columns,
        2 * (STAGED * cap) ** 2 * width,
        own, third_in, second_in, inner_in,
    )
    moved = [toggle(blocks[m], m * PLANE) for m in reversed(range(1, columns))]
    return [outer_in, inner_in, blocks[0]] + moved


def on_device(
    grid_latent,
    mesh_latent,
    encoder_weight,
    processor_weights,
    decoder_weight,
    cotangent,
    grid_halo_rows,
    encoder_neighbours,
    halo_rows,
    far_sources,
    mesh_neighbours,
    decoder_neighbours,
):
    devices = lax.axis_size("dom")
    grid_rows, width = grid_latent.shape
    mesh_rows = mesh_latent.shape[0]
    ghalo = grid_halo_rows.shape[2]
    halo = halo_rows.shape[2]
    cap = far_sources.shape[2]
    slots = devices * cap
    listed = 2 * halo + slots
    scale = 1.0 / mesh_neighbours.shape[1]
    me = lax.axis_index("dom").astype(jnp.int32).reshape(1)

    def square(rows, depth):
        return 2 * rows * depth * width

    def sends(per_side):
        if devices != STAGED:
            return [((per_side, width), BF), ((slots, width), BF)]
        block = slots // PLANE
        return [((per_side + block, width), BF)] + [((block, width), BF)] * (PLANE - 1)

    state = ((mesh_rows, width), BF)
    total = ((mesh_rows, width), F32)
    rim = ((halo, width), BF)
    wide = ((2 * halo, width), BF)
    grid_rim = ((ghalo, width), BF)
    step = 3 * square(mesh_rows, width)
    rim_flops = square(halo, mesh_rows)
    forth = functools.partial(outer_forth, size=halo)
    back = functools.partial(outer_back, size=halo)

    outer, inner = call(
        grid_send,
        [grid_rim, grid_rim],
        64 * square(grid_rows, width),
        me, grid_latent, grid_halo_rows,
        scalars=1, hbm=2, limit=60 * 1024 * 1024,
        scratch=copies_of([grid_latent, grid_halo_rows]) + [pltpu.SemaphoreType.DMA((CHUNKS + 1,))],
    )
    outer_in, inner_in = across(outer), toggle(inner, 1)

    near, grid_own_t, grid_rim_t, grid_slope, send, receive = call(
        functools.partial(encoder_local, size=ghalo),
        [
            total,
            ((grid_rows, mesh_rows), BF),
            ((2 * ghalo, mesh_rows), BF),
            ((grid_rows, width), BF),
            ((mesh_rows, listed), BF),
            ((mesh_rows, listed), BF),
        ],
        4 * square(grid_rows, width),
        me, encoder_neighbours.T, halo_rows, far_sources[0].T, encoder_weight, grid_latent, mesh_latent,
        scalars=1,
    )

    own_t, forth_t, back_t = call(
        functools.partial(mesh_tables, size=halo, devices=devices),
        [((mesh_rows, mesh_rows), BF)] + [((listed, mesh_rows), BF)] * 2,
        square(mesh_rows, mesh_rows),
        me, mesh_neighbours.T,
        scalars=1,
    )

    hidden, message, slope_0, *outs = call(
        functools.partial(first_hidden, size=halo),
        [state, state, total] + sends(halo),
        step,
        near, grid_rim_t, outer_in, inner_in, encoder_weight, processor_weights, send, back_t,
        free=1,
    )
    (outer,) = call(forth, [rim], rim_flops, send, message)
    local = functools.partial(layer_local, scale=scale)
    ins = exchange(outer, outs, cap)
    (near,) = call(local, [total], square(mesh_rows, mesh_rows), hidden, own_t, message, ins[2], free=1)
    decoder_own_t, decoder_rim_t, decoder_near, outer_extra, inner_extra = call(
        decoder_back,
        [((mesh_rows, grid_rows), BF), ((2 * halo, grid_rows), BF), total, rim, rim],
        square(grid_rows, mesh_rows),
        me, decoder_neighbours.T, cotangent, ins[2],
        scalars=1, free=1,
    )

    hidden, message, slope_1, *outs = call(
        functools.partial(next_hidden, ins=len(ins), layer=1, scale=scale, size=halo),
        [state, state, total] + sends(2 * halo),
        step,
        near, forth_t, processor_weights, send, inner_extra, *ins,
    )
    (outer,) = call(forth, [wide], rim_flops, send, message, outer_extra)
    (near,) = call(local, [total], 6 * square(mesh_rows, mesh_rows), hidden, own_t, message)
    ins = exchange(outer, outs, cap)

    message, grad, *outs = call(
        functools.partial(turn, ins=len(ins), scale=scale, size=halo),
        [state, state] + sends(2 * halo),
        2 * step,
        near, forth_t, decoder_weight, send, receive, back_t, decoder_near, *ins,
    )
    (outer,) = call(back, [wide], rim_flops, back_t, grad, send, message)
    (near,) = call(back_local, [total], 6 * square(mesh_rows, mesh_rows), own_t, grad)
    ins = exchange(outer, outs, cap)
    outer_decoder, inner_decoder = ins[:2]

    grad, *outs = call(
        functools.partial(middle_back, ins=len(ins), layer=1, scale=scale, size=halo),
        [state] + sends(halo),
        step,
        near, receive, slope_1, processor_weights, grad, back_t, *ins,
    )
    (outer,) = call(back, [rim], rim_flops, back_t, grad)
    (near,) = call(back_local, [total], 6 * square(mesh_rows, mesh_rows), own_t, grad)
    ins = exchange(outer, outs, cap)
    grad, outer, inner = call(
        functools.partial(last_back, ins=len(ins), scale=scale),
        [state, grid_rim, grid_rim],
        step,
        near, receive, slope_0, processor_weights, grad, grid_rim_t, *ins,
    )
    outer_in, inner_in = across(outer), toggle(inner, 1)
    (output,) = call(
        decode,
        [((grid_rows, width), BF)],
        square(grid_rows, mesh_rows),
        grid_latent, decoder_own_t, decoder_rim_t, message, outer_decoder, inner_decoder, grad,
        free=1,
    )
    base, table, slope_rows, mesh_grad = call(
        grid_local,
        [((grid_rows, width), F32), ((grid_rows, 2 * ghalo), BF), ((2 * ghalo, width), F32), state],
        square(mesh_rows, grid_rows) + square(grid_rows, width),
        me, grid_own_t, grad, grid_halo_rows, grid_slope, encoder_weight, cotangent,
        scalars=1,
    )
    (grid_grad,) = call(
        grid_back,
        [((grid_rows, width), BF)],
        square(grid_rows, 4 * ghalo),
        base, table, slope_rows, encoder_weight, outer_in, inner_in,
        hbm_out=1,
        scratch=[pltpu.VMEM((grid_rows, width), BF), pltpu.SemaphoreType.DMA((CHUNKS,))],
    )
    return (output, grid_grad, mesh_grad)


def solution(mesh):
    in_specs = (
        P(("groups", "dom"), None),
        P(("groups", "dom"), None),
        P(),
        P(),
        P(),
        P(("groups", "dom"), None),
        P("dom", None, None),
        P("dom", None),
        P("dom", None, None),
        P("dom", None, None),
        P("dom", None),
        P("dom", None),
    )
    out_specs = (P(("groups", "dom"), None), P(("groups", "dom"), None), P(("groups", "dom"), None))
    return jax.shard_map(
        on_device, mesh=mesh, in_specs=in_specs, out_specs=out_specs, check_vma=False
    )
```

```python
import functools

import jax
import jax.numpy as jnp
from jax import lax
from jax.experimental import pallas as pl
from jax.experimental.pallas import tpu as pltpu
from jax.sharding import PartitionSpec as P

BF = jnp.bfloat16
F32 = jnp.float32
VMEM_LIMIT = 24 * 1024 * 1024
PLANE = 4
STAGED = 16
CHUNKS = 4


def mm(a, b):
    return jnp.dot(a, b, preferred_element_type=F32)


def mm_t(a, b):
    return lax.dot_general(a, b, (((1,), (1,)), ((), ())), preferred_element_type=F32)


def t_mm(a, b):
    return lax.dot_general(a, b, (((0,), (0,)), ((), ())), preferred_element_type=F32)


def silu_pair(value):
    sigma = 0.5 + 0.5 * jnp.tanh(0.5 * value)
    message = value * sigma
    return message, sigma + message * (1.0 - sigma)


def pick(rows, wanted):
    places = lax.broadcasted_iota(jnp.int32, (rows, wanted.shape[1]), 0)
    return (places == wanted).astype(F32).astype(BF)


def counts_t(columns, first, entries):
    degree, rows = entries.shape
    places = lax.broadcasted_iota(jnp.int32, (columns, rows), 0) + first
    total = jnp.zeros((columns, rows), F32)
    for k in range(degree):
        total = total + (places == entries[k : k + 1]).astype(F32)
    return total.astype(BF)


def side_swap(entries, rows, size, me):
    swapped = jnp.where(entries < rows + size, entries + size, entries - size)
    rim = (entries >= rows) & (entries < rows + 2 * size)
    return jnp.where(rim & (me % 2 == 1), swapped, entries)


def pair_order(lists, me):
    left, right = lists[0, 0:1], lists[0, 1:2]
    odd = me % 2
    return left + odd * (right - left), right + odd * (left - right)


def by_stage(x, devices):
    return (x % PLANE) * (devices // PLANE) + x // PLANE


def call(body, out_shapes, flops, *args, scalars=0, hbm=0, free=0, hbm_out=0, scratch=(), limit=VMEM_LIMIT):
    shapes = [jax.ShapeDtypeStruct(s, t) for s, t in out_shapes]
    size = sum(a.size * a.dtype.itemsize for a in args)
    size += sum(s.size * s.dtype.itemsize for s in shapes)
    size *= hbm == 0
    places = [pltpu.SMEM] * scalars + [pltpu.HBM] * hbm + [pltpu.VMEM] * (len(args) - scalars - hbm - free)
    places += [pl.ANY] * free
    out_places = [pltpu.HBM] * hbm_out + [pltpu.VMEM] * (len(shapes) - hbm_out)
    kept = len(args) - free
    inner = body if free == 0 else lambda *refs: body(*refs[:kept], *refs[len(args) :])
    return pl.pallas_call(
        inner,
        out_shape=shapes,
        in_specs=[pl.BlockSpec(memory_space=place) for place in places],
        out_specs=[pl.BlockSpec(memory_space=place) for place in out_places],
        scratch_shapes=list(scratch),
        compiler_params=pltpu.CompilerParams(vmem_limit_bytes=limit),
        cost_estimate=pl.CostEstimate(flops=flops, bytes_accessed=size, transcendentals=0),
    )(*args)


def copies_of(arrays):
    return [pltpu.VMEM(a.shape, a.dtype) for a in arrays]


def fetch(sources, targets, sems):
    copies = [pltpu.make_async_copy(s, t, sems.at[i]) for i, (s, t) in enumerate(zip(sources, targets))]
    for copy in copies:
        copy.start()
    return copies


def row_chunks(rows):
    step = rows // CHUNKS
    return [pl.ds(i * step, step) for i in range(CHUNKS)]


def grid_send(me, latent, lists, outer, inner, values, wanted, sems):
    parts = row_chunks(latent.shape[0])
    sources = [lists] + [latent.at[part] for part in parts]
    copies = fetch(sources, [wanted] + [values.at[part] for part in parts], sems)
    copies[0].wait()
    wanted_outer, wanted_inner = pair_order(wanted, me[0])
    step = latent.shape[0] // CHUNKS
    outer_rows = inner_rows = 0.0
    for i, part in enumerate(parts):
        copies[i + 1].wait()
        chunk = values[part]
        outer_rows += t_mm(pick(step, wanted_outer - i * step), chunk)
        inner_rows += t_mm(pick(step, wanted_inner - i * step), chunk)
    outer[...] = outer_rows.astype(BF)
    inner[...] = inner_rows.astype(BF)


def encoder_local(me, entries, lists, far_lists, weight, latent, mesh,
                  near, grid_own_t, grid_rim_t, slope, send, receive, *, size):
    rows = latent.shape[0]
    columns = side_swap(entries[...], rows, size, me[0])
    own = counts_t(rows, 0, columns)
    grid_own_t[...] = own
    grid_rim_t[...] = counts_t(2 * size, rows, columns)
    list_tables(me, lists, far_lists, send, receive)
    message, gradient = silu_pair(mm(latent[...], weight[...]))
    slope[...] = gradient.astype(BF)
    near[...] = mesh[...].astype(F32) + t_mm(own, message.astype(BF))


def list_tables(me, lists, far_lists, send, receive):
    rows = send.shape[0]
    size = lists.shape[2]
    cap, devices = far_lists.shape
    outer, inner = pair_order(lists, me[0])
    rim = [pick(rows, outer), pick(rows, inner)]
    for k in range(2):
        send[:, k * size : (k + 1) * size] = rim[k]
        receive[:, k * size : (k + 1) * size] = rim[k]
    partner = lax.broadcasted_iota(jnp.int32, (devices, devices * cap), 0)
    place = lax.broadcasted_iota(jnp.int32, (devices, devices * cap), 1)
    if devices == STAGED:
        x = partner ^ me[0]
        send_place, receive_place = x * cap, by_stage(x, devices) * cap
    else:
        send_place, receive_place = partner * cap, partner * cap
    send_far = jnp.zeros((rows, devices * cap), F32)
    receive_far = jnp.zeros((rows, devices * cap), F32)
    for j in range(cap):
        chosen = pick(rows, far_lists[j : j + 1])
        send_far += mm(chosen, (place == send_place + j).astype(F32).astype(BF))
        receive_far += mm(chosen, (place == receive_place + j).astype(F32).astype(BF))
    send[:, 2 * size :] = send_far.astype(BF)
    receive[:, 2 * size :] = receive_far.astype(BF)


def mesh_tables(me, entries, own_t, forth_t, back_t, *, size, devices):
    rows = own_t.shape[0]
    slots = forth_t.shape[0] - 2 * size
    cap = slots // devices
    columns = side_swap(entries[...], rows, size, me[0])
    own_t[...] = counts_t(rows, 0, columns)
    rim = counts_t(2 * size, rows, columns)
    forth_t[: 2 * size] = rim
    back_t[: 2 * size] = rim
    far = jnp.maximum(columns - rows - 2 * size, 0)
    partner, slot = far // cap, far % cap
    if devices == STAGED:
        partner = partner ^ me[0]
        send_place, receive_place = partner * cap + slot, by_stage(partner, devices) * cap + slot
    else:
        send_place, receive_place = far, far
    is_far = columns >= rows + 2 * size
    forth_t[2 * size :] = counts_t(slots, 0, jnp.where(is_far, receive_place, -1))
    back_t[2 * size :] = counts_t(slots, 0, jnp.where(is_far, send_place, -1))


def decoder_back(me, entries, cotangent, own_t, rim_t, near, outer, inner):
    rows = near.shape[0]
    size = outer.shape[0]
    columns = side_swap(entries[...], rows, size, me[0])
    own = counts_t(rows, 0, columns)
    side = counts_t(2 * size, rows, columns)
    own_t[...] = own
    rim_t[...] = side
    grads = cotangent[...]
    near[...] = mm(own, grads)
    back = mm(side, grads).astype(BF)
    outer[...] = back[:size]
    inner[...] = back[size:]


def emit(outs, rows, size, extra=None):
    inner = outs[0]
    rows = rows.astype(BF)
    inner[:size] = rows[:size]
    if extra is not None:
        inner[size:] = extra
    far = rows[size:]
    block = far.shape[0] // (len(outs) - 1)
    for m, out in enumerate(outs[1:]):
        out[...] = far[m * block : (m + 1) * block]


def outer_forth(send, message, *refs, size):
    outer = refs[-1]
    outer[:size] = t_mm(send[:, :size], message[...]).astype(BF)
    if len(refs) == 2:
        outer[size:] = refs[0][...]


def outer_back(back_t, grad, *refs, size):
    outer = refs[-1]
    outer[:size] = mm(back_t[:size], grad[...]).astype(BF)
    if len(refs) == 3:
        send, message = refs[:2]
        outer[size:] = t_mm(send[:, :size], message[...]).astype(BF)


def arrived(ins, size):
    outer, inner = ins[:2]
    parts = [outer[:size], inner[:size]]
    if len(ins) > 3:
        third, second, own = ins[2:]
        parts += [own[...], inner[inner.shape[0] - own.shape[0] :], second[...], third[...]]
    else:
        parts += [ref[...] for ref in ins[2:]]
    return jnp.concatenate(parts, axis=0)


def shuffle(inner, own, *refs):
    columns = STAGED // PLANE
    parts = [own[...]] + [ref[...] for ref in refs[: columns - 1][::-1]]
    rows = jnp.concatenate(parts, axis=0)
    outs = refs[columns - 1 :]
    count = rows.shape[0]
    cap = count // STAGED
    target = lax.broadcasted_iota(jnp.int32, (count, count), 0)
    source = lax.broadcasted_iota(jnp.int32, (count, count), 1)
    place, slot = target // cap, target % cap
    wanted = ((place % columns) * PLANE + place // columns) * cap + slot
    moved = mm((source == wanted).astype(F32).astype(BF), rows).astype(BF)
    block = columns * cap
    used = inner.shape[0]
    outs[1][:used] = inner[...]
    outs[1][used:] = moved[block : 2 * block]
    for k in (0, 2, 3):
        outs[k][...] = moved[k * block : (k + 1) * block]


def layer_local(hidden, own_t, message, near, *, scale):
    near[...] = hidden[...].astype(F32) + scale * t_mm(own_t[...], message[...])


def back_local(own_t, grad, near):
    near[...] = mm(own_t[...], grad[...])


def first_hidden(near, rim_t, outer_in, inner_in, encoder, weight, send, hidden, message, slope, *outs, size):
    incoming = silu_pair(mm(arrived([outer_in, inner_in], outer_in.shape[0]), encoder[...]))[0].astype(BF)
    state = (near[...] + t_mm(rim_t[...], incoming)).astype(BF)
    hidden[...] = state
    value, gradient = silu_pair(mm(state, weight[0]))
    value = value.astype(BF)
    message[...] = value
    slope[...] = gradient
    emit(outs, t_mm(send[:, size:], value), size)


def next_hidden(near, forth_t, weight, send, inner_extra, *refs, ins, layer, scale, size):
    rows = arrived(refs[:ins], size)
    hidden, message, slope = refs[ins : ins + 3]
    state = (near[...] + scale * t_mm(forth_t[...], rows)).astype(BF)
    hidden[...] = state
    value, gradient = silu_pair(mm(state, weight[layer]))
    value = value.astype(BF)
    message[...] = value
    slope[...] = gradient
    emit(refs[ins + 3 :], t_mm(send[:, size:], value), size, inner_extra[...])


def turn(near, forth_t, weight, send, receive, back_t, back_near, *refs, ins, scale, size):
    rows = arrived(refs[:ins], size)
    message, grad = refs[ins : ins + 2]
    state = (near[...] + scale * t_mm(forth_t[...], rows)).astype(BF)
    value, gradient = silu_pair(mm(state, weight[...]))
    value = value.astype(BF)
    message[...] = value
    returned = jnp.concatenate([refs[0][size : 2 * size], refs[1][size : 2 * size]], axis=0)
    back = back_near[...] + mm(receive[:, : 2 * size], returned)
    change = mm_t((back * gradient).astype(BF), weight[...]).astype(BF)
    grad[...] = change
    rim = t_mm(send[:, size : 2 * size], value).astype(BF)
    emit(refs[ins + 2 :], mm(back_t[size:], change), size, rim)


def layer_back(near, receive, rows, slope, weight, grad, scale):
    total = near[...] + mm(receive[...], rows)
    change = (total * scale * slope[...]).astype(BF)
    return (grad[...].astype(F32) + mm_t(change, weight)).astype(BF)


def middle_back(near, receive, slope, weight, grad, back_t, *refs, ins, layer, scale, size):
    rows = arrived(refs[:ins], size)
    change = layer_back(near, receive, rows, slope, weight[layer], grad, scale)
    refs[ins][...] = change
    emit(refs[ins + 1 :], mm(back_t[size:], change), size)


def last_back(near, receive, slope, weight, grad, grid_rim_t, *refs, ins, scale):
    new_grad, outer, inner = refs[ins:]
    rows = arrived(refs[:ins], refs[0].shape[0])
    change = layer_back(near, receive, rows, slope, weight[0], grad, scale)
    new_grad[...] = change
    back = mm(grid_rim_t[...], change).astype(BF)
    outer[...] = back[: outer.shape[0]]
    inner[...] = back[outer.shape[0] :]


def decode(latent, own_t, rim_t, message, outer_in, inner_in, output):
    size = outer_in.shape[0] // 2
    incoming = jnp.concatenate([outer_in[size:], inner_in[size : 2 * size]], axis=0)
    total = t_mm(own_t[...], message[...]) + t_mm(rim_t[...], incoming)
    output[...] = (latent[...].astype(F32) + total).astype(BF)


def grid_local(me, own_t, grad, lists, slope, weight, cotangent, base, table, slope_rows, mesh_grad):
    mesh_grad[...] = grad[...]
    rows = own_t.shape[0]
    size = lists.shape[2]
    for k, wanted in enumerate(pair_order(lists, me[0])):
        table[:, k * size : (k + 1) * size] = pick(rows, wanted)
    slope_rows[...] = t_mm(table[...], slope[...])
    change = (mm(own_t[...], grad[...]) * slope[...].astype(F32)).astype(BF)
    base[...] = cotangent[...].astype(F32) + mm_t(change, weight[...])


def grid_back(base, table, slope_rows, weight, outer_in, inner_in, output, staging, sems):
    returned = jnp.concatenate([outer_in[...], inner_in[...]], axis=0).astype(F32)
    change = mm_t((returned * slope_rows[...]).astype(BF), weight[...]).astype(BF)
    copies = []
    for i, part in enumerate(row_chunks(base.shape[0])):
        staging[part] = (base[part] + mm(table[part], change)).astype(BF)
        copies.append(pltpu.make_async_copy(staging.at[part], output.at[part], sems.at[i]))
        copies[-1].start()
    for copy in copies:
        copy.wait()


def toggle(value, bits):
    peers = lax.axis_size("dom")
    return lax.ppermute(value, "dom", [(i, i ^ bits) for i in range(peers)])


def across(value):
    peers = lax.axis_size("dom")
    pairs = [(i, (i + 1) % peers if i % 2 else (i - 1) % peers) for i in range(peers)]
    return lax.ppermute(value, "dom", pairs)


def exchange(outer, outs, cap):
    width = outer.shape[1]
    if len(outs) == 2:
        inner, far = outs
        peers = lax.axis_size("dom")
        blocks = far.reshape(peers, cap, width)
        blocks = lax.all_to_all(blocks, "dom", split_axis=0, concat_axis=0, tiled=True)
        return [across(outer), toggle(inner, 1), blocks.reshape(-1, width)]
    inner, own, *rest = outs
    columns = STAGED // PLANE
    moved = [toggle(rest[m - 1], m * PLANE) for m in reversed(range(1, columns))]
    outer_in = across(outer)
    block = columns * cap
    blocks = call(
        shuffle,
        [((block, width), BF), ((inner.shape[0] + block, width), BF), ((block, width), BF), ((block, width), BF)],
        2 * (STAGED * cap) ** 2 * width,
        inner, own, *moved,
    )
    return [outer_in, toggle(blocks[1], 1), toggle(blocks[3], 3), toggle(blocks[2], 2), blocks[0]]


def on_device(
    grid_latent,
    mesh_latent,
    encoder_weight,
    processor_weights,
    decoder_weight,
    cotangent,
    grid_halo_rows,
    encoder_neighbours,
    halo_rows,
    far_sources,
    mesh_neighbours,
    decoder_neighbours,
):
    devices = lax.axis_size("dom")
    grid_rows, width = grid_latent.shape
    mesh_rows = mesh_latent.shape[0]
    ghalo = grid_halo_rows.shape[2]
    halo = halo_rows.shape[2]
    cap = far_sources.shape[2]
    slots = devices * cap
    listed = 2 * halo + slots
    scale = 1.0 / mesh_neighbours.shape[1]
    me = lax.axis_index("dom").astype(jnp.int32).reshape(1)

    def square(rows, depth):
        return 2 * rows * depth * width

    def sends(per_side):
        stages = STAGED // PLANE if devices == STAGED else 1
        return [((per_side, width), BF)] + [((slots // stages, width), BF)] * stages

    state = ((mesh_rows, width), BF)
    total = ((mesh_rows, width), F32)
    rim = ((halo, width), BF)
    wide = ((2 * halo, width), BF)
    grid_rim = ((ghalo, width), BF)
    step = 3 * square(mesh_rows, width)
    rim_flops = square(halo, mesh_rows)
    forth = functools.partial(outer_forth, size=halo)
    back = functools.partial(outer_back, size=halo)

    outer, inner = call(
        grid_send,
        [grid_rim, grid_rim],
        64 * square(grid_rows, width),
        me, grid_latent, grid_halo_rows,
        scalars=1, hbm=2, limit=60 * 1024 * 1024,
        scratch=copies_of([grid_latent, grid_halo_rows]) + [pltpu.SemaphoreType.DMA((CHUNKS + 1,))],
    )
    outer_in, inner_in = across(outer), toggle(inner, 1)

    near, grid_own_t, grid_rim_t, grid_slope, send, receive = call(
        functools.partial(encoder_local, size=ghalo),
        [
            total,
            ((grid_rows, mesh_rows), BF),
            ((2 * ghalo, mesh_rows), BF),
            ((grid_rows, width), BF),
            ((mesh_rows, listed), BF),
            ((mesh_rows, listed), BF),
        ],
        4 * square(grid_rows, width),
        me, encoder_neighbours.T, halo_rows, far_sources[0].T, encoder_weight, grid_latent, mesh_latent,
        scalars=1,
    )

    own_t, forth_t, back_t = call(
        functools.partial(mesh_tables, size=halo, devices=devices),
        [((mesh_rows, mesh_rows), BF)] + [((listed, mesh_rows), BF)] * 2,
        square(mesh_rows, mesh_rows),
        me, mesh_neighbours.T,
        scalars=1,
    )

    hidden, message, slope_0, *outs = call(
        functools.partial(first_hidden, size=halo),
        [state, state, total] + sends(halo),
        step,
        near, grid_rim_t, outer_in, inner_in, encoder_weight, processor_weights, send, back_t,
        free=1,
    )
    (outer,) = call(forth, [rim], rim_flops, send, message)
    local = functools.partial(layer_local, scale=scale)
    ins = exchange(outer, outs, cap)
    (near,) = call(local, [total], 6 * square(mesh_rows, mesh_rows), hidden, own_t, message, ins[-1], free=1)
    decoder_own_t, decoder_rim_t, decoder_near, outer_extra, inner_extra = call(
        decoder_back,
        [((mesh_rows, grid_rows), BF), ((2 * halo, grid_rows), BF), total, rim, rim],
        square(grid_rows, mesh_rows),
        me, decoder_neighbours.T, cotangent, ins[-1],
        scalars=1, free=1,
    )

    hidden, message, slope_1, *outs = call(
        functools.partial(next_hidden, ins=len(ins), layer=1, scale=scale, size=halo),
        [state, state, total] + sends(2 * halo),
        step,
        near, forth_t, processor_weights, send, inner_extra, *ins,
    )
    (outer,) = call(forth, [wide], rim_flops, send, message, outer_extra)
    (near,) = call(local, [total], 6 * square(mesh_rows, mesh_rows), hidden, own_t, message)
    ins = exchange(outer, outs, cap)

    message, grad, *outs = call(
        functools.partial(turn, ins=len(ins), scale=scale, size=halo),
        [state, state] + sends(2 * halo),
        2 * step,
        near, forth_t, decoder_weight, send, receive, back_t, decoder_near, *ins,
    )
    (outer,) = call(back, [wide], rim_flops, back_t, grad, send, message)
    (near,) = call(back_local, [total], 6 * square(mesh_rows, mesh_rows), own_t, grad)
    ins = exchange(outer, outs, cap)
    outer_decoder, inner_decoder = ins[:2]

    grad, *outs = call(
        functools.partial(middle_back, ins=len(ins), layer=1, scale=scale, size=halo),
        [state] + sends(halo),
        step,
        near, receive, slope_1, processor_weights, grad, back_t, *ins,
    )
    (outer,) = call(back, [rim], rim_flops, back_t, grad)
    (near,) = call(back_local, [total], 6 * square(mesh_rows, mesh_rows), own_t, grad)
    ins = exchange(outer, outs, cap)
    grad, outer, inner = call(
        functools.partial(last_back, ins=len(ins), scale=scale),
        [state, grid_rim, grid_rim],
        step,
        near, receive, slope_0, processor_weights, grad, grid_rim_t, *ins,
    )
    outer_in, inner_in = across(outer), toggle(inner, 1)
    (output,) = call(
        decode,
        [((grid_rows, width), BF)],
        square(grid_rows, mesh_rows),
        grid_latent, decoder_own_t, decoder_rim_t, message, outer_decoder, inner_decoder, grad,
        free=1,
    )
    base, table, slope_rows, mesh_grad = call(
        grid_local,
        [((grid_rows, width), F32), ((grid_rows, 2 * ghalo), BF), ((2 * ghalo, width), F32), state],
        square(mesh_rows, grid_rows) + square(grid_rows, width),
        me, grid_own_t, grad, grid_halo_rows, grid_slope, encoder_weight, cotangent,
        scalars=1,
    )
    (grid_grad,) = call(
        grid_back,
        [((grid_rows, width), BF)],
        square(grid_rows, 4 * ghalo),
        base, table, slope_rows, encoder_weight, outer_in, inner_in,
        hbm_out=1,
        scratch=[pltpu.VMEM((grid_rows, width), BF), pltpu.SemaphoreType.DMA((CHUNKS,))],
    )
    return (output, grid_grad, mesh_grad)


def solution(mesh):
    in_specs = (
        P(("groups", "dom"), None),
        P(("groups", "dom"), None),
        P(),
        P(),
        P(),
        P(("groups", "dom"), None),
        P("dom", None, None),
        P("dom", None),
        P("dom", None, None),
        P("dom", None, None),
        P("dom", None),
        P("dom", None),
    )
    out_specs = (P(("groups", "dom"), None), P(("groups", "dom"), None), P(("groups", "dom"), None))
    return jax.shard_map(
        on_device, mesh=mesh, in_specs=in_specs, out_specs=out_specs, check_vma=False
    )
```

```python
import functools

import jax
import jax.numpy as jnp
from jax import lax
from jax.experimental import pallas as pl
from jax.experimental.pallas import tpu as pltpu
from jax.sharding import PartitionSpec as P

BF = jnp.bfloat16
F32 = jnp.float32
VMEM_LIMIT = 24 * 1024 * 1024
PLANE = 4
STAGED = 16
CHUNKS = 4


def mm(a, b):
    return jnp.dot(a, b, preferred_element_type=F32)


def mm_t(a, b):
    return lax.dot_general(a, b, (((1,), (1,)), ((), ())), preferred_element_type=F32)


def t_mm(a, b):
    return lax.dot_general(a, b, (((0,), (0,)), ((), ())), preferred_element_type=F32)


def silu_pair(value):
    sigma = 0.5 + 0.5 * jnp.tanh(0.5 * value)
    message = value * sigma
    return message, sigma + message * (1.0 - sigma)


def pick(rows, wanted):
    places = lax.broadcasted_iota(jnp.int32, (rows, wanted.shape[1]), 0)
    return (places == wanted).astype(F32).astype(BF)


def counts_t(columns, first, entries):
    degree, rows = entries.shape
    places = lax.broadcasted_iota(jnp.int32, (columns, rows), 0) + first
    total = jnp.zeros((columns, rows), F32)
    for k in range(degree):
        total = total + (places == entries[k : k + 1]).astype(F32)
    return total.astype(BF)


def side_swap(entries, rows, size, me):
    swapped = jnp.where(entries < rows + size, entries + size, entries - size)
    rim = (entries >= rows) & (entries < rows + 2 * size)
    return jnp.where(rim & (me % 2 == 1), swapped, entries)


def pair_order(lists, me):
    left, right = lists[0, 0:1], lists[0, 1:2]
    odd = me % 2
    return left + odd * (right - left), right + odd * (left - right)


def by_stage(x, devices):
    return (x % PLANE) * (devices // PLANE) + x // PLANE


def call(body, out_shapes, flops, *args, scalars=0, hbm=0, free=0, hbm_out=0, scratch=(), limit=VMEM_LIMIT):
    shapes = [jax.ShapeDtypeStruct(s, t) for s, t in out_shapes]
    size = sum(a.size * a.dtype.itemsize for a in args)
    size += sum(s.size * s.dtype.itemsize for s in shapes)
    size *= hbm == 0
    places = [pltpu.SMEM] * scalars + [pltpu.HBM] * hbm + [pltpu.VMEM] * (len(args) - scalars - hbm - free)
    places += [pl.ANY] * free
    out_places = [pltpu.HBM] * hbm_out + [pltpu.VMEM] * (len(shapes) - hbm_out)
    kept = len(args) - free
    inner = body if free == 0 else lambda *refs: body(*refs[:kept], *refs[len(args) :])
    return pl.pallas_call(
        inner,
        out_shape=shapes,
        in_specs=[pl.BlockSpec(memory_space=place) for place in places],
        out_specs=[pl.BlockSpec(memory_space=place) for place in out_places],
        scratch_shapes=list(scratch),
        compiler_params=pltpu.CompilerParams(vmem_limit_bytes=limit),
        cost_estimate=pl.CostEstimate(flops=flops, bytes_accessed=size, transcendentals=0),
    )(*args)


def copies_of(arrays):
    return [pltpu.VMEM(a.shape, a.dtype) for a in arrays]


def fetch(sources, targets, sems):
    copies = [pltpu.make_async_copy(s, t, sems.at[i]) for i, (s, t) in enumerate(zip(sources, targets))]
    for copy in copies:
        copy.start()
    return copies


def row_chunks(rows):
    step = rows // CHUNKS
    return [pl.ds(i * step, step) for i in range(CHUNKS)]


def grid_send(me, latent, lists, outer, inner, values, wanted, sems):
    parts = row_chunks(latent.shape[0])
    sources = [lists] + [latent.at[part] for part in parts]
    copies = fetch(sources, [wanted] + [values.at[part] for part in parts], sems)
    copies[0].wait()
    wanted_outer, wanted_inner = pair_order(wanted, me[0])
    step = latent.shape[0] // CHUNKS
    outer_rows = inner_rows = 0.0
    for i, part in enumerate(parts):
        copies[i + 1].wait()
        chunk = values[part]
        outer_rows += t_mm(pick(step, wanted_outer - i * step), chunk)
        inner_rows += t_mm(pick(step, wanted_inner - i * step), chunk)
    outer[...] = outer_rows.astype(BF)
    inner[...] = inner_rows.astype(BF)


def encoder_local(me, entries, lists, far_lists, weight, latent, mesh,
                  near, grid_own_t, grid_rim_t, slope, send, receive, *, size):
    rows = latent.shape[0]
    columns = side_swap(entries[...], rows, size, me[0])
    own = counts_t(rows, 0, columns)
    grid_own_t[...] = own
    grid_rim_t[...] = counts_t(2 * size, rows, columns)
    list_tables(me, lists, far_lists, send, receive)
    message, gradient = silu_pair(mm(latent[...], weight[...]))
    slope[...] = gradient.astype(BF)
    near[...] = mesh[...].astype(F32) + t_mm(own, message.astype(BF))


def list_tables(me, lists, far_lists, send, receive):
    rows = send.shape[0]
    size = lists.shape[2]
    cap, devices = far_lists.shape
    outer, inner = pair_order(lists, me[0])
    rim = [pick(rows, outer), pick(rows, inner)]
    for k in range(2):
        send[:, k * size : (k + 1) * size] = rim[k]
        receive[:, k * size : (k + 1) * size] = rim[k]
    partner = lax.broadcasted_iota(jnp.int32, (devices, devices * cap), 0)
    place = lax.broadcasted_iota(jnp.int32, (devices, devices * cap), 1)
    if devices == STAGED:
        x = partner ^ me[0]
        send_place, receive_place = x * cap, by_stage(x, devices) * cap
    else:
        send_place, receive_place = partner * cap, partner * cap
    send_far = jnp.zeros((rows, devices * cap), F32)
    receive_far = jnp.zeros((rows, devices * cap), F32)
    for j in range(cap):
        chosen = pick(rows, far_lists[j : j + 1])
        send_far += mm(chosen, (place == send_place + j).astype(F32).astype(BF))
        receive_far += mm(chosen, (place == receive_place + j).astype(F32).astype(BF))
    send[:, 2 * size :] = send_far.astype(BF)
    receive[:, 2 * size :] = receive_far.astype(BF)


def mesh_tables(me, entries, own_t, forth_t, back_t, *, size, devices):
    rows = own_t.shape[0]
    slots = forth_t.shape[0] - 2 * size
    cap = slots // devices
    columns = side_swap(entries[...], rows, size, me[0])
    own_t[...] = counts_t(rows, 0, columns)
    rim = counts_t(2 * size, rows, columns)
    forth_t[: 2 * size] = rim
    back_t[: 2 * size] = rim
    far = jnp.maximum(columns - rows - 2 * size, 0)
    partner, slot = far // cap, far % cap
    if devices == STAGED:
        partner = partner ^ me[0]
        send_place, receive_place = partner * cap + slot, by_stage(partner, devices) * cap + slot
    else:
        send_place, receive_place = far, far
    is_far = columns >= rows + 2 * size
    forth_t[2 * size :] = counts_t(slots, 0, jnp.where(is_far, receive_place, -1))
    back_t[2 * size :] = counts_t(slots, 0, jnp.where(is_far, send_place, -1))


def decoder_back(me, entries, cotangent, own_t, rim_t, near, outer, inner):
    rows = near.shape[0]
    size = outer.shape[0]
    columns = side_swap(entries[...], rows, size, me[0])
    own = counts_t(rows, 0, columns)
    side = counts_t(2 * size, rows, columns)
    own_t[...] = own
    rim_t[...] = side
    grads = cotangent[...]
    near[...] = mm(own, grads)
    back = mm(side, grads).astype(BF)
    outer[...] = back[:size]
    inner[...] = back[size:]


def emit(outs, rows, size, extra=None):
    rows = rows.astype(BF)
    for k in range(2):
        outs[k][:size] = rows[k * size : (k + 1) * size]
        if extra is not None:
            outs[k][size:] = extra[k]
    far = rows[2 * size :]
    block = far.shape[0] // (len(outs) - 2)
    for m, out in enumerate(outs[2:]):
        out[...] = far[m * block : (m + 1) * block]


def arrived(ins, size):
    outer, inner = ins[:2]
    parts = [outer[:size], inner[:size]]
    if len(ins) > 3:
        third, second, own = ins[2:]
        parts += [own[...], inner[inner.shape[0] - own.shape[0] :], second[...], third[...]]
    else:
        parts += [ref[...] for ref in ins[2:]]
    return jnp.concatenate(parts, axis=0)


def shuffle(inner, own, *refs):
    columns = STAGED // PLANE
    parts = [own[...]] + [ref[...] for ref in refs[: columns - 1][::-1]]
    rows = jnp.concatenate(parts, axis=0)
    outs = refs[columns - 1 :]
    count = rows.shape[0]
    cap = count // STAGED
    target = lax.broadcasted_iota(jnp.int32, (count, count), 0)
    source = lax.broadcasted_iota(jnp.int32, (count, count), 1)
    place, slot = target // cap, target % cap
    wanted = ((place % columns) * PLANE + place // columns) * cap + slot
    moved = mm((source == wanted).astype(F32).astype(BF), rows).astype(BF)
    block = columns * cap
    used = inner.shape[0]
    outs[1][:used] = inner[...]
    outs[1][used:] = moved[block : 2 * block]
    for k in (0, 2, 3):
        outs[k][...] = moved[k * block : (k + 1) * block]


def layer_local(hidden, own_t, message, near, *, scale):
    near[...] = hidden[...].astype(F32) + scale * t_mm(own_t[...], message[...])


def back_local(own_t, grad, near):
    near[...] = mm(own_t[...], grad[...])


def first_hidden(near, rim_t, outer_in, inner_in, encoder, weight, send, hidden, message, slope, *outs, size):
    incoming = silu_pair(mm(arrived([outer_in, inner_in], outer_in.shape[0]), encoder[...]))[0].astype(BF)
    state = (near[...] + t_mm(rim_t[...], incoming)).astype(BF)
    hidden[...] = state
    value, gradient = silu_pair(mm(state, weight[0]))
    value = value.astype(BF)
    message[...] = value
    slope[...] = gradient
    emit(outs, t_mm(send[...], value), size)


def next_hidden(near, forth_t, weight, send, outer_extra, inner_extra, *refs, ins, layer, scale, size):
    rows = arrived(refs[:ins], size)
    hidden, message, slope = refs[ins : ins + 3]
    state = (near[...] + scale * t_mm(forth_t[...], rows)).astype(BF)
    hidden[...] = state
    value, gradient = silu_pair(mm(state, weight[layer]))
    value = value.astype(BF)
    message[...] = value
    slope[...] = gradient
    emit(refs[ins + 3 :], t_mm(send[...], value), size, (outer_extra[...], inner_extra[...]))


def turn(near, forth_t, weight, send, receive, back_t, back_near, *refs, ins, scale, size):
    rows = arrived(refs[:ins], size)
    message, grad = refs[ins : ins + 2]
    state = (near[...] + scale * t_mm(forth_t[...], rows)).astype(BF)
    value, gradient = silu_pair(mm(state, weight[...]))
    value = value.astype(BF)
    message[...] = value
    returned = jnp.concatenate([refs[0][size : 2 * size], refs[1][size : 2 * size]], axis=0)
    back = back_near[...] + mm(receive[:, : 2 * size], returned)
    change = mm_t((back * gradient).astype(BF), weight[...]).astype(BF)
    grad[...] = change
    rim = t_mm(send[:, : 2 * size], value).astype(BF)
    emit(refs[ins + 2 :], mm(back_t[...], change), size, (rim[:size], rim[size:]))


def layer_back(near, receive, rows, slope, weight, grad, scale):
    total = near[...] + mm(receive[...], rows)
    change = (total * scale * slope[...]).astype(BF)
    return (grad[...].astype(F32) + mm_t(change, weight)).astype(BF)


def middle_back(near, receive, slope, weight, grad, back_t, *refs, ins, layer, scale, size):
    rows = arrived(refs[:ins], size)
    change = layer_back(near, receive, rows, slope, weight[layer], grad, scale)
    refs[ins][...] = change
    emit(refs[ins + 1 :], mm(back_t[...], change), size)


def last_back(near, receive, slope, weight, grad, grid_rim_t, *refs, ins, scale):
    new_grad, outer, inner = refs[ins:]
    rows = arrived(refs[:ins], refs[0].shape[0])
    change = layer_back(near, receive, rows, slope, weight[0], grad, scale)
    new_grad[...] = change
    back = mm(grid_rim_t[...], change).astype(BF)
    outer[...] = back[: outer.shape[0]]
    inner[...] = back[outer.shape[0] :]


def decode(latent, own_t, rim_t, message, outer_in, inner_in, output):
    size = outer_in.shape[0] // 2
    incoming = jnp.concatenate([outer_in[size:], inner_in[size : 2 * size]], axis=0)
    total = t_mm(own_t[...], message[...]) + t_mm(rim_t[...], incoming)
    output[...] = (latent[...].astype(F32) + total).astype(BF)


def grid_local(me, own_t, grad, lists, slope, weight, cotangent, base, table, slope_rows, mesh_grad):
    mesh_grad[...] = grad[...]
    rows = own_t.shape[0]
    size = lists.shape[2]
    for k, wanted in enumerate(pair_order(lists, me[0])):
        table[:, k * size : (k + 1) * size] = pick(rows, wanted)
    slope_rows[...] = t_mm(table[...], slope[...])
    change = (mm(own_t[...], grad[...]) * slope[...].astype(F32)).astype(BF)
    base[...] = cotangent[...].astype(F32) + mm_t(change, weight[...])


def grid_back(base, table, slope_rows, weight, outer_in, inner_in, output, staging, sems):
    returned = jnp.concatenate([outer_in[...], inner_in[...]], axis=0).astype(F32)
    change = mm_t((returned * slope_rows[...]).astype(BF), weight[...]).astype(BF)
    copies = []
    for i, part in enumerate(row_chunks(base.shape[0])):
        staging[part] = (base[part] + mm(table[part], change)).astype(BF)
        copies.append(pltpu.make_async_copy(staging.at[part], output.at[part], sems.at[i]))
        copies[-1].start()
    for copy in copies:
        copy.wait()


def toggle(value, bits):
    peers = lax.axis_size("dom")
    return lax.ppermute(value, "dom", [(i, i ^ bits) for i in range(peers)])


def across(value):
    peers = lax.axis_size("dom")
    pairs = [(i, (i + 1) % peers if i % 2 else (i - 1) % peers) for i in range(peers)]
    return lax.ppermute(value, "dom", pairs)


def exchange(outs, cap, after=()):
    width = outs[0].shape[1]
    if len(outs) == 3:
        outer, inner, far = outs
        peers = lax.axis_size("dom")
        blocks = far.reshape(peers, cap, width)
        blocks = lax.all_to_all(blocks, "dom", split_axis=0, concat_axis=0, tiled=True)
        return [across(outer), toggle(inner, 1), blocks.reshape(-1, width)]
    outer, inner, own, *rest = outs
    columns = STAGED // PLANE
    moved = [toggle(rest[m - 1], m * PLANE) for m in reversed(range(1, columns))]
    outer_in = across(outer)
    block = columns * cap
    blocks = call(
        shuffle,
        [((block, width), BF), ((inner.shape[0] + block, width), BF), ((block, width), BF), ((block, width), BF)],
        2 * (STAGED * cap) ** 2 * width,
        inner, own, *moved, outer_in, *after,
        free=len(after) + 1,
    )
    return [outer_in, toggle(blocks[1], 1), toggle(blocks[3], 3), toggle(blocks[2], 2), blocks[0]]


def on_device(
    grid_latent,
    mesh_latent,
    encoder_weight,
    processor_weights,
    decoder_weight,
    cotangent,
    grid_halo_rows,
    encoder_neighbours,
    halo_rows,
    far_sources,
    mesh_neighbours,
    decoder_neighbours,
):
    devices = lax.axis_size("dom")
    grid_rows, width = grid_latent.shape
    mesh_rows = mesh_latent.shape[0]
    ghalo = grid_halo_rows.shape[2]
    halo = halo_rows.shape[2]
    cap = far_sources.shape[2]
    slots = devices * cap
    listed = 2 * halo + slots
    scale = 1.0 / mesh_neighbours.shape[1]
    me = lax.axis_index("dom").astype(jnp.int32).reshape(1)

    def square(rows, depth):
        return 2 * rows * depth * width

    def sends(per_side):
        stages = STAGED // PLANE if devices == STAGED else 1
        return [((per_side, width), BF)] * 2 + [((slots // stages, width), BF)] * stages

    state = ((mesh_rows, width), BF)
    total = ((mesh_rows, width), F32)
    rim = ((halo, width), BF)
    grid_rim = ((ghalo, width), BF)
    step = 3 * square(mesh_rows, width)

    outer, inner = call(
        grid_send,
        [grid_rim, grid_rim],
        64 * square(grid_rows, width),
        me, grid_latent, grid_halo_rows,
        scalars=1, hbm=2, limit=60 * 1024 * 1024,
        scratch=copies_of([grid_latent, grid_halo_rows]) + [pltpu.SemaphoreType.DMA((CHUNKS + 1,))],
    )
    outer_in, inner_in = across(outer), toggle(inner, 1)

    near, grid_own_t, grid_rim_t, grid_slope, send, receive = call(
        functools.partial(encoder_local, size=ghalo),
        [
            total,
            ((grid_rows, mesh_rows), BF),
            ((2 * ghalo, mesh_rows), BF),
            ((grid_rows, width), BF),
            ((mesh_rows, listed), BF),
            ((mesh_rows, listed), BF),
        ],
        4 * square(grid_rows, width),
        me, encoder_neighbours.T, halo_rows, far_sources[0].T, encoder_weight, grid_latent, mesh_latent,
        scalars=1,
    )

    own_t, forth_t, back_t = call(
        functools.partial(mesh_tables, size=halo, devices=devices),
        [((mesh_rows, mesh_rows), BF)] + [((listed, mesh_rows), BF)] * 2,
        square(mesh_rows, mesh_rows),
        me, mesh_neighbours.T,
        scalars=1,
    )

    hidden, message, slope_0, *outs = call(
        functools.partial(first_hidden, size=halo),
        [state, state, total] + sends(halo),
        step,
        near, grid_rim_t, outer_in, inner_in, encoder_weight, processor_weights, send, back_t,
        free=1,
    )
    local = functools.partial(layer_local, scale=scale)
    (near,) = call(local, [total], square(mesh_rows, mesh_rows), hidden, own_t, message)
    ins = exchange(outs, cap, [near])
    decoder_own_t, decoder_rim_t, decoder_near, outer_extra, inner_extra = call(
        decoder_back,
        [((mesh_rows, grid_rows), BF), ((2 * halo, grid_rows), BF), total, rim, rim],
        square(grid_rows, mesh_rows),
        me, decoder_neighbours.T, cotangent, ins[-1],
        scalars=1, free=1,
    )

    hidden, message, slope_1, *outs = call(
        functools.partial(next_hidden, ins=len(ins), layer=1, scale=scale, size=halo),
        [state, state, total] + sends(2 * halo),
        step,
        near, forth_t, processor_weights, send, outer_extra, inner_extra, *ins,
    )
    (near,) = call(local, [total], square(mesh_rows, mesh_rows), hidden, own_t, message)
    ins = exchange(outs, cap, [near])

    message, grad, *outs = call(
        functools.partial(turn, ins=len(ins), scale=scale, size=halo),
        [state, state] + sends(2 * halo),
        2 * step,
        near, forth_t, decoder_weight, send, receive, back_t, decoder_near, *ins,
    )
    (near,) = call(back_local, [total], square(mesh_rows, mesh_rows), own_t, grad)
    ins = exchange(outs, cap, [near])
    outer_decoder, inner_decoder = ins[:2]

    grad, *outs = call(
        functools.partial(middle_back, ins=len(ins), layer=1, scale=scale, size=halo),
        [state] + sends(halo),
        step,
        near, receive, slope_1, processor_weights, grad, back_t, *ins,
    )
    (near,) = call(back_local, [total], square(mesh_rows, mesh_rows), own_t, grad)
    ins = exchange(outs, cap, [near])
    grad, outer, inner = call(
        functools.partial(last_back, ins=len(ins), scale=scale),
        [state, grid_rim, grid_rim],
        step,
        near, receive, slope_0, processor_weights, grad, grid_rim_t, *ins,
    )
    outer_in, inner_in = across(outer), toggle(inner, 1)
    (output,) = call(
        decode,
        [((grid_rows, width), BF)],
        square(grid_rows, mesh_rows),
        grid_latent, decoder_own_t, decoder_rim_t, message, outer_decoder, inner_decoder, grad,
        free=1,
    )
    base, table, slope_rows, mesh_grad = call(
        grid_local,
        [((grid_rows, width), F32), ((grid_rows, 2 * ghalo), BF), ((2 * ghalo, width), F32), state],
        square(mesh_rows, grid_rows) + square(grid_rows, width),
        me, grid_own_t, grad, grid_halo_rows, grid_slope, encoder_weight, cotangent,
        scalars=1,
    )
    (grid_grad,) = call(
        grid_back,
        [((grid_rows, width), BF)],
        square(grid_rows, 4 * ghalo),
        base, table, slope_rows, encoder_weight, outer_in, inner_in,
        hbm_out=1,
        scratch=[pltpu.VMEM((grid_rows, width), BF), pltpu.SemaphoreType.DMA((CHUNKS,))],
    )
    return (output, grid_grad, mesh_grad)


def solution(mesh):
    in_specs = (
        P(("groups", "dom"), None),
        P(("groups", "dom"), None),
        P(),
        P(),
        P(),
        P(("groups", "dom"), None),
        P("dom", None, None),
        P("dom", None),
        P("dom", None, None),
        P("dom", None, None),
        P("dom", None),
        P("dom", None),
    )
    out_specs = (P(("groups", "dom"), None), P(("groups", "dom"), None), P(("groups", "dom"), None))
    return jax.shard_map(
        on_device, mesh=mesh, in_specs=in_specs, out_specs=out_specs, check_vma=False
    )
```

```python
import functools

import jax
import jax.numpy as jnp
from jax import lax
from jax.experimental import pallas as pl
from jax.experimental.pallas import tpu as pltpu
from jax.sharding import PartitionSpec as P

BF = jnp.bfloat16
F32 = jnp.float32
VMEM_LIMIT = 24 * 1024 * 1024
PLANE = 4
STAGED = 16
CHUNKS = 4


def mm(a, b):
    return jnp.dot(a, b, preferred_element_type=F32)


def mm_t(a, b):
    return lax.dot_general(a, b, (((1,), (1,)), ((), ())), preferred_element_type=F32)


def t_mm(a, b):
    return lax.dot_general(a, b, (((0,), (0,)), ((), ())), preferred_element_type=F32)


def silu_pair(value):
    sigma = 0.5 + 0.5 * jnp.tanh(0.5 * value)
    message = value * sigma
    return message, sigma + message * (1.0 - sigma)


def pick(rows, wanted):
    places = lax.broadcasted_iota(jnp.int32, (rows, wanted.shape[1]), 0)
    return (places == wanted).astype(F32).astype(BF)


def counts_t(columns, first, entries):
    degree, rows = entries.shape
    places = lax.broadcasted_iota(jnp.int32, (columns, rows), 0) + first
    total = jnp.zeros((columns, rows), F32)
    for k in range(degree):
        total = total + (places == entries[k : k + 1]).astype(F32)
    return total.astype(BF)


def side_swap(entries, rows, size, me):
    swapped = jnp.where(entries < rows + size, entries + size, entries - size)
    rim = (entries >= rows) & (entries < rows + 2 * size)
    return jnp.where(rim & (me % 2 == 1), swapped, entries)


def pair_order(lists, me):
    left, right = lists[0, 0:1], lists[0, 1:2]
    odd = me % 2
    return left + odd * (right - left), right + odd * (left - right)


def by_stage(x, devices):
    return (x % PLANE) * (devices // PLANE) + x // PLANE


def call(body, out_shapes, flops, *args, scalars=0, hbm=0, free=0, hbm_out=0, scratch=(), limit=VMEM_LIMIT):
    shapes = [jax.ShapeDtypeStruct(s, t) for s, t in out_shapes]
    size = sum(a.size * a.dtype.itemsize for a in args)
    size += sum(s.size * s.dtype.itemsize for s in shapes)
    size *= hbm == 0
    places = [pltpu.SMEM] * scalars + [pltpu.HBM] * hbm + [pltpu.VMEM] * (len(args) - scalars - hbm - free)
    places += [pl.ANY] * free
    out_places = [pltpu.HBM] * hbm_out + [pltpu.VMEM] * (len(shapes) - hbm_out)
    kept = len(args) - free
    inner = body if free == 0 else lambda *refs: body(*refs[:kept], *refs[len(args) :])
    return pl.pallas_call(
        inner,
        out_shape=shapes,
        in_specs=[pl.BlockSpec(memory_space=place) for place in places],
        out_specs=[pl.BlockSpec(memory_space=place) for place in out_places],
        scratch_shapes=list(scratch),
        compiler_params=pltpu.CompilerParams(vmem_limit_bytes=limit),
        cost_estimate=pl.CostEstimate(flops=flops, bytes_accessed=size, transcendentals=0),
    )(*args)


def copies_of(arrays):
    return [pltpu.VMEM(a.shape, a.dtype) for a in arrays]


def fetch(sources, targets, sems):
    copies = [pltpu.make_async_copy(s, t, sems.at[i]) for i, (s, t) in enumerate(zip(sources, targets))]
    for copy in copies:
        copy.start()
    return copies


def row_chunks(rows):
    step = rows // CHUNKS
    return [pl.ds(i * step, step) for i in range(CHUNKS)]


def grid_send(me, latent, lists, outer, inner, values, wanted, sems):
    parts = row_chunks(latent.shape[0])
    sources = [lists] + [latent.at[part] for part in parts]
    copies = fetch(sources, [wanted] + [values.at[part] for part in parts], sems)
    copies[0].wait()
    wanted_outer, wanted_inner = pair_order(wanted, me[0])
    step = latent.shape[0] // CHUNKS
    outer_rows = inner_rows = 0.0
    for i, part in enumerate(parts):
        copies[i + 1].wait()
        chunk = values[part]
        outer_rows += t_mm(pick(step, wanted_outer - i * step), chunk)
        inner_rows += t_mm(pick(step, wanted_inner - i * step), chunk)
    outer[...] = outer_rows.astype(BF)
    inner[...] = inner_rows.astype(BF)


def encoder_local(me, entries, weight, latent, mesh, near, grid_own_t, grid_rim_t, slope, *, size):
    rows = latent.shape[0]
    columns = side_swap(entries[...], rows, size, me[0])
    own = counts_t(rows, 0, columns)
    grid_own_t[...] = own
    grid_rim_t[...] = counts_t(2 * size, rows, columns)
    message, gradient = silu_pair(mm(latent[...], weight[...]))
    slope[...] = gradient.astype(BF)
    near[...] = mesh[...].astype(F32) + t_mm(own, message.astype(BF))


def list_tables(me, lists, far_lists, send, receive):
    rows = send.shape[0]
    size = lists.shape[2]
    cap, devices = far_lists.shape
    outer, inner = pair_order(lists, me[0])
    rim = [pick(rows, outer), pick(rows, inner)]
    for k in range(2):
        send[:, k * size : (k + 1) * size] = rim[k]
        receive[:, k * size : (k + 1) * size] = rim[k]
    partner = lax.broadcasted_iota(jnp.int32, (devices, devices * cap), 0)
    place = lax.broadcasted_iota(jnp.int32, (devices, devices * cap), 1)
    if devices == STAGED:
        x = partner ^ me[0]
        send_place, receive_place = x * cap, by_stage(x, devices) * cap
    else:
        send_place, receive_place = partner * cap, partner * cap
    send_far = jnp.zeros((rows, devices * cap), F32)
    receive_far = jnp.zeros((rows, devices * cap), F32)
    for j in range(cap):
        chosen = pick(rows, far_lists[j : j + 1])
        send_far += mm(chosen, (place == send_place + j).astype(F32).astype(BF))
        receive_far += mm(chosen, (place == receive_place + j).astype(F32).astype(BF))
    send[:, 2 * size :] = send_far.astype(BF)
    receive[:, 2 * size :] = receive_far.astype(BF)


def mesh_tables(me, entries, own_t, forth_t, back_t, size, devices):
    rows = own_t.shape[0]
    slots = forth_t.shape[0] - 2 * size
    cap = slots // devices
    columns = side_swap(entries[...], rows, size, me[0])
    own_t[...] = counts_t(rows, 0, columns)
    rim = counts_t(2 * size, rows, columns)
    forth_t[: 2 * size] = rim
    back_t[: 2 * size] = rim
    far = jnp.maximum(columns - rows - 2 * size, 0)
    partner, slot = far // cap, far % cap
    if devices == STAGED:
        partner = partner ^ me[0]
        send_place, receive_place = partner * cap + slot, by_stage(partner, devices) * cap + slot
    else:
        send_place, receive_place = far, far
    is_far = columns >= rows + 2 * size
    forth_t[2 * size :] = counts_t(slots, 0, jnp.where(is_far, receive_place, -1))
    back_t[2 * size :] = counts_t(slots, 0, jnp.where(is_far, send_place, -1))


def decoder_back(me, entries, cotangent, own_t, rim_t, near, outer, inner):
    rows = near.shape[0]
    size = outer.shape[0]
    columns = side_swap(entries[...], rows, size, me[0])
    own = counts_t(rows, 0, columns)
    side = counts_t(2 * size, rows, columns)
    own_t[...] = own
    rim_t[...] = side
    grads = cotangent[...]
    near[...] = mm(own, grads)
    back = mm(side, grads).astype(BF)
    outer[...] = back[:size]
    inner[...] = back[size:]


def emit(outs, rows, size, extra=None):
    rows = rows.astype(BF)
    for k in range(2):
        outs[k][:size] = rows[k * size : (k + 1) * size]
        if extra is not None:
            outs[k][size:] = extra[k]
    far = rows[2 * size :]
    block = far.shape[0] // (len(outs) - 2)
    for m, out in enumerate(outs[2:]):
        out[...] = far[m * block : (m + 1) * block]


def arrived(ins, size):
    outer, inner = ins[:2]
    parts = [outer[:size], inner[:size]]
    if len(ins) > 3:
        third, second, own = ins[2:]
        parts += [own[...], inner[inner.shape[0] - own.shape[0] :], second[...], third[...]]
    else:
        parts += [ref[...] for ref in ins[2:]]
    return jnp.concatenate(parts, axis=0)


def shuffle(inner, own, *refs):
    columns = STAGED // PLANE
    parts = [own[...]] + [ref[...] for ref in refs[: columns - 1][::-1]]
    rows = jnp.concatenate(parts, axis=0)
    outs = refs[columns - 1 :]
    count = rows.shape[0]
    cap = count // STAGED
    target = lax.broadcasted_iota(jnp.int32, (count, count), 0)
    source = lax.broadcasted_iota(jnp.int32, (count, count), 1)
    place, slot = target // cap, target % cap
    wanted = ((place % columns) * PLANE + place // columns) * cap + slot
    moved = mm((source == wanted).astype(F32).astype(BF), rows).astype(BF)
    block = columns * cap
    used = inner.shape[0]
    outs[1][:used] = inner[...]
    outs[1][used:] = moved[block : 2 * block]
    for k in (0, 2, 3):
        outs[k][...] = moved[k * block : (k + 1) * block]


def tables(me, entries, lists, far_lists, own_t, forth_t, back_t, send, receive, *, size, devices):
    mesh_tables(me, entries, own_t, forth_t, back_t, size, devices)
    list_tables(me, lists, far_lists, send, receive)


def layer_local(hidden, own_t, message, near, *, scale):
    near[...] = hidden[...].astype(F32) + scale * t_mm(own_t[...], message[...])


def back_local(own_t, grad, near):
    near[...] = mm(own_t[...], grad[...])


def first_hidden(near, rim_t, outer_in, inner_in, encoder, weight, send, hidden, message, slope, *outs, size):
    incoming = silu_pair(mm(arrived([outer_in, inner_in], outer_in.shape[0]), encoder[...]))[0].astype(BF)
    state = (near[...] + t_mm(rim_t[...], incoming)).astype(BF)
    hidden[...] = state
    value, gradient = silu_pair(mm(state, weight[0]))
    value = value.astype(BF)
    message[...] = value
    slope[...] = gradient
    emit(outs, t_mm(send[...], value), size)


def next_hidden(near, forth_t, weight, send, outer_extra, inner_extra, *refs, ins, layer, scale, size):
    rows = arrived(refs[:ins], size)
    hidden, message, slope = refs[ins : ins + 3]
    state = (near[...] + scale * t_mm(forth_t[...], rows)).astype(BF)
    hidden[...] = state
    value, gradient = silu_pair(mm(state, weight[layer]))
    value = value.astype(BF)
    message[...] = value
    slope[...] = gradient
    emit(refs[ins + 3 :], t_mm(send[...], value), size, (outer_extra[...], inner_extra[...]))


def turn(near, forth_t, weight, send, receive, back_t, back_near, *refs, ins, scale, size):
    rows = arrived(refs[:ins], size)
    message, grad = refs[ins : ins + 2]
    state = (near[...] + scale * t_mm(forth_t[...], rows)).astype(BF)
    value, gradient = silu_pair(mm(state, weight[...]))
    value = value.astype(BF)
    message[...] = value
    returned = jnp.concatenate([refs[0][size : 2 * size], refs[1][size : 2 * size]], axis=0)
    back = back_near[...] + mm(receive[:, : 2 * size], returned)
    change = mm_t((back * gradient).astype(BF), weight[...]).astype(BF)
    grad[...] = change
    rim = t_mm(send[:, : 2 * size], value).astype(BF)
    emit(refs[ins + 2 :], mm(back_t[...], change), size, (rim[:size], rim[size:]))


def layer_back(near, receive, rows, slope, weight, grad, scale):
    total = near[...] + mm(receive[...], rows)
    change = (total * scale * slope[...]).astype(BF)
    return (grad[...].astype(F32) + mm_t(change, weight)).astype(BF)


def middle_back(near, receive, slope, weight, grad, back_t, *refs, ins, layer, scale, size):
    rows = arrived(refs[:ins], size)
    change = layer_back(near, receive, rows, slope, weight[layer], grad, scale)
    refs[ins][...] = change
    emit(refs[ins + 1 :], mm(back_t[...], change), size)


def last_back(near, receive, slope, weight, grad, grid_rim_t, *refs, ins, scale):
    new_grad, outer, inner = refs[ins:]
    rows = arrived(refs[:ins], refs[0].shape[0])
    change = layer_back(near, receive, rows, slope, weight[0], grad, scale)
    new_grad[...] = change
    back = mm(grid_rim_t[...], change).astype(BF)
    outer[...] = back[: outer.shape[0]]
    inner[...] = back[outer.shape[0] :]


def decode(latent, own_t, rim_t, message, outer_in, inner_in, output):
    size = outer_in.shape[0] // 2
    incoming = jnp.concatenate([outer_in[size:], inner_in[size : 2 * size]], axis=0)
    total = t_mm(own_t[...], message[...]) + t_mm(rim_t[...], incoming)
    output[...] = (latent[...].astype(F32) + total).astype(BF)


def grid_local(me, own_t, grad, lists, slope, weight, cotangent, base, table, slope_rows, mesh_grad):
    mesh_grad[...] = grad[...]
    rows = own_t.shape[0]
    size = lists.shape[2]
    for k, wanted in enumerate(pair_order(lists, me[0])):
        table[:, k * size : (k + 1) * size] = pick(rows, wanted)
    slope_rows[...] = t_mm(table[...], slope[...])
    change = (mm(own_t[...], grad[...]) * slope[...].astype(F32)).astype(BF)
    base[...] = cotangent[...].astype(F32) + mm_t(change, weight[...])


def grid_back(base, table, slope_rows, weight, outer_in, inner_in, output, staging, sems):
    returned = jnp.concatenate([outer_in[...], inner_in[...]], axis=0).astype(F32)
    change = mm_t((returned * slope_rows[...]).astype(BF), weight[...]).astype(BF)
    copies = []
    for i, part in enumerate(row_chunks(base.shape[0])):
        staging[part] = (base[part] + mm(table[part], change)).astype(BF)
        copies.append(pltpu.make_async_copy(staging.at[part], output.at[part], sems.at[i]))
        copies[-1].start()
    for copy in copies:
        copy.wait()


def toggle(value, bits):
    peers = lax.axis_size("dom")
    return lax.ppermute(value, "dom", [(i, i ^ bits) for i in range(peers)])


def across(value):
    peers = lax.axis_size("dom")
    pairs = [(i, (i + 1) % peers if i % 2 else (i - 1) % peers) for i in range(peers)]
    return lax.ppermute(value, "dom", pairs)


def exchange(outs, cap):
    width = outs[0].shape[1]
    if len(outs) == 3:
        outer, inner, far = outs
        peers = lax.axis_size("dom")
        blocks = far.reshape(peers, cap, width)
        blocks = lax.all_to_all(blocks, "dom", split_axis=0, concat_axis=0, tiled=True)
        return [across(outer), toggle(inner, 1), blocks.reshape(-1, width)]
    outer, inner, own, *rest = outs
    columns = STAGED // PLANE
    moved = [toggle(rest[m - 1], m * PLANE) for m in reversed(range(1, columns))]
    outer_in = across(outer)
    block = columns * cap
    blocks = call(
        shuffle,
        [((block, width), BF), ((inner.shape[0] + block, width), BF), ((block, width), BF), ((block, width), BF)],
        2 * (STAGED * cap) ** 2 * width,
        inner, own, *moved,
    )
    return [outer_in, toggle(blocks[1], 1), toggle(blocks[3], 3), toggle(blocks[2], 2), blocks[0]]


def on_device(
    grid_latent,
    mesh_latent,
    encoder_weight,
    processor_weights,
    decoder_weight,
    cotangent,
    grid_halo_rows,
    encoder_neighbours,
    halo_rows,
    far_sources,
    mesh_neighbours,
    decoder_neighbours,
):
    devices = lax.axis_size("dom")
    grid_rows, width = grid_latent.shape
    mesh_rows = mesh_latent.shape[0]
    ghalo = grid_halo_rows.shape[2]
    halo = halo_rows.shape[2]
    cap = far_sources.shape[2]
    slots = devices * cap
    listed = 2 * halo + slots
    scale = 1.0 / mesh_neighbours.shape[1]
    me = lax.axis_index("dom").astype(jnp.int32).reshape(1)

    def square(rows, depth):
        return 2 * rows * depth * width

    def sends(per_side):
        stages = STAGED // PLANE if devices == STAGED else 1
        return [((per_side, width), BF)] * 2 + [((slots // stages, width), BF)] * stages

    state = ((mesh_rows, width), BF)
    total = ((mesh_rows, width), F32)
    rim = ((halo, width), BF)
    grid_rim = ((ghalo, width), BF)
    step = 3 * square(mesh_rows, width)

    outer, inner = call(
        grid_send,
        [grid_rim, grid_rim],
        64 * square(grid_rows, width),
        me, grid_latent, grid_halo_rows,
        scalars=1, hbm=2, limit=60 * 1024 * 1024,
        scratch=copies_of([grid_latent, grid_halo_rows]) + [pltpu.SemaphoreType.DMA((CHUNKS + 1,))],
    )
    outer_in, inner_in = across(outer), toggle(inner, 1)

    own_t, forth_t, back_t, send, receive = call(
        functools.partial(tables, size=halo, devices=devices),
        [((mesh_rows, mesh_rows), BF)] + [((listed, mesh_rows), BF)] * 2 + [((mesh_rows, listed), BF)] * 2,
        64 * square(mesh_rows, mesh_rows),
        me, mesh_neighbours.T, halo_rows, far_sources[0].T,
        scalars=1,
    )
    _, latent, weight, mesh = lax.optimization_barrier((inner, grid_latent, encoder_weight, mesh_latent))
    near, grid_own_t, grid_rim_t, grid_slope = call(
        functools.partial(encoder_local, size=ghalo),
        [total, ((grid_rows, mesh_rows), BF), ((2 * ghalo, mesh_rows), BF), ((grid_rows, width), BF)],
        4 * square(grid_rows, width),
        me, encoder_neighbours.T, weight, latent, mesh,
        scalars=1,
    )

    hidden, message, slope_0, *outs = call(
        functools.partial(first_hidden, size=halo),
        [state, state, total] + sends(halo),
        step,
        near, grid_rim_t, outer_in, inner_in, encoder_weight, processor_weights, send,
    )
    local = functools.partial(layer_local, scale=scale)
    ins = exchange(outs, cap)
    (near,) = call(local, [total], 6 * square(mesh_rows, mesh_rows), hidden, own_t, message, ins[-1], free=1)

    decoder_own_t, decoder_rim_t, decoder_near, outer_extra, inner_extra = call(
        decoder_back,
        [((mesh_rows, grid_rows), BF), ((2 * halo, grid_rows), BF), total, rim, rim],
        square(grid_rows, mesh_rows),
        me, decoder_neighbours.T, cotangent, ins[-1],
        scalars=1, free=1,
    )

    hidden, message, slope_1, *outs = call(
        functools.partial(next_hidden, ins=len(ins), layer=1, scale=scale, size=halo),
        [state, state, total] + sends(2 * halo),
        step,
        near, forth_t, processor_weights, send, outer_extra, inner_extra, *ins,
    )
    ins = exchange(outs, cap)
    (near,) = call(local, [total], 6 * square(mesh_rows, mesh_rows), hidden, own_t, message)


    message, grad, *outs = call(
        functools.partial(turn, ins=len(ins), scale=scale, size=halo),
        [state, state] + sends(2 * halo),
        2 * step,
        near, forth_t, decoder_weight, send, receive, back_t, decoder_near, *ins,
    )
    ins = exchange(outs, cap)
    (near,) = call(back_local, [total], 6 * square(mesh_rows, mesh_rows), own_t, grad)

    outer_decoder, inner_decoder = ins[:2]

    grad, *outs = call(
        functools.partial(middle_back, ins=len(ins), layer=1, scale=scale, size=halo),
        [state] + sends(halo),
        step,
        near, receive, slope_1, processor_weights, grad, back_t, *ins,
    )
    ins = exchange(outs, cap)
    (near,) = call(back_local, [total], 6 * square(mesh_rows, mesh_rows), own_t, grad)

    grad, outer, inner = call(
        functools.partial(last_back, ins=len(ins), scale=scale),
        [state, grid_rim, grid_rim],
        step,
        near, receive, slope_0, processor_weights, grad, grid_rim_t, *ins,
    )
    outer_in, inner_in = across(outer), toggle(inner, 1)
    (output,) = call(
        decode,
        [((grid_rows, width), BF)],
        square(grid_rows, mesh_rows),
        grid_latent, decoder_own_t, decoder_rim_t, message, outer_decoder, inner_decoder, grad,
        free=1,
    )
    base, table, slope_rows, mesh_grad = call(
        grid_local,
        [((grid_rows, width), F32), ((grid_rows, 2 * ghalo), BF), ((2 * ghalo, width), F32), state],
        square(mesh_rows, grid_rows) + square(grid_rows, width),
        me, grid_own_t, grad, grid_halo_rows, grid_slope, encoder_weight, cotangent,
        scalars=1,
    )
    (grid_grad,) = call(
        grid_back,
        [((grid_rows, width), BF)],
        square(grid_rows, 4 * ghalo),
        base, table, slope_rows, encoder_weight, outer_in, inner_in,
        hbm_out=1,
        scratch=[pltpu.VMEM((grid_rows, width), BF), pltpu.SemaphoreType.DMA((CHUNKS,))],
    )
    return (output, grid_grad, mesh_grad)


def solution(mesh):
    in_specs = (
        P(("groups", "dom"), None),
        P(("groups", "dom"), None),
        P(),
        P(),
        P(),
        P(("groups", "dom"), None),
        P("dom", None, None),
        P("dom", None),
        P("dom", None, None),
        P("dom", None, None),
        P("dom", None),
        P("dom", None),
    )
    out_specs = (P(("groups", "dom"), None), P(("groups", "dom"), None), P(("groups", "dom"), None))
    return jax.shard_map(
        on_device, mesh=mesh, in_specs=in_specs, out_specs=out_specs, check_vma=False
    )
```

```python
import functools

import jax
import jax.numpy as jnp
from jax import lax
from jax.experimental import pallas as pl
from jax.experimental.pallas import tpu as pltpu
from jax.sharding import PartitionSpec as P

BF = jnp.bfloat16
F32 = jnp.float32
VMEM_LIMIT = 24 * 1024 * 1024
PLANE = 4
STAGED = 16
CHUNKS = 4


def mm(a, b):
    return jnp.dot(a, b, preferred_element_type=F32)


def mm_t(a, b):
    return lax.dot_general(a, b, (((1,), (1,)), ((), ())), preferred_element_type=F32)


def t_mm(a, b):
    return lax.dot_general(a, b, (((0,), (0,)), ((), ())), preferred_element_type=F32)


def silu_pair(value):
    sigma = 0.5 + 0.5 * jnp.tanh(0.5 * value)
    message = value * sigma
    return message, sigma + message * (1.0 - sigma)


def match(places, wanted):
    shape = places.shape
    wanted = jnp.broadcast_to(wanted, shape).astype(jnp.int16)
    return jnp.where(places == wanted, jnp.ones(shape, BF), jnp.zeros(shape, BF))


def pick(rows, wanted):
    places = lax.broadcasted_iota(jnp.int32, (rows, wanted.shape[1]), 0).astype(jnp.int16)
    return match(places, wanted)


def counts_t(columns, first, entries):
    degree, rows = entries.shape
    places = (lax.broadcasted_iota(jnp.int32, (columns, rows), 0) + first).astype(jnp.int16)
    total = match(places, entries[0:1])
    for k in range(1, degree):
        total = total + match(places, entries[k : k + 1])
    return total


def side_swap(entries, rows, size, me):
    swapped = jnp.where(entries < rows + size, entries + size, entries - size)
    rim = (entries >= rows) & (entries < rows + 2 * size)
    return jnp.where(rim & (me % 2 == 1), swapped, entries)


def pair_order(lists, me):
    left, right = lists[0, 0:1], lists[0, 1:2]
    odd = me % 2
    return left + odd * (right - left), right + odd * (left - right)


def by_stage(x, devices):
    return (x % PLANE) * (devices // PLANE) + x // PLANE


def call(body, out_shapes, flops, *args, scalars=0, hbm=0, free=0, hbm_out=0, scratch=(), limit=VMEM_LIMIT):
    shapes = [jax.ShapeDtypeStruct(s, t) for s, t in out_shapes]
    size = sum(a.size * a.dtype.itemsize for a in args)
    size += sum(s.size * s.dtype.itemsize for s in shapes)
    size *= hbm == 0
    places = [pltpu.SMEM] * scalars + [pltpu.HBM] * hbm + [pltpu.VMEM] * (len(args) - scalars - hbm - free)
    places += [pl.ANY] * free
    out_places = [pltpu.HBM] * hbm_out + [pltpu.VMEM] * (len(shapes) - hbm_out)
    kept = len(args) - free
    inner = body if free == 0 else lambda *refs: body(*refs[:kept], *refs[len(args) :])
    return pl.pallas_call(
        inner,
        out_shape=shapes,
        in_specs=[pl.BlockSpec(memory_space=place) for place in places],
        out_specs=[pl.BlockSpec(memory_space=place) for place in out_places],
        scratch_shapes=list(scratch),
        compiler_params=pltpu.CompilerParams(vmem_limit_bytes=limit),
        cost_estimate=pl.CostEstimate(flops=flops, bytes_accessed=size, transcendentals=0),
    )(*args)


def copies_of(arrays):
    return [pltpu.VMEM(a.shape, a.dtype) for a in arrays]


def fetch(sources, targets, sems):
    copies = [pltpu.make_async_copy(s, t, sems.at[i]) for i, (s, t) in enumerate(zip(sources, targets))]
    for copy in copies:
        copy.start()
    return copies


def row_chunks(rows):
    step = rows // CHUNKS
    return [pl.ds(i * step, step) for i in range(CHUNKS)]


def grid_send(me, latent, lists, outer, inner, values, wanted, sems):
    parts = row_chunks(latent.shape[0])
    sources = [lists] + [latent.at[part] for part in parts]
    copies = fetch(sources, [wanted] + [values.at[part] for part in parts], sems)
    copies[0].wait()
    wanted_outer, wanted_inner = pair_order(wanted, me[0])
    step = latent.shape[0] // CHUNKS
    outer_rows = inner_rows = 0.0
    for i, part in enumerate(parts):
        copies[i + 1].wait()
        chunk = values[part]
        outer_rows += t_mm(pick(step, wanted_outer - i * step), chunk)
        inner_rows += t_mm(pick(step, wanted_inner - i * step), chunk)
    outer[...] = outer_rows.astype(BF)
    inner[...] = inner_rows.astype(BF)


def encoder_local(me, entries, weight, latent, mesh, near, grid_own_t, grid_rim_t, slope, *, size):
    rows = latent.shape[0]
    columns = side_swap(entries[...], rows, size, me[0])
    own = counts_t(rows, 0, columns)
    grid_own_t[...] = own
    grid_rim_t[...] = counts_t(2 * size, rows, columns)
    message, gradient = silu_pair(mm(latent[...], weight[...]))
    slope[...] = gradient.astype(BF)
    near[...] = mesh[...].astype(F32) + t_mm(own, message.astype(BF))


def list_tables(me, lists, far_lists, send, receive):
    rows = send.shape[0]
    size = lists.shape[2]
    cap, devices = far_lists.shape
    outer, inner = pair_order(lists, me[0])
    rim = [pick(rows, outer), pick(rows, inner)]
    for k in range(2):
        send[:, k * size : (k + 1) * size] = rim[k]
        receive[:, k * size : (k + 1) * size] = rim[k]
    partner = lax.broadcasted_iota(jnp.int32, (devices, devices * cap), 0)
    place = lax.broadcasted_iota(jnp.int32, (devices, devices * cap), 1)
    if devices == STAGED:
        x = partner ^ me[0]
        send_place, receive_place = x * cap, by_stage(x, devices) * cap
    else:
        send_place, receive_place = partner * cap, partner * cap
    send_far = jnp.zeros((rows, devices * cap), F32)
    receive_far = jnp.zeros((rows, devices * cap), F32)
    for j in range(cap):
        chosen = pick(rows, far_lists[j : j + 1])
        send_far += mm(chosen, (place == send_place + j).astype(F32).astype(BF))
        receive_far += mm(chosen, (place == receive_place + j).astype(F32).astype(BF))
    send[:, 2 * size :] = send_far.astype(BF)
    receive[:, 2 * size :] = receive_far.astype(BF)


def mesh_tables(me, entries, own_t, forth_t, back_t, size, devices):
    rows = own_t.shape[0]
    slots = forth_t.shape[0] - 2 * size
    cap = slots // devices
    columns = side_swap(entries[...], rows, size, me[0])
    own_t[...] = counts_t(rows, 0, columns)
    rim = counts_t(2 * size, rows, columns)
    forth_t[: 2 * size] = rim
    back_t[: 2 * size] = rim
    far = jnp.maximum(columns - rows - 2 * size, 0)
    partner, slot = far // cap, far % cap
    if devices == STAGED:
        partner = partner ^ me[0]
        send_place, receive_place = partner * cap + slot, by_stage(partner, devices) * cap + slot
    else:
        send_place, receive_place = far, far
    is_far = columns >= rows + 2 * size
    forth_t[2 * size :] = counts_t(slots, 0, jnp.where(is_far, receive_place, -1))
    back_t[2 * size :] = counts_t(slots, 0, jnp.where(is_far, send_place, -1))


def decoder_back(me, entries, cotangent, own_t, rim_t, near, outer, inner):
    rows = near.shape[0]
    size = outer.shape[0]
    columns = side_swap(entries[...], rows, size, me[0])
    own = counts_t(rows, 0, columns)
    side = counts_t(2 * size, rows, columns)
    own_t[...] = own
    rim_t[...] = side
    grads = cotangent[...]
    near[...] = mm(own, grads)
    back = mm(side, grads).astype(BF)
    outer[...] = back[:size]
    inner[...] = back[size:]


def emit(outs, rows, size, extra=None):
    rows = rows.astype(BF)
    for k in range(2):
        outs[k][:size] = rows[k * size : (k + 1) * size]
        if extra is not None:
            outs[k][size:] = extra[k]
    far = rows[2 * size :]
    block = far.shape[0] // (len(outs) - 2)
    for m, out in enumerate(outs[2:]):
        out[...] = far[m * block : (m + 1) * block]


def arrived(ins, size):
    outer, inner = ins[:2]
    parts = [outer[:size], inner[:size]]
    if len(ins) > 3:
        third, second, own = ins[2:]
        parts += [own[...], inner[inner.shape[0] - own.shape[0] :], second[...], third[...]]
    else:
        parts += [ref[...] for ref in ins[2:]]
    return jnp.concatenate(parts, axis=0)


def shuffle(inner, own, *refs):
    columns = STAGED // PLANE
    parts = [own[...]] + [ref[...] for ref in refs[: columns - 1][::-1]]
    rows = jnp.concatenate(parts, axis=0)
    outs = refs[columns - 1 :]
    count = rows.shape[0]
    cap = count // STAGED
    target = lax.broadcasted_iota(jnp.int32, (count, count), 0)
    source = lax.broadcasted_iota(jnp.int32, (count, count), 1)
    place, slot = target // cap, target % cap
    wanted = ((place % columns) * PLANE + place // columns) * cap + slot
    moved = mm((source == wanted).astype(F32).astype(BF), rows).astype(BF)
    block = columns * cap
    used = inner.shape[0]
    outs[1][:used] = inner[...]
    outs[1][used:] = moved[block : 2 * block]
    for k in (0, 2, 3):
        outs[k][...] = moved[k * block : (k + 1) * block]


def tables(me, entries, lists, far_lists, own_t, forth_t, back_t, send, receive, *, size, devices):
    mesh_tables(me, entries, own_t, forth_t, back_t, size, devices)
    list_tables(me, lists, far_lists, send, receive)


def layer_local(hidden, own_t, weight, near, slope, *, layer, scale):
    state = hidden[...]
    value, gradient = silu_pair(mm(state, weight[layer]))
    slope[...] = gradient
    near[...] = state.astype(F32) + scale * t_mm(own_t[...], value.astype(BF))


def back_local(own_t, grad, near):
    near[...] = mm(own_t[...], grad[...])


def chosen_messages(send, state, weight):
    return silu_pair(mm(t_mm(send[...], state).astype(BF), weight))[0]


def first_hidden(near, rim_t, outer_in, inner_in, encoder, weight, send, hidden, *outs, size):
    incoming = silu_pair(mm(arrived([outer_in, inner_in], outer_in.shape[0]), encoder[...]))[0].astype(BF)
    state = (near[...] + t_mm(rim_t[...], incoming)).astype(BF)
    hidden[...] = state
    emit(outs, chosen_messages(send, state, weight[0]), size)


def next_hidden(near, forth_t, weight, send, outer_extra, inner_extra, *refs, ins, layer, scale, size):
    rows = arrived(refs[:ins], size)
    state = (near[...] + scale * t_mm(forth_t[...], rows)).astype(BF)
    refs[ins][...] = state
    emit(refs[ins + 1 :], chosen_messages(send, state, weight[layer]), size, (outer_extra[...], inner_extra[...]))


def turn(near, forth_t, weight, send, receive, back_t, back_near, *refs, ins, scale, size):
    rows = arrived(refs[:ins], size)
    message, grad = refs[ins : ins + 2]
    state = (near[...] + scale * t_mm(forth_t[...], rows)).astype(BF)
    value, gradient = silu_pair(mm(state, weight[...]))
    value = value.astype(BF)
    message[...] = value
    returned = jnp.concatenate([refs[0][size : 2 * size], refs[1][size : 2 * size]], axis=0)
    back = back_near[...] + mm(receive[:, : 2 * size], returned)
    change = mm_t((back * gradient).astype(BF), weight[...]).astype(BF)
    grad[...] = change
    rim = t_mm(send[:, : 2 * size], value).astype(BF)
    emit(refs[ins + 2 :], mm(back_t[...], change), size, (rim[:size], rim[size:]))


def layer_back(near, receive, rows, slope, weight, grad, scale):
    total = near[...] + mm(receive[...], rows)
    change = (total * scale * slope[...]).astype(BF)
    return (grad[...].astype(F32) + mm_t(change, weight)).astype(BF)


def middle_back(near, receive, slope, weight, grad, back_t, *refs, ins, layer, scale, size):
    rows = arrived(refs[:ins], size)
    change = layer_back(near, receive, rows, slope, weight[layer], grad, scale)
    refs[ins][...] = change
    emit(refs[ins + 1 :], mm(back_t[...], change), size)


def last_back(near, receive, slope, weight, grad, grid_rim_t, *refs, ins, scale):
    new_grad, outer, inner = refs[ins:]
    rows = arrived(refs[:ins], refs[0].shape[0])
    change = layer_back(near, receive, rows, slope, weight[0], grad, scale)
    new_grad[...] = change
    back = mm(grid_rim_t[...], change).astype(BF)
    outer[...] = back[: outer.shape[0]]
    inner[...] = back[outer.shape[0] :]


def decode_own(latent, own_t, message, base):
    base[...] = latent[...].astype(F32) + t_mm(own_t[...], message[...])


def decode_rim(base, rim_t, outer_in, inner_in, output, token):
    size = outer_in.shape[0] // 2
    incoming = jnp.concatenate([outer_in[size:], inner_in[size : 2 * size]], axis=0)
    output[...] = (base[...] + t_mm(rim_t[...], incoming)).astype(BF)
    token[...] = jnp.zeros(token.shape, F32)


def grid_local(me, own_t, grad, lists, slope, weight, cotangent, base, table, slope_rows, mesh_grad):
    mesh_grad[...] = grad[...]
    rows = own_t.shape[0]
    size = lists.shape[2]
    for k, wanted in enumerate(pair_order(lists, me[0])):
        table[:, k * size : (k + 1) * size] = pick(rows, wanted)
    slope_rows[...] = t_mm(table[...], slope[...])
    change = (mm(own_t[...], grad[...]) * slope[...].astype(F32)).astype(BF)
    base[...] = cotangent[...].astype(F32) + mm_t(change, weight[...])


def grid_back(base, table, slope_rows, weight, outer_in, inner_in, output, staging, sems):
    returned = jnp.concatenate([outer_in[...], inner_in[...]], axis=0).astype(F32)
    change = mm_t((returned * slope_rows[...]).astype(BF), weight[...]).astype(BF)
    copies = []
    for i, part in enumerate(row_chunks(base.shape[0])):
        staging[part] = (base[part] + mm(table[part], change)).astype(BF)
        copies.append(pltpu.make_async_copy(staging.at[part], output.at[part], sems.at[i]))
        copies[-1].start()
    for copy in copies:
        copy.wait()


def toggle(value, bits):
    peers = lax.axis_size("dom")
    return lax.ppermute(value, "dom", [(i, i ^ bits) for i in range(peers)])


def across(value):
    peers = lax.axis_size("dom")
    pairs = [(i, (i + 1) % peers if i % 2 else (i - 1) % peers) for i in range(peers)]
    return lax.ppermute(value, "dom", pairs)


def exchange(outs, cap):
    width = outs[0].shape[1]
    if len(outs) == 3:
        outer, inner, far = outs
        peers = lax.axis_size("dom")
        blocks = far.reshape(peers, cap, width)
        blocks = lax.all_to_all(blocks, "dom", split_axis=0, concat_axis=0, tiled=True)
        return [across(outer), toggle(inner, 1), blocks.reshape(-1, width)]
    outer, inner, own, *rest = outs
    columns = STAGED // PLANE
    moved = [toggle(rest[m - 1], m * PLANE) for m in reversed(range(1, columns))]
    outer_in = across(outer)
    block = columns * cap
    blocks = call(
        shuffle,
        [((block, width), BF), ((inner.shape[0] + block, width), BF), ((block, width), BF), ((block, width), BF)],
        2 * (STAGED * cap) ** 2 * width,
        inner, own, *moved,
    )
    return [outer_in, toggle(blocks[1], 1), toggle(blocks[3], 3), toggle(blocks[2], 2), blocks[0]]


def on_device(
    grid_latent,
    mesh_latent,
    encoder_weight,
    processor_weights,
    decoder_weight,
    cotangent,
    grid_halo_rows,
    encoder_neighbours,
    halo_rows,
    far_sources,
    mesh_neighbours,
    decoder_neighbours,
):
    devices = lax.axis_size("dom")
    grid_rows, width = grid_latent.shape
    mesh_rows = mesh_latent.shape[0]
    ghalo = grid_halo_rows.shape[2]
    halo = halo_rows.shape[2]
    cap = far_sources.shape[2]
    slots = devices * cap
    listed = 2 * halo + slots
    scale = 1.0 / mesh_neighbours.shape[1]
    me = lax.axis_index("dom").astype(jnp.int32).reshape(1)

    def square(rows, depth):
        return 2 * rows * depth * width

    def sends(per_side):
        stages = STAGED // PLANE if devices == STAGED else 1
        return [((per_side, width), BF)] * 2 + [((slots // stages, width), BF)] * stages

    state = ((mesh_rows, width), BF)
    total = ((mesh_rows, width), F32)
    rim = ((halo, width), BF)
    grid_rim = ((ghalo, width), BF)
    step = 3 * square(mesh_rows, width)

    outer, inner = call(
        grid_send,
        [grid_rim, grid_rim],
        64 * square(grid_rows, width),
        me, grid_latent, grid_halo_rows,
        scalars=1, hbm=2, limit=60 * 1024 * 1024,
        scratch=copies_of([grid_latent, grid_halo_rows]) + [pltpu.SemaphoreType.DMA((CHUNKS + 1,))],
    )
    outer_in, inner_in = across(outer), toggle(inner, 1)

    own_t, forth_t, back_t, send, receive = call(
        functools.partial(tables, size=halo, devices=devices),
        [((mesh_rows, mesh_rows), BF)] + [((listed, mesh_rows), BF)] * 2 + [((mesh_rows, listed), BF)] * 2,
        64 * square(mesh_rows, mesh_rows),
        me, mesh_neighbours.T, halo_rows, far_sources[0].T,
        scalars=1,
    )
    _, latent, weight, mesh = lax.optimization_barrier((inner, grid_latent, encoder_weight, mesh_latent))
    near, grid_own_t, grid_rim_t, grid_slope = call(
        functools.partial(encoder_local, size=ghalo),
        [total, ((grid_rows, mesh_rows), BF), ((2 * ghalo, mesh_rows), BF), ((grid_rows, width), BF)],
        4 * square(grid_rows, width),
        me, encoder_neighbours.T, weight, latent, mesh,
        scalars=1,
    )

    hidden, *outs = call(
        functools.partial(first_hidden, size=halo),
        [state] + sends(halo),
        step,
        near, grid_rim_t, outer_in, inner_in, encoder_weight, processor_weights, send,
    )
    ins = exchange(outs, cap)
    near, slope_0 = call(
        functools.partial(layer_local, layer=0, scale=scale),
        [total, total],
        6 * square(mesh_rows, mesh_rows),
        hidden, own_t, processor_weights, ins[-1],
        free=1,
    )
    decoder_own_t, decoder_rim_t, decoder_near, outer_extra, inner_extra = call(
        decoder_back,
        [((mesh_rows, grid_rows), BF), ((2 * halo, grid_rows), BF), total, rim, rim],
        square(grid_rows, mesh_rows),
        me, decoder_neighbours.T, cotangent, ins[-1],
        scalars=1, free=1,
    )

    hidden, *outs = call(
        functools.partial(next_hidden, ins=len(ins), layer=1, scale=scale, size=halo),
        [state] + sends(2 * halo),
        step,
        near, forth_t, processor_weights, send, outer_extra, inner_extra, *ins,
    )
    ins = exchange(outs, cap)
    near, slope_1 = call(
        functools.partial(layer_local, layer=1, scale=scale),
        [total, total],
        6 * square(mesh_rows, mesh_rows),
        hidden, own_t, processor_weights, ins[-1],
        free=1,
    )

    message, grad, *outs = call(
        functools.partial(turn, ins=len(ins), scale=scale, size=halo),
        [state, state] + sends(2 * halo),
        2 * step,
        near, forth_t, decoder_weight, send, receive, back_t, decoder_near, *ins,
    )
    ins = exchange(outs, cap)
    (near,) = call(back_local, [total], 6 * square(mesh_rows, mesh_rows), own_t, grad)

    outer_decoder, inner_decoder = ins[:2]
    (near,) = call(back_local, [total], 6 * square(mesh_rows, mesh_rows), own_t, grad, ins[-1], free=1)
    (base,) = call(
        decode_own,
        [((grid_rows, width), F32)],
        square(grid_rows, mesh_rows),
        grid_latent, decoder_own_t, message, ins[-1],
        free=1,
    )

    grad, *outs = call(
        functools.partial(middle_back, ins=len(ins), layer=1, scale=scale, size=halo),
        [state] + sends(halo),
        step,
        near, receive, slope_1, processor_weights, grad, back_t, *ins, base,
        free=1,
    )
    ins = exchange(outs, cap)
    (near,) = call(back_local, [total], 6 * square(mesh_rows, mesh_rows), own_t, grad, ins[-1], free=1)
    output, token = call(
        decode_rim,
        [((grid_rows, width), BF), ((8, 128), F32)],
        square(grid_rows, 2 * halo),
        base, decoder_rim_t, outer_decoder, inner_decoder, ins[-1],
        free=1,
    )

    grad, outer, inner = call(
        functools.partial(last_back, ins=len(ins), scale=scale),
        [state, grid_rim, grid_rim],
        step,
        near, receive, slope_0, processor_weights, grad, grid_rim_t, *ins, token,
        free=1,
    )
    outer_in, inner_in = across(outer), toggle(inner, 1)
    base, table, slope_rows, mesh_grad = call(
        grid_local,
        [((grid_rows, width), F32), ((grid_rows, 2 * ghalo), BF), ((2 * ghalo, width), F32), state],
        square(mesh_rows, grid_rows) + square(grid_rows, width),
        me, grid_own_t, grad, grid_halo_rows, grid_slope, encoder_weight, cotangent,
        scalars=1,
    )
    (grid_grad,) = call(
        grid_back,
        [((grid_rows, width), BF)],
        square(grid_rows, 4 * ghalo),
        base, table, slope_rows, encoder_weight, outer_in, inner_in,
        hbm_out=1,
        scratch=[pltpu.VMEM((grid_rows, width), BF), pltpu.SemaphoreType.DMA((CHUNKS,))],
    )
    return (output, grid_grad, mesh_grad)


def solution(mesh):
    in_specs = (
        P(("groups", "dom"), None),
        P(("groups", "dom"), None),
        P(),
        P(),
        P(),
        P(("groups", "dom"), None),
        P("dom", None, None),
        P("dom", None),
        P("dom", None, None),
        P("dom", None, None),
        P("dom", None),
        P("dom", None),
    )
    out_specs = (P(("groups", "dom"), None), P(("groups", "dom"), None), P(("groups", "dom"), None))
    return jax.shard_map(
        on_device, mesh=mesh, in_specs=in_specs, out_specs=out_specs, check_vma=False
    )
```

```python
import functools

import jax
import jax.numpy as jnp
from jax import lax
from jax.experimental import pallas as pl
from jax.experimental.pallas import tpu as pltpu
from jax.sharding import PartitionSpec as P

BF = jnp.bfloat16
F32 = jnp.float32
VMEM_LIMIT = 24 * 1024 * 1024
PLANE = 4
STAGED = 16
CHUNKS = 4


def mm(a, b):
    return jnp.dot(a, b, preferred_element_type=F32)


def mm_t(a, b):
    return lax.dot_general(a, b, (((1,), (1,)), ((), ())), preferred_element_type=F32)


def t_mm(a, b):
    return lax.dot_general(a, b, (((0,), (0,)), ((), ())), preferred_element_type=F32)


def silu_pair(value):
    sigma = 0.5 + 0.5 * jnp.tanh(0.5 * value)
    message = value * sigma
    return message, sigma + message * (1.0 - sigma)


def match(places, wanted):
    shape = places.shape
    wanted = jnp.broadcast_to(wanted, shape).astype(jnp.int16)
    return jnp.where(places == wanted, jnp.ones(shape, BF), jnp.zeros(shape, BF))


def pick(rows, wanted):
    places = lax.broadcasted_iota(jnp.int32, (rows, wanted.shape[1]), 0).astype(jnp.int16)
    return match(places, wanted)


def counts_t(columns, first, entries):
    degree, rows = entries.shape
    places = (lax.broadcasted_iota(jnp.int32, (columns, rows), 0) + first).astype(jnp.int16)
    total = match(places, entries[0:1])
    for k in range(1, degree):
        total = total + match(places, entries[k : k + 1])
    return total


def side_swap(entries, rows, size, me):
    swapped = jnp.where(entries < rows + size, entries + size, entries - size)
    rim = (entries >= rows) & (entries < rows + 2 * size)
    return jnp.where(rim & (me % 2 == 1), swapped, entries)


def pair_order(lists, me):
    left, right = lists[0, 0:1], lists[0, 1:2]
    odd = me % 2
    return left + odd * (right - left), right + odd * (left - right)


def by_stage(x, devices):
    return (x % PLANE) * (devices // PLANE) + x // PLANE


def call(body, out_shapes, flops, *args, hbm=0, free=0, hbm_out=0, scratch=(), limit=VMEM_LIMIT):
    shapes = [jax.ShapeDtypeStruct(s, t) for s, t in out_shapes]
    size = sum(a.size * a.dtype.itemsize for a in args)
    size += sum(s.size * s.dtype.itemsize for s in shapes)
    size *= hbm == 0
    places = [pltpu.HBM] * hbm + [pltpu.VMEM] * (len(args) - hbm - free)
    places += [pl.ANY] * free
    out_places = [pltpu.HBM] * hbm_out + [pltpu.VMEM] * (len(shapes) - hbm_out)
    kept = len(args) - free
    inner = body if free == 0 else lambda *refs: body(*refs[:kept], *refs[len(args) :])
    return pl.pallas_call(
        inner,
        out_shape=shapes,
        in_specs=[pl.BlockSpec(memory_space=place) for place in places],
        out_specs=[pl.BlockSpec(memory_space=place) for place in out_places],
        scratch_shapes=list(scratch),
        compiler_params=pltpu.CompilerParams(vmem_limit_bytes=limit),
        cost_estimate=pl.CostEstimate(flops=flops, bytes_accessed=size, transcendentals=0),
    )(*args)


def copies_of(arrays):
    return [pltpu.VMEM(a.shape, a.dtype) for a in arrays]


def fetch(sources, targets, sems):
    copies = [pltpu.make_async_copy(s, t, sems.at[i]) for i, (s, t) in enumerate(zip(sources, targets))]
    for copy in copies:
        copy.start()
    return copies


def row_chunks(rows):
    step = rows // CHUNKS
    return [pl.ds(i * step, step) for i in range(CHUNKS)]


def grid_send(latent, lists, outer, inner, values, wanted, sems):
    me = lax.axis_index("dom")
    parts = row_chunks(latent.shape[0])
    sources = [lists] + [latent.at[part] for part in parts]
    copies = fetch(sources, [wanted] + [values.at[part] for part in parts], sems)
    copies[0].wait()
    wanted_outer, wanted_inner = pair_order(wanted, me)
    step = latent.shape[0] // CHUNKS
    outer_rows = inner_rows = 0.0
    for i, part in enumerate(parts):
        copies[i + 1].wait()
        chunk = values[part]
        outer_rows += t_mm(pick(step, wanted_outer - i * step), chunk)
        inner_rows += t_mm(pick(step, wanted_inner - i * step), chunk)
    outer[...] = outer_rows.astype(BF)
    inner[...] = inner_rows.astype(BF)


def encoder_local(entries, weight, latent, mesh, near, grid_own_t, grid_rim_t, slope, *, size):
    me = lax.axis_index("dom")
    rows = latent.shape[0]
    columns = side_swap(entries[...], rows, size, me)
    own = counts_t(rows, 0, columns)
    grid_own_t[...] = own
    grid_rim_t[...] = counts_t(2 * size, rows, columns)
    message, gradient = silu_pair(mm(latent[...], weight[...]))
    slope[...] = gradient.astype(BF)
    near[...] = mesh[...].astype(F32) + t_mm(own, message.astype(BF))


def list_tables(me, lists, far_lists, send, receive):
    rows = send.shape[0]
    size = lists.shape[2]
    cap, devices = far_lists.shape
    outer, inner = pair_order(lists, me)
    rim = [pick(rows, outer), pick(rows, inner)]
    for k in range(2):
        send[:, k * size : (k + 1) * size] = rim[k]
        receive[:, k * size : (k + 1) * size] = rim[k]
    partner = lax.broadcasted_iota(jnp.int32, (devices, devices * cap), 0)
    place = lax.broadcasted_iota(jnp.int32, (devices, devices * cap), 1)
    if devices == STAGED:
        x = partner ^ me
        send_place, receive_place = x * cap, by_stage(x, devices) * cap
    else:
        send_place, receive_place = partner * cap, partner * cap
    send_far = jnp.zeros((rows, devices * cap), F32)
    receive_far = jnp.zeros((rows, devices * cap), F32)
    for j in range(cap):
        chosen = pick(rows, far_lists[j : j + 1])
        send_far += mm(chosen, (place == send_place + j).astype(F32).astype(BF))
        receive_far += mm(chosen, (place == receive_place + j).astype(F32).astype(BF))
    send[:, 2 * size :] = send_far.astype(BF)
    receive[:, 2 * size :] = receive_far.astype(BF)


def mesh_tables(me, entries, own_t, forth_t, back_t, size, devices):
    rows = own_t.shape[0]
    slots = forth_t.shape[0] - 2 * size
    cap = slots // devices
    columns = side_swap(entries[...], rows, size, me)
    own_t[...] = counts_t(rows, 0, columns)
    rim = counts_t(2 * size, rows, columns)
    forth_t[: 2 * size] = rim
    back_t[: 2 * size] = rim
    far = jnp.maximum(columns - rows - 2 * size, 0)
    partner, slot = far // cap, far % cap
    if devices == STAGED:
        partner = partner ^ me
        send_place, receive_place = partner * cap + slot, by_stage(partner, devices) * cap + slot
    else:
        send_place, receive_place = far, far
    is_far = columns >= rows + 2 * size
    forth_t[2 * size :] = counts_t(slots, 0, jnp.where(is_far, receive_place, -1))
    back_t[2 * size :] = counts_t(slots, 0, jnp.where(is_far, send_place, -1))


def decoder_back(entries, cotangent, own_t, rim_t, near, outer, inner):
    me = lax.axis_index("dom")
    rows = near.shape[0]
    size = outer.shape[0]
    columns = side_swap(entries[...], rows, size, me)
    own = counts_t(rows, 0, columns)
    side = counts_t(2 * size, rows, columns)
    own_t[...] = own
    rim_t[...] = side
    grads = cotangent[...]
    near[...] = mm(own, grads)
    back = mm(side, grads).astype(BF)
    outer[...] = back[:size]
    inner[...] = back[size:]


def emit(outs, rows, size, extra=None):
    rows = rows.astype(BF)
    for k in range(2):
        outs[k][:size] = rows[k * size : (k + 1) * size]
        if extra is not None:
            outs[k][size:] = extra[k]
    far = rows[2 * size :]
    block = far.shape[0] // (len(outs) - 2)
    for m, out in enumerate(outs[2:]):
        out[...] = far[m * block : (m + 1) * block]


def arrived(ins, size):
    outer, inner = ins[:2]
    parts = [outer[:size], inner[:size]]
    if len(ins) > 3:
        third, second, own = ins[2:]
        parts += [own[...], inner[inner.shape[0] - own.shape[0] :], second[...], third[...]]
    else:
        parts += [ref[...] for ref in ins[2:]]
    return jnp.concatenate(parts, axis=0)


def shuffle(inner, own, *refs):
    columns = STAGED // PLANE
    parts = [own[...]] + [ref[...] for ref in refs[: columns - 1][::-1]]
    rows = jnp.concatenate(parts, axis=0)
    outs = refs[columns - 1 :]
    count = rows.shape[0]
    cap = count // STAGED
    target = lax.broadcasted_iota(jnp.int32, (count, count), 0)
    source = lax.broadcasted_iota(jnp.int32, (count, count), 1)
    place, slot = target // cap, target % cap
    wanted = ((place % columns) * PLANE + place // columns) * cap + slot
    moved = mm((source == wanted).astype(F32).astype(BF), rows).astype(BF)
    block = columns * cap
    used = inner.shape[0]
    outs[1][:used] = inner[...]
    outs[1][used:] = moved[block : 2 * block]
    for k in (0, 2, 3):
        outs[k][...] = moved[k * block : (k + 1) * block]


def tables(entries, lists, far_lists, own_t, forth_t, back_t, send, receive, *, size, devices):
    me = lax.axis_index("dom")
    mesh_tables(me, entries, own_t, forth_t, back_t, size, devices)
    list_tables(me, lists, far_lists, send, receive)


def layer_local(hidden, own_t, weight, near, slope, *, layer, scale):
    state = hidden[...]
    value, gradient = silu_pair(mm(state, weight[layer]))
    slope[...] = gradient
    near[...] = state.astype(F32) + scale * t_mm(own_t[...], value.astype(BF))


def back_local(own_t, grad, near):
    near[...] = mm(own_t[...], grad[...])


def chosen_messages(send, state, weight):
    return silu_pair(mm(t_mm(send[...], state).astype(BF), weight))[0]


def first_hidden(near, rim_t, outer_in, inner_in, encoder, weight, send, hidden, *outs, size):
    incoming = silu_pair(mm(arrived([outer_in, inner_in], outer_in.shape[0]), encoder[...]))[0].astype(BF)
    state = (near[...] + t_mm(rim_t[...], incoming)).astype(BF)
    hidden[...] = state
    emit(outs, chosen_messages(send, state, weight[0]), size)


def next_hidden(near, forth_t, weight, send, outer_extra, inner_extra, *refs, ins, layer, scale, size):
    rows = arrived(refs[:ins], size)
    state = (near[...] + scale * t_mm(forth_t[...], rows)).astype(BF)
    refs[ins][...] = state
    emit(refs[ins + 1 :], chosen_messages(send, state, weight[layer]), size, (outer_extra[...], inner_extra[...]))


def turn(near, forth_t, weight, receive, back_t, back_near, *refs, ins, scale, size):
    rows = arrived(refs[:ins], size)
    message, grad = refs[ins : ins + 2]
    state = (near[...] + scale * t_mm(forth_t[...], rows)).astype(BF)
    value, gradient = silu_pair(mm(state, weight[...]))
    value = value.astype(BF)
    message[...] = value
    returned = jnp.concatenate([refs[0][size : 2 * size], refs[1][size : 2 * size]], axis=0)
    back = back_near[...] + mm(receive[:, : 2 * size], returned)
    change = mm_t((back * gradient).astype(BF), weight[...]).astype(BF)
    grad[...] = change
    emit(refs[ins + 2 :], mm(back_t[...], change), size)


def rim_messages(send, message, outer, inner):
    size = outer.shape[0]
    rows = t_mm(send[:, : 2 * size], message[...]).astype(BF)
    outer[...] = rows[:size]
    inner[...] = rows[size:]


def layer_back(near, receive, rows, slope, weight, grad, scale):
    total = near[...] + mm(receive[...], rows)
    change = (total * scale * slope[...]).astype(BF)
    return (grad[...].astype(F32) + mm_t(change, weight)).astype(BF)


def middle_back(near, receive, slope, weight, grad, back_t, *refs, ins, layer, scale, size):
    rows = arrived(refs[:ins], size)
    change = layer_back(near, receive, rows, slope, weight[layer], grad, scale)
    refs[ins][...] = change
    emit(refs[ins + 1 :], mm(back_t[...], change), size)


def last_back(near, receive, slope, weight, grad, grid_rim_t, *refs, ins, scale):
    new_grad, outer, inner = refs[ins:]
    rows = arrived(refs[:ins], refs[0].shape[0])
    change = layer_back(near, receive, rows, slope, weight[0], grad, scale)
    new_grad[...] = change
    back = mm(grid_rim_t[...], change).astype(BF)
    outer[...] = back[: outer.shape[0]]
    inner[...] = back[outer.shape[0] :]


def decode_own(latent, own_t, message, base):
    base[...] = latent[...].astype(F32) + t_mm(own_t[...], message[...])


def decode_rim(base, rim_t, outer_in, inner_in, output):
    incoming = jnp.concatenate([outer_in[...], inner_in[...]], axis=0)
    output[...] = (base[...] + t_mm(rim_t[...], incoming)).astype(BF)


def grid_local(own_t, grad, lists, slope, weight, cotangent, base, table, slope_rows, mesh_grad):
    me = lax.axis_index("dom")
    mesh_grad[...] = grad[...]
    rows = own_t.shape[0]
    size = lists.shape[2]
    for k, wanted in enumerate(pair_order(lists, me)):
        table[:, k * size : (k + 1) * size] = pick(rows, wanted)
    slope_rows[...] = t_mm(table[...], slope[...])
    change = (mm(own_t[...], grad[...]) * slope[...].astype(F32)).astype(BF)
    base[...] = cotangent[...].astype(F32) + mm_t(change, weight[...])


def grid_back(base, table, slope_rows, weight, outer_in, inner_in, output, staging, sems):
    returned = jnp.concatenate([outer_in[...], inner_in[...]], axis=0).astype(F32)
    change = mm_t((returned * slope_rows[...]).astype(BF), weight[...]).astype(BF)
    copies = []
    for i, part in enumerate(row_chunks(base.shape[0])):
        staging[part] = (base[part] + mm(table[part], change)).astype(BF)
        copies.append(pltpu.make_async_copy(staging.at[part], output.at[part], sems.at[i]))
        copies[-1].start()
    for copy in copies:
        copy.wait()


def toggle(value, bits):
    peers = lax.axis_size("dom")
    return lax.ppermute(value, "dom", [(i, i ^ bits) for i in range(peers)])


def across(value):
    peers = lax.axis_size("dom")
    pairs = [(i, (i + 1) % peers if i % 2 else (i - 1) % peers) for i in range(peers)]
    return lax.ppermute(value, "dom", pairs)


def exchange(outs, cap, after=()):
    width = outs[0].shape[1]
    if len(outs) == 3:
        outer, inner, far = outs
        peers = lax.axis_size("dom")
        blocks = far.reshape(peers, cap, width)
        blocks = lax.all_to_all(blocks, "dom", split_axis=0, concat_axis=0, tiled=True)
        return [across(outer), toggle(inner, 1), blocks.reshape(-1, width)]
    outer, inner, own, *rest = outs
    columns = STAGED // PLANE
    moved = [toggle(rest[m - 1], m * PLANE) for m in reversed(range(1, columns))]
    outer_in = across(outer)
    block = columns * cap
    blocks = call(
        shuffle,
        [((block, width), BF), ((inner.shape[0] + block, width), BF), ((block, width), BF), ((block, width), BF)],
        2 * (STAGED * cap) ** 2 * width,
        inner, own, *moved, *after,
        free=len(after),
    )
    return [outer_in, toggle(blocks[1], 1), toggle(blocks[3], 3), toggle(blocks[2], 2), blocks[0]]


def on_device(
    grid_latent,
    mesh_latent,
    encoder_weight,
    processor_weights,
    decoder_weight,
    cotangent,
    grid_halo_rows,
    encoder_neighbours,
    halo_rows,
    far_sources,
    mesh_neighbours,
    decoder_neighbours,
):
    devices = lax.axis_size("dom")
    grid_rows, width = grid_latent.shape
    mesh_rows = mesh_latent.shape[0]
    ghalo = grid_halo_rows.shape[2]
    halo = halo_rows.shape[2]
    cap = far_sources.shape[2]
    slots = devices * cap
    listed = 2 * halo + slots
    scale = 1.0 / mesh_neighbours.shape[1]

    def square(rows, depth):
        return 2 * rows * depth * width

    def sends(per_side):
        stages = STAGED // PLANE if devices == STAGED else 1
        return [((per_side, width), BF)] * 2 + [((slots // stages, width), BF)] * stages

    state = ((mesh_rows, width), BF)
    total = ((mesh_rows, width), F32)
    rim = ((halo, width), BF)
    grid_rim = ((ghalo, width), BF)
    step = 3 * square(mesh_rows, width)

    outer, inner = call(
        grid_send,
        [grid_rim, grid_rim],
        64 * square(grid_rows, width),
        grid_latent, grid_halo_rows,
        hbm=2, limit=60 * 1024 * 1024,
        scratch=copies_of([grid_latent, grid_halo_rows]) + [pltpu.SemaphoreType.DMA((CHUNKS + 1,))],
    )
    outer_in, inner_in = across(outer), toggle(inner, 1)

    own_t, forth_t, back_t, send, receive = call(
        functools.partial(tables, size=halo, devices=devices),
        [((mesh_rows, mesh_rows), BF)] + [((listed, mesh_rows), BF)] * 2 + [((mesh_rows, listed), BF)] * 2,
        64 * square(mesh_rows, mesh_rows),
        mesh_neighbours.T, halo_rows, far_sources[0].T,
    )
    _, latent, weight, mesh = lax.optimization_barrier((inner, grid_latent, encoder_weight, mesh_latent))
    near, grid_own_t, grid_rim_t, grid_slope = call(
        functools.partial(encoder_local, size=ghalo),
        [total, ((grid_rows, mesh_rows), BF), ((2 * ghalo, mesh_rows), BF), ((grid_rows, width), BF)],
        4 * square(grid_rows, width),
        encoder_neighbours.T, weight, latent, mesh,
    )

    hidden, *outs = call(
        functools.partial(first_hidden, size=halo),
        [state] + sends(halo),
        step,
        near, grid_rim_t, outer_in, inner_in, encoder_weight, processor_weights, send,
    )
    ins = exchange(outs, cap)
    near, slope_0 = call(
        functools.partial(layer_local, layer=0, scale=scale),
        [total, total],
        6 * square(mesh_rows, mesh_rows),
        hidden, own_t, processor_weights, ins[-1],
        free=1,
    )
    decoder_own_t, decoder_rim_t, decoder_near, outer_extra, inner_extra = call(
        decoder_back,
        [((mesh_rows, grid_rows), BF), ((2 * halo, grid_rows), BF), total, rim, rim],
        square(grid_rows, mesh_rows),
        decoder_neighbours.T, cotangent, ins[-1],
        free=1,
    )

    hidden, *outs = call(
        functools.partial(next_hidden, ins=len(ins), layer=1, scale=scale, size=halo),
        [state] + sends(2 * halo),
        step,
        near, forth_t, processor_weights, send, outer_extra, inner_extra, *ins,
    )
    ins = exchange(outs, cap)
    near, slope_1 = call(
        functools.partial(layer_local, layer=1, scale=scale),
        [total, total],
        6 * square(mesh_rows, mesh_rows),
        hidden, own_t, processor_weights, ins[-1],
        free=1,
    )

    message, grad, *outs = call(
        functools.partial(turn, ins=len(ins), scale=scale, size=halo),
        [state, state] + sends(halo),
        2 * step,
        near, forth_t, decoder_weight, receive, back_t, decoder_near, *ins,
    )
    ins = exchange(outs, cap)
    (near,) = call(back_local, [total], 6 * square(mesh_rows, mesh_rows), own_t, grad)

    outer, inner = call(rim_messages, [rim, rim], square(2 * halo, mesh_rows), send, message, ins[-1], free=1)
    outer_decoder, inner_decoder = across(outer), toggle(inner, 1)
    (near,) = call(back_local, [total], 3 * square(mesh_rows, mesh_rows), own_t, grad, ins[-1], free=1)

    grad, *outs = call(
        functools.partial(middle_back, ins=len(ins), layer=1, scale=scale, size=halo),
        [state] + sends(halo),
        step,
        near, receive, slope_1, processor_weights, grad, back_t, *ins,
    )
    ins = exchange(outs, cap, [outer_decoder, inner_decoder])
    (near,) = call(back_local, [total], 6 * square(mesh_rows, mesh_rows), own_t, grad, ins[-1], free=1)
    (decoded,) = call(
        decode_own,
        [((grid_rows, width), F32)],
        square(grid_rows, mesh_rows),
        grid_latent, decoder_own_t, message, ins[-1],
        free=1,
    )

    grad, outer, inner = call(
        functools.partial(last_back, ins=len(ins), scale=scale),
        [state, grid_rim, grid_rim],
        step,
        near, receive, slope_0, processor_weights, grad, grid_rim_t, *ins, decoded,
        free=1,
    )
    outer_in, inner_in = across(outer), toggle(inner, 1)
    (output,) = call(
        decode_rim,
        [((grid_rows, width), BF)],
        square(grid_rows, 2 * halo),
        decoded, decoder_rim_t, outer_decoder, inner_decoder, grad,
        free=1,
    )
    base, table, slope_rows, mesh_grad = call(
        grid_local,
        [((grid_rows, width), F32), ((grid_rows, 2 * ghalo), BF), ((2 * ghalo, width), F32), state],
        square(mesh_rows, grid_rows) + square(grid_rows, width),
        grid_own_t, grad, grid_halo_rows, grid_slope, encoder_weight, cotangent,
    )
    (grid_grad,) = call(
        grid_back,
        [((grid_rows, width), BF)],
        square(grid_rows, 4 * ghalo),
        base, table, slope_rows, encoder_weight, outer_in, inner_in,
        hbm_out=1,
        scratch=[pltpu.VMEM((grid_rows, width), BF), pltpu.SemaphoreType.DMA((CHUNKS,))],
    )
    return (output, grid_grad, mesh_grad)


def solution(mesh):
    in_specs = (
        P(("groups", "dom"), None),
        P(("groups", "dom"), None),
        P(),
        P(),
        P(),
        P(("groups", "dom"), None),
        P("dom", None, None),
        P("dom", None),
        P("dom", None, None),
        P("dom", None, None),
        P("dom", None),
        P("dom", None),
    )
    out_specs = (P(("groups", "dom"), None), P(("groups", "dom"), None), P(("groups", "dom"), None))
    return jax.shard_map(
        on_device, mesh=mesh, in_specs=in_specs, out_specs=out_specs, check_vma=False
    )
```

```python
import functools

import jax
import jax.numpy as jnp
from jax import lax
from jax.experimental import pallas as pl
from jax.experimental.pallas import tpu as pltpu
from jax.sharding import PartitionSpec as P

BF = jnp.bfloat16
F32 = jnp.float32
VMEM_LIMIT = 24 * 1024 * 1024
FIRST_LIMIT = 60 * 1024 * 1024
PLANE = 4
STAGED = 16
CHUNKS = 4


def mm(a, b):
    return jnp.dot(a, b, preferred_element_type=F32)


def mm_t(a, b):
    return lax.dot_general(a, b, (((1,), (1,)), ((), ())), preferred_element_type=F32)


def t_mm(a, b):
    return lax.dot_general(a, b, (((0,), (0,)), ((), ())), preferred_element_type=F32)


def silu_pair(value):
    sigma = 0.5 + 0.5 * jnp.tanh(0.5 * value)
    message = value * sigma
    return message, sigma + message * (1.0 - sigma)


def match(places, wanted):
    shape = places.shape
    wanted = jnp.broadcast_to(wanted, shape).astype(jnp.int16)
    return jnp.where(places == wanted, jnp.ones(shape, BF), jnp.zeros(shape, BF))


def pick(rows, wanted):
    places = lax.broadcasted_iota(jnp.int32, (rows, wanted.shape[1]), 0).astype(jnp.int16)
    return match(places, wanted)


def counts_t(columns, first, entries):
    degree, rows = entries.shape
    places = (lax.broadcasted_iota(jnp.int32, (columns, rows), 0) + first).astype(jnp.int16)
    total = match(places, entries[0:1])
    for k in range(1, degree):
        total = total + match(places, entries[k : k + 1])
    return total


def side_swap(entries, rows, size, me):
    swapped = jnp.where(entries < rows + size, entries + size, entries - size)
    rim = (entries >= rows) & (entries < rows + 2 * size)
    return jnp.where(rim & (me % 2 == 1), swapped, entries)


def pair_order(lists, me):
    left, right = lists[0, 0:1], lists[0, 1:2]
    odd = me % 2
    return left + odd * (right - left), right + odd * (left - right)


def by_stage(x, devices):
    return (x % PLANE) * (devices // PLANE) + x // PLANE


def call(body, out_shapes, flops, *args, hbm=0, free=0, hbm_out=0, scratch=(), limit=VMEM_LIMIT):
    shapes = [jax.ShapeDtypeStruct(s, t) for s, t in out_shapes]
    size = sum(a.size * a.dtype.itemsize for a in args)
    size += sum(s.size * s.dtype.itemsize for s in shapes)
    size *= hbm == 0
    places = [pltpu.HBM] * hbm + [pltpu.VMEM] * (len(args) - hbm - free)
    places += [pl.ANY] * free
    out_places = [pltpu.HBM] * hbm_out + [pltpu.VMEM] * (len(shapes) - hbm_out)
    kept = len(args) - free
    inner = body if free == 0 else lambda *refs: body(*refs[:kept], *refs[len(args) :])
    return pl.pallas_call(
        inner,
        out_shape=shapes,
        in_specs=[pl.BlockSpec(memory_space=place) for place in places],
        out_specs=[pl.BlockSpec(memory_space=place) for place in out_places],
        scratch_shapes=list(scratch),
        compiler_params=pltpu.CompilerParams(vmem_limit_bytes=limit),
        cost_estimate=pl.CostEstimate(flops=flops, bytes_accessed=size, transcendentals=0),
    )(*args)


def copies_of(arrays):
    return [pltpu.VMEM(a.shape, a.dtype) for a in arrays]


def fetch(sources, targets, sems):
    copies = [pltpu.make_async_copy(s, t, sems.at[i]) for i, (s, t) in enumerate(zip(sources, targets))]
    for copy in copies:
        copy.start()
    return copies


def row_chunks(rows):
    step = rows // CHUNKS
    return [pl.ds(i * step, step) for i in range(CHUNKS)]


def grid_send(latent, lists, outer, inner, values, wanted, rows, sems):
    parts = row_chunks(latent.shape[0])
    copies = fetch([lists] + [latent.at[part] for part in parts], [wanted] + [values.at[part] for part in parts], sems)
    size = outer.shape[0]
    step = latent.shape[0] // CHUNKS
    copies[0].wait()
    listed = jnp.concatenate(pair_order(wanted, lax.axis_index("dom")), axis=1)
    chosen = pick(latent.shape[0], listed)
    total = 0.0
    for i, part in enumerate(parts):
        copies[i + 1].wait()
        total += t_mm(chosen[i * step : (i + 1) * step], values[part])
    rows[...] = total.astype(BF)
    sides = [rows.at[pl.ds(0, size)], rows.at[pl.ds(size, size)]]
    for copy in fetch(sides, [outer, inner], sems):
        copy.wait()


def encoder_local(entries, weight, latent, mesh, near, grid_own_t, grid_rim_t, slope, *, size):
    me = lax.axis_index("dom")
    rows = latent.shape[0]
    columns = side_swap(entries[...], rows, size, me)
    own = counts_t(rows, 0, columns)
    grid_own_t[...] = own
    grid_rim_t[...] = counts_t(2 * size, rows, columns)
    message, gradient = silu_pair(mm(latent[...], weight[...]))
    slope[...] = gradient.astype(BF)
    near[...] = mesh[...].astype(F32) + t_mm(own, message.astype(BF))


def list_tables(me, lists, far_lists, send, receive):
    rows = send.shape[0]
    size = lists.shape[2]
    cap, devices = far_lists.shape
    outer, inner = pair_order(lists, me)
    rim = [pick(rows, outer), pick(rows, inner)]
    for k in range(2):
        send[:, k * size : (k + 1) * size] = rim[k]
        receive[:, k * size : (k + 1) * size] = rim[k]
    partner = lax.broadcasted_iota(jnp.int32, (devices, devices * cap), 0)
    place = lax.broadcasted_iota(jnp.int32, (devices, devices * cap), 1)
    if devices == STAGED:
        x = partner ^ me
        send_place, receive_place = x * cap, by_stage(x, devices) * cap
    else:
        send_place, receive_place = partner * cap, partner * cap
    send_far = jnp.zeros((rows, devices * cap), F32)
    receive_far = jnp.zeros((rows, devices * cap), F32)
    for j in range(cap):
        chosen = pick(rows, far_lists[j : j + 1])
        send_far += mm(chosen, (place == send_place + j).astype(F32).astype(BF))
        receive_far += mm(chosen, (place == receive_place + j).astype(F32).astype(BF))
    send[:, 2 * size :] = send_far.astype(BF)
    receive[:, 2 * size :] = receive_far.astype(BF)


def mesh_tables(me, entries, own_t, forth_t, back_t, size, devices):
    rows = own_t.shape[0]
    slots = forth_t.shape[0] - 2 * size
    cap = slots // devices
    columns = side_swap(entries[...], rows, size, me)
    own_t[...] = counts_t(rows, 0, columns)
    rim = counts_t(2 * size, rows, columns)
    forth_t[: 2 * size] = rim
    back_t[: 2 * size] = rim
    far = jnp.maximum(columns - rows - 2 * size, 0)
    partner, slot = far // cap, far % cap
    if devices == STAGED:
        partner = partner ^ me
        send_place, receive_place = partner * cap + slot, by_stage(partner, devices) * cap + slot
    else:
        send_place, receive_place = far, far
    is_far = columns >= rows + 2 * size
    forth_t[2 * size :] = counts_t(slots, 0, jnp.where(is_far, receive_place, -1))
    back_t[2 * size :] = counts_t(slots, 0, jnp.where(is_far, send_place, -1))


def decoder_back(entries, cotangent, own_t, rim_t, near, outer, inner):
    me = lax.axis_index("dom")
    rows = near.shape[0]
    size = outer.shape[0]
    columns = side_swap(entries[...], rows, size, me)
    own = counts_t(rows, 0, columns)
    side = counts_t(2 * size, rows, columns)
    own_t[...] = own
    rim_t[...] = side
    grads = cotangent[...]
    near[...] = mm(own, grads)
    back = mm(side, grads).astype(BF)
    outer[...] = back[:size]
    inner[...] = back[size:]


def emit(outs, rows, size, extra=None):
    rows = rows.astype(BF)
    for k in range(2):
        outs[k][:size] = rows[k * size : (k + 1) * size]
        if extra is not None:
            outs[k][size:] = extra[k]
    far = rows[2 * size :]
    block = far.shape[0] // (len(outs) - 2)
    for m, out in enumerate(outs[2:]):
        out[...] = far[m * block : (m + 1) * block]


def arrived(ins, size):
    outer, inner = ins[:2]
    parts = [outer[:size], inner[:size]]
    if len(ins) > 3:
        third, second, own = ins[2:]
        parts += [own[...], inner[inner.shape[0] - own.shape[0] :], second[...], third[...]]
    else:
        parts += [ref[...] for ref in ins[2:]]
    return jnp.concatenate(parts, axis=0)


def shuffle(inner, own, *refs):
    columns = STAGED // PLANE
    parts = [own[...]] + [ref[...] for ref in refs[: columns - 1][::-1]]
    rows = jnp.concatenate(parts, axis=0)
    outs = refs[columns - 1 :]
    count = rows.shape[0]
    cap = count // STAGED
    target = lax.broadcasted_iota(jnp.int32, (count, count), 0)
    source = lax.broadcasted_iota(jnp.int32, (count, count), 1)
    place, slot = target // cap, target % cap
    wanted = ((place % columns) * PLANE + place // columns) * cap + slot
    moved = mm((source == wanted).astype(F32).astype(BF), rows).astype(BF)
    block = columns * cap
    used = inner.shape[0]
    outs[1][:used] = inner[...]
    outs[1][used:] = moved[block : 2 * block]
    for k in (0, 2, 3):
        outs[k][...] = moved[k * block : (k + 1) * block]


def tables(entries, lists, far_lists, own_t, forth_t, back_t, send, receive, *, size, devices):
    me = lax.axis_index("dom")
    mesh_tables(me, entries, own_t, forth_t, back_t, size, devices)
    list_tables(me, lists, far_lists, send, receive)


def layer_local(hidden, own_t, weight, near, slope, *, layer, scale):
    state = hidden[...]
    value, gradient = silu_pair(mm(state, weight[layer]))
    slope[...] = gradient
    near[...] = state.astype(F32) + scale * t_mm(own_t[...], value.astype(BF))


def back_local(own_t, grad, near):
    near[...] = mm(own_t[...], grad[...])


def chosen_messages(send, state, weight):
    return silu_pair(mm(t_mm(send[...], state).astype(BF), weight))[0]


def first_hidden(near, rim_t, outer_in, inner_in, encoder, weight, send, hidden, *outs, size):
    incoming = silu_pair(mm(arrived([outer_in, inner_in], outer_in.shape[0]), encoder[...]))[0].astype(BF)
    state = (near[...] + t_mm(rim_t[...], incoming)).astype(BF)
    hidden[...] = state
    emit(outs, chosen_messages(send, state, weight[0]), size)


def next_hidden(near, forth_t, weight, send, outer_extra, inner_extra, *refs, ins, layer, scale, size):
    rows = arrived(refs[:ins], size)
    state = (near[...] + scale * t_mm(forth_t[...], rows)).astype(BF)
    refs[ins][...] = state
    emit(refs[ins + 1 :], chosen_messages(send, state, weight[layer]), size, (outer_extra[...], inner_extra[...]))


def turn(near, forth_t, weight, send, receive, back_t, back_near, *refs, ins, scale, size):
    rows = arrived(refs[:ins], size)
    message, grad = refs[ins : ins + 2]
    state = (near[...] + scale * t_mm(forth_t[...], rows)).astype(BF)
    value, gradient = silu_pair(mm(state, weight[...]))
    value = value.astype(BF)
    message[...] = value
    returned = jnp.concatenate([refs[0][size : 2 * size], refs[1][size : 2 * size]], axis=0)
    back = back_near[...] + mm(receive[:, : 2 * size], returned)
    change = mm_t((back * gradient).astype(BF), weight[...]).astype(BF)
    grad[...] = change
    rim = t_mm(send[:, : 2 * size], value).astype(BF)
    emit(refs[ins + 2 :], mm(back_t[...], change), size, (rim[:size], rim[size:]))


def layer_back(near, receive, rows, slope, weight, grad, scale):
    total = near[...] + mm(receive[...], rows)
    change = (total * scale * slope[...]).astype(BF)
    return (grad[...].astype(F32) + mm_t(change, weight)).astype(BF)


def middle_back(near, receive, slope, weight, grad, back_t, *refs, ins, layer, scale, size):
    rows = arrived(refs[:ins], size)
    change = layer_back(near, receive, rows, slope, weight[layer], grad, scale)
    refs[ins][...] = change
    emit(refs[ins + 1 :], mm(back_t[...], change), size)


def last_back(near, receive, slope, weight, grad, grid_rim_t, *refs, ins, scale):
    new_grad, outer, inner = refs[ins:]
    rows = arrived(refs[:ins], refs[0].shape[0])
    change = layer_back(near, receive, rows, slope, weight[0], grad, scale)
    new_grad[...] = change
    back = mm(grid_rim_t[...], change).astype(BF)
    outer[...] = back[: outer.shape[0]]
    inner[...] = back[outer.shape[0] :]


def decode_own(latent, own_t, message, base):
    base[...] = latent[...].astype(F32) + t_mm(own_t[...], message[...])


def decode_rim(base, rim_t, outer_in, inner_in, output, token):
    size = outer_in.shape[0] // 2
    incoming = jnp.concatenate([outer_in[size:], inner_in[size : 2 * size]], axis=0)
    output[...] = (base[...] + t_mm(rim_t[...], incoming)).astype(BF)
    token[...] = jnp.zeros(token.shape, F32)


def grid_local(own_t, grad, lists, slope, weight, cotangent, base, table, slope_rows, mesh_grad):
    me = lax.axis_index("dom")
    mesh_grad[...] = grad[...]
    rows = own_t.shape[0]
    size = lists.shape[2]
    for k, wanted in enumerate(pair_order(lists, me)):
        table[:, k * size : (k + 1) * size] = pick(rows, wanted)
    slope_rows[...] = t_mm(table[...], slope[...])
    change = (mm(own_t[...], grad[...]) * slope[...].astype(F32)).astype(BF)
    base[...] = cotangent[...].astype(F32) + mm_t(change, weight[...])


def grid_back(base, table, slope_rows, weight, outer_in, inner_in, output, staging, sems):
    returned = jnp.concatenate([outer_in[...], inner_in[...]], axis=0).astype(F32)
    change = mm_t((returned * slope_rows[...]).astype(BF), weight[...]).astype(BF)
    copies = []
    for i, part in enumerate(row_chunks(base.shape[0])):
        staging[part] = (base[part] + mm(table[part], change)).astype(BF)
        copies.append(pltpu.make_async_copy(staging.at[part], output.at[part], sems.at[i]))
        copies[-1].start()
    for copy in copies:
        copy.wait()


def toggle(value, bits):
    peers = lax.axis_size("dom")
    return lax.ppermute(value, "dom", [(i, i ^ bits) for i in range(peers)])


def across(value):
    peers = lax.axis_size("dom")
    pairs = [(i, (i + 1) % peers if i % 2 else (i - 1) % peers) for i in range(peers)]
    return lax.ppermute(value, "dom", pairs)


def exchange(outs, cap):
    width = outs[0].shape[1]
    if len(outs) == 3:
        outer, inner, far = outs
        peers = lax.axis_size("dom")
        blocks = far.reshape(peers, cap, width)
        blocks = lax.all_to_all(blocks, "dom", split_axis=0, concat_axis=0, tiled=True)
        return [across(outer), toggle(inner, 1), blocks.reshape(-1, width)]
    outer, inner, own, *rest = outs
    columns = STAGED // PLANE
    moved = [toggle(rest[m - 1], m * PLANE) for m in reversed(range(1, columns))]
    outer_in = across(outer)
    block = columns * cap
    blocks = call(
        shuffle,
        [((block, width), BF), ((inner.shape[0] + block, width), BF), ((block, width), BF), ((block, width), BF)],
        2 * (STAGED * cap) ** 2 * width,
        inner, own, *moved,
    )
    return [outer_in, toggle(blocks[1], 1), toggle(blocks[3], 3), toggle(blocks[2], 2), blocks[0]]


def on_device(
    grid_latent,
    mesh_latent,
    encoder_weight,
    processor_weights,
    decoder_weight,
    cotangent,
    grid_halo_rows,
    encoder_neighbours,
    halo_rows,
    far_sources,
    mesh_neighbours,
    decoder_neighbours,
):
    devices = lax.axis_size("dom")
    grid_rows, width = grid_latent.shape
    mesh_rows = mesh_latent.shape[0]
    ghalo = grid_halo_rows.shape[2]
    halo = halo_rows.shape[2]
    cap = far_sources.shape[2]
    slots = devices * cap
    listed = 2 * halo + slots
    scale = 1.0 / mesh_neighbours.shape[1]

    def square(rows, depth):
        return 2 * rows * depth * width

    def sends(per_side):
        stages = STAGED // PLANE if devices == STAGED else 1
        return [((per_side, width), BF)] * 2 + [((slots // stages, width), BF)] * stages

    state = ((mesh_rows, width), BF)
    total = ((mesh_rows, width), F32)
    rim = ((halo, width), BF)
    grid_rim = ((ghalo, width), BF)
    step = 3 * square(mesh_rows, width)

    outer, inner = call(
        grid_send,
        [grid_rim, grid_rim],
        64 * square(grid_rows, width),
        grid_latent, grid_halo_rows,
        hbm=2, hbm_out=2, limit=FIRST_LIMIT,
        scratch=copies_of([grid_latent, grid_halo_rows])
        + [pltpu.VMEM((2 * ghalo, width), BF), pltpu.SemaphoreType.DMA((CHUNKS + 1,))],
    )
    outer_in, inner_in = across(outer), toggle(inner, 1)

    own_t, forth_t, back_t, send, receive = call(
        functools.partial(tables, size=halo, devices=devices),
        [((mesh_rows, mesh_rows), BF)] + [((listed, mesh_rows), BF)] * 2 + [((mesh_rows, listed), BF)] * 2,
        64 * square(mesh_rows, mesh_rows),
        mesh_neighbours.T, halo_rows, far_sources[0].T,
    )
    _, latent, weight, mesh = lax.optimization_barrier((inner, grid_latent, encoder_weight, mesh_latent))
    near, grid_own_t, grid_rim_t, grid_slope = call(
        functools.partial(encoder_local, size=ghalo),
        [total, ((grid_rows, mesh_rows), BF), ((2 * ghalo, mesh_rows), BF), ((grid_rows, width), BF)],
        4 * square(grid_rows, width),
        encoder_neighbours.T, weight, latent, mesh,
    )

    hidden, *outs = call(
        functools.partial(first_hidden, size=halo),
        [state] + sends(halo),
        step,
        near, grid_rim_t, outer_in, inner_in, encoder_weight, processor_weights, send,
    )
    ins = exchange(outs, cap)
    near, slope_0 = call(
        functools.partial(layer_local, layer=0, scale=scale),
        [total, total],
        6 * square(mesh_rows, mesh_rows),
        hidden, own_t, processor_weights, ins[-1],
        free=1,
    )
    decoder_own_t, decoder_rim_t, decoder_near, outer_extra, inner_extra = call(
        decoder_back,
        [((mesh_rows, grid_rows), BF), ((2 * halo, grid_rows), BF), total, rim, rim],
        square(grid_rows, mesh_rows),
        decoder_neighbours.T, cotangent, ins[-1],
        free=1,
    )

    hidden, *outs = call(
        functools.partial(next_hidden, ins=len(ins), layer=1, scale=scale, size=halo),
        [state] + sends(2 * halo),
        step,
        near, forth_t, processor_weights, send, outer_extra, inner_extra, *ins,
    )
    ins = exchange(outs, cap)
    near, slope_1 = call(
        functools.partial(layer_local, layer=1, scale=scale),
        [total, total],
        6 * square(mesh_rows, mesh_rows),
        hidden, own_t, processor_weights, ins[-1],
        free=1,
    )

    message, grad, *outs = call(
        functools.partial(turn, ins=len(ins), scale=scale, size=halo),
        [state, state] + sends(2 * halo),
        2 * step,
        near, forth_t, decoder_weight, send, receive, back_t, decoder_near, *ins,
    )
    ins = exchange(outs, cap)
    (near,) = call(back_local, [total], 6 * square(mesh_rows, mesh_rows), own_t, grad)

    outer_decoder, inner_decoder = ins[:2]
    (near,) = call(back_local, [total], 6 * square(mesh_rows, mesh_rows), own_t, grad, ins[-1], free=1)
    (base,) = call(
        decode_own,
        [((grid_rows, width), F32)],
        square(grid_rows, mesh_rows),
        grid_latent, decoder_own_t, message, ins[-1],
        free=1,
    )

    grad, *outs = call(
        functools.partial(middle_back, ins=len(ins), layer=1, scale=scale, size=halo),
        [state] + sends(halo),
        step,
        near, receive, slope_1, processor_weights, grad, back_t, *ins, base,
        free=1,
    )
    ins = exchange(outs, cap)
    (near,) = call(back_local, [total], 6 * square(mesh_rows, mesh_rows), own_t, grad, ins[-1], free=1)
    output, token = call(
        decode_rim,
        [((grid_rows, width), BF), ((8, 128), F32)],
        square(grid_rows, 2 * halo),
        base, decoder_rim_t, outer_decoder, inner_decoder, ins[-1],
        free=1,
    )

    grad, outer, inner = call(
        functools.partial(last_back, ins=len(ins), scale=scale),
        [state, grid_rim, grid_rim],
        step,
        near, receive, slope_0, processor_weights, grad, grid_rim_t, *ins, token,
        free=1,
    )
    outer_in, inner_in = across(outer), toggle(inner, 1)
    base, table, slope_rows, mesh_grad = call(
        grid_local,
        [((grid_rows, width), F32), ((grid_rows, 2 * ghalo), BF), ((2 * ghalo, width), F32), state],
        square(mesh_rows, grid_rows) + square(grid_rows, width),
        grid_own_t, grad, grid_halo_rows, grid_slope, encoder_weight, cotangent,
    )
    (grid_grad,) = call(
        grid_back,
        [((grid_rows, width), BF)],
        square(grid_rows, 4 * ghalo),
        base, table, slope_rows, encoder_weight, outer_in, inner_in,
        hbm_out=1,
        scratch=[pltpu.VMEM((grid_rows, width), BF), pltpu.SemaphoreType.DMA((CHUNKS,))],
    )
    return (output, grid_grad, mesh_grad)


def solution(mesh):
    in_specs = (
        P(("groups", "dom"), None),
        P(("groups", "dom"), None),
        P(),
        P(),
        P(),
        P(("groups", "dom"), None),
        P("dom", None, None),
        P("dom", None),
        P("dom", None, None),
        P("dom", None, None),
        P("dom", None),
        P("dom", None),
    )
    out_specs = (P(("groups", "dom"), None), P(("groups", "dom"), None), P(("groups", "dom"), None))
    return jax.shard_map(
        on_device, mesh=mesh, in_specs=in_specs, out_specs=out_specs, check_vma=False
    )
```

```python
import functools

import jax
import jax.numpy as jnp
from jax import lax
from jax.experimental import pallas as pl
from jax.experimental.pallas import tpu as pltpu
from jax.sharding import PartitionSpec as P

BF = jnp.bfloat16
F32 = jnp.float32
VMEM_LIMIT = 24 * 1024 * 1024
FIRST_LIMIT = 60 * 1024 * 1024
PLANE = 4
STAGED = 16
CHUNKS = 4


def mm(a, b):
    return jnp.dot(a, b, preferred_element_type=F32)


def mm_t(a, b):
    return lax.dot_general(a, b, (((1,), (1,)), ((), ())), preferred_element_type=F32)


def t_mm(a, b):
    return lax.dot_general(a, b, (((0,), (0,)), ((), ())), preferred_element_type=F32)


def silu_pair(value):
    sigma = 0.5 + 0.5 * jnp.tanh(0.5 * value)
    message = value * sigma
    return message, sigma + message * (1.0 - sigma)


def match(places, wanted):
    shape = places.shape
    wanted = jnp.broadcast_to(wanted, shape).astype(jnp.int16)
    return jnp.where(places == wanted, jnp.ones(shape, BF), jnp.zeros(shape, BF))


def pick(rows, wanted):
    places = lax.broadcasted_iota(jnp.int32, (rows, wanted.shape[1]), 0).astype(jnp.int16)
    return match(places, wanted)


def counts_t(columns, first, entries):
    degree, rows = entries.shape
    places = (lax.broadcasted_iota(jnp.int32, (columns, rows), 0) + first).astype(jnp.int16)
    total = match(places, entries[0:1])
    for k in range(1, degree):
        total = total + match(places, entries[k : k + 1])
    return total


def side_swap(entries, rows, size, me):
    swapped = jnp.where(entries < rows + size, entries + size, entries - size)
    rim = (entries >= rows) & (entries < rows + 2 * size)
    return jnp.where(rim & (me % 2 == 1), swapped, entries)


def pair_order(lists, me):
    left, right = lists[0, 0:1], lists[0, 1:2]
    odd = me % 2
    return left + odd * (right - left), right + odd * (left - right)


def by_stage(x, devices):
    return (x % PLANE) * (devices // PLANE) + x // PLANE


def call(body, out_shapes, flops, *args, hbm=0, free=0, hbm_out=0, scratch=(), limit=VMEM_LIMIT):
    shapes = [jax.ShapeDtypeStruct(s, t) for s, t in out_shapes]
    size = sum(a.size * a.dtype.itemsize for a in args)
    size += sum(s.size * s.dtype.itemsize for s in shapes)
    size *= hbm == 0
    places = [pltpu.HBM] * hbm + [pltpu.VMEM] * (len(args) - hbm - free)
    places += [pl.ANY] * free
    out_places = [pltpu.HBM] * hbm_out + [pltpu.VMEM] * (len(shapes) - hbm_out)
    kept = len(args) - free
    inner = body if free == 0 else lambda *refs: body(*refs[:kept], *refs[len(args) :])
    return pl.pallas_call(
        inner,
        out_shape=shapes,
        in_specs=[pl.BlockSpec(memory_space=place) for place in places],
        out_specs=[pl.BlockSpec(memory_space=place) for place in out_places],
        scratch_shapes=list(scratch),
        compiler_params=pltpu.CompilerParams(vmem_limit_bytes=limit),
        cost_estimate=pl.CostEstimate(flops=flops, bytes_accessed=size, transcendentals=0),
    )(*args)


def copies_of(arrays):
    return [pltpu.VMEM(a.shape, a.dtype) for a in arrays]


def fetch(sources, targets, sems):
    copies = [pltpu.make_async_copy(s, t, sems.at[i]) for i, (s, t) in enumerate(zip(sources, targets))]
    for copy in copies:
        copy.start()
    return copies


def row_chunks(rows):
    step = rows // CHUNKS
    return [pl.ds(i * step, step) for i in range(CHUNKS)]


def grid_send(latent, lists, outer, inner, values, wanted, rows, sems):
    parts = row_chunks(latent.shape[0])
    copies = fetch([lists] + [latent.at[part] for part in parts], [wanted] + [values.at[part] for part in parts], sems)
    size = outer.shape[0]
    step = latent.shape[0] // CHUNKS
    copies[0].wait()
    listed = jnp.concatenate(pair_order(wanted, lax.axis_index("dom")), axis=1)
    chosen = pick(latent.shape[0], listed)
    total = 0.0
    for i, part in enumerate(parts):
        copies[i + 1].wait()
        total += t_mm(chosen[i * step : (i + 1) * step], values[part])
    rows[...] = total.astype(BF)
    sides = [rows.at[pl.ds(0, size)], rows.at[pl.ds(size, size)]]
    for copy in fetch(sides, [outer, inner], sems):
        copy.wait()


def encoder_local(entries, weight, latent, mesh, near, grid_own_t, grid_rim_t, slope, *, size):
    me = lax.axis_index("dom")
    rows = latent.shape[0]
    columns = side_swap(entries[...], rows, size, me)
    own = counts_t(rows, 0, columns)
    grid_own_t[...] = own
    grid_rim_t[...] = counts_t(2 * size, rows, columns)
    message, gradient = silu_pair(mm(latent[...], weight[...]))
    slope[...] = gradient.astype(BF)
    near[...] = mesh[...].astype(F32) + t_mm(own, message.astype(BF))


def list_tables(me, lists, far_lists, send, receive):
    rows = send.shape[0]
    size = lists.shape[2]
    cap, devices = far_lists.shape
    outer, inner = pair_order(lists, me)
    rim = [pick(rows, outer), pick(rows, inner)]
    for k in range(2):
        send[:, k * size : (k + 1) * size] = rim[k]
        receive[:, k * size : (k + 1) * size] = rim[k]
    partner = lax.broadcasted_iota(jnp.int32, (devices, devices * cap), 0)
    place = lax.broadcasted_iota(jnp.int32, (devices, devices * cap), 1)
    if devices == STAGED:
        x = partner ^ me
        send_place, receive_place = x * cap, by_stage(x, devices) * cap
    else:
        send_place, receive_place = partner * cap, partner * cap
    send_far = jnp.zeros((rows, devices * cap), F32)
    receive_far = jnp.zeros((rows, devices * cap), F32)
    for j in range(cap):
        chosen = pick(rows, far_lists[j : j + 1])
        send_far += mm(chosen, (place == send_place + j).astype(F32).astype(BF))
        receive_far += mm(chosen, (place == receive_place + j).astype(F32).astype(BF))
    send[:, 2 * size :] = send_far.astype(BF)
    receive[:, 2 * size :] = receive_far.astype(BF)


def mesh_tables(me, entries, own_t, forth_t, back_t, size, devices):
    rows = own_t.shape[0]
    slots = forth_t.shape[0] - 2 * size
    cap = slots // devices
    columns = side_swap(entries[...], rows, size, me)
    own_t[...] = counts_t(rows, 0, columns)
    rim = counts_t(2 * size, rows, columns)
    forth_t[: 2 * size] = rim
    back_t[: 2 * size] = rim
    far = jnp.maximum(columns - rows - 2 * size, 0)
    partner, slot = far // cap, far % cap
    if devices == STAGED:
        partner = partner ^ me
        send_place, receive_place = partner * cap + slot, by_stage(partner, devices) * cap + slot
    else:
        send_place, receive_place = far, far
    is_far = columns >= rows + 2 * size
    forth_t[2 * size :] = counts_t(slots, 0, jnp.where(is_far, receive_place, -1))
    back_t[2 * size :] = counts_t(slots, 0, jnp.where(is_far, send_place, -1))


def decoder_back(entries, cotangent, own_t, rim_t, near, outer, inner):
    me = lax.axis_index("dom")
    rows = near.shape[0]
    size = outer.shape[0]
    columns = side_swap(entries[...], rows, size, me)
    own = counts_t(rows, 0, columns)
    side = counts_t(2 * size, rows, columns)
    own_t[...] = own
    rim_t[...] = side
    grads = cotangent[...]
    near[...] = mm(own, grads)
    back = mm(side, grads).astype(BF)
    outer[...] = back[:size]
    inner[...] = back[size:]


def emit(outs, rows, size, extra=None):
    rows = rows.astype(BF)
    for k in range(2):
        outs[k][:size] = rows[k * size : (k + 1) * size]
        if extra is not None:
            outs[k][size:] = extra[k]
    far = rows[2 * size :]
    block = far.shape[0] // (len(outs) - 2)
    for m, out in enumerate(outs[2:]):
        out[...] = far[m * block : (m + 1) * block]


def arrived(ins, size):
    outer, inner = ins[:2]
    parts = [outer[:size], inner[:size]]
    if len(ins) > 3:
        third, second, own = ins[2:]
        parts += [own[...], inner[inner.shape[0] - own.shape[0] :], second[...], third[...]]
    else:
        parts += [ref[...] for ref in ins[2:]]
    return jnp.concatenate(parts, axis=0)


def shuffle(inner, own, *refs):
    columns = STAGED // PLANE
    parts = [own[...]] + [ref[...] for ref in refs[: columns - 1][::-1]]
    rows = jnp.concatenate(parts, axis=0)
    outs = refs[columns - 1 :]
    count = rows.shape[0]
    cap = count // STAGED
    target = lax.broadcasted_iota(jnp.int32, (count, count), 0)
    source = lax.broadcasted_iota(jnp.int32, (count, count), 1)
    place, slot = target // cap, target % cap
    wanted = ((place % columns) * PLANE + place // columns) * cap + slot
    moved = mm((source == wanted).astype(F32).astype(BF), rows).astype(BF)
    block = columns * cap
    used = inner.shape[0]
    outs[1][:used] = inner[...]
    outs[1][used:] = moved[block : 2 * block]
    for k in (0, 2, 3):
        outs[k][...] = moved[k * block : (k + 1) * block]


def tables(entries, lists, far_lists, own_t, forth_t, back_t, send, receive, *, size, devices):
    me = lax.axis_index("dom")
    mesh_tables(me, entries, own_t, forth_t, back_t, size, devices)
    list_tables(me, lists, far_lists, send, receive)


def layer_local(hidden, own_t, weight, near, slope, *, layer, scale):
    state = hidden[...]
    value, gradient = silu_pair(mm(state, weight[layer]))
    slope[...] = gradient
    near[...] = state.astype(F32) + scale * t_mm(own_t[...], value.astype(BF))


def back_local(own_t, grad, near):
    near[...] = mm(own_t[...], grad[...])


def chosen_messages(send, state, weight):
    return silu_pair(mm(t_mm(send[...], state).astype(BF), weight))[0]


def first_hidden(near, rim_t, outer_in, inner_in, encoder, weight, send, hidden, *outs, size):
    incoming = silu_pair(mm(arrived([outer_in, inner_in], outer_in.shape[0]), encoder[...]))[0].astype(BF)
    state = (near[...] + t_mm(rim_t[...], incoming)).astype(BF)
    hidden[...] = state
    emit(outs, chosen_messages(send, state, weight[0]), size)


def next_hidden(near, forth_t, weight, send, outer_extra, inner_extra, *refs, ins, layer, scale, size):
    rows = arrived(refs[:ins], size)
    state = (near[...] + scale * t_mm(forth_t[...], rows)).astype(BF)
    refs[ins][...] = state
    emit(refs[ins + 1 :], chosen_messages(send, state, weight[layer]), size, (outer_extra[...], inner_extra[...]))


def turn(near, forth_t, weight, send, receive, back_t, back_near, *refs, ins, scale, size):
    rows = arrived(refs[:ins], size)
    message, grad = refs[ins : ins + 2]
    state = (near[...] + scale * t_mm(forth_t[...], rows)).astype(BF)
    value, gradient = silu_pair(mm(state, weight[...]))
    value = value.astype(BF)
    message[...] = value
    returned = jnp.concatenate([refs[0][size : 2 * size], refs[1][size : 2 * size]], axis=0)
    back = back_near[...] + mm(receive[:, : 2 * size], returned)
    change = mm_t((back * gradient).astype(BF), weight[...]).astype(BF)
    grad[...] = change
    rim = t_mm(send[:, : 2 * size], value).astype(BF)
    emit(refs[ins + 2 :], mm(back_t[...], change), size, (rim[:size], rim[size:]))


def layer_back(near, receive, rows, slope, weight, grad, scale):
    total = near[...] + mm(receive[...], rows)
    change = (total * scale * slope[...]).astype(BF)
    return (grad[...].astype(F32) + mm_t(change, weight)).astype(BF)


def middle_back(near, receive, slope, weight, grad, back_t, *refs, ins, layer, scale, size):
    rows = arrived(refs[:ins], size)
    change = layer_back(near, receive, rows, slope, weight[layer], grad, scale)
    refs[ins][...] = change
    emit(refs[ins + 1 :], mm(back_t[...], change), size)


def grid_base(own_t, grad, slope, weight, cotangent, base):
    change = (mm(own_t[...], grad[...]) * slope[...].astype(F32)).astype(BF)
    base[...] = cotangent[...].astype(F32) + mm_t(change, weight[...])


def last_even(near, receive, slope, weight, grad, grid_rim_t, own_t, grid_slope, grid_weight, cotangent, *refs, ins, scale):
    new_grad, outer, inner, base = refs[-4:]
    last_back(near, receive, slope, weight, grad, grid_rim_t, *refs[:-1], ins=ins, scale=scale, parity=0)

    @pl.when(lax.axis_index("dom") % 2 == 0)
    def _():
        grid_base(own_t, new_grad, grid_slope, grid_weight, cotangent, base)


def last_back(near, receive, slope, weight, grad, grid_rim_t, *refs, ins, scale, parity):
    new_grad, outer, inner = refs[-3:]
    mine = lax.axis_index("dom") % 2 == parity

    @pl.when(mine)
    def _():
        rows = arrived(refs[:ins], refs[0].shape[0])
        change = layer_back(near, receive, rows, slope, weight[0], grad, scale)
        new_grad[...] = change
        back = mm(grid_rim_t[...], change).astype(BF)
        outer[...] = back[: outer.shape[0]]
        inner[...] = back[outer.shape[0] :]

    if len(refs) > ins + 3:

        @pl.when(jnp.logical_not(mine))
        def _():
            new_grad[...] = refs[ins][...]
            inner[...] = refs[ins + 1][...]


def decode_own(latent, own_t, message, base):
    base[...] = latent[...].astype(F32) + t_mm(own_t[...], message[...])


def decode_rim(base, rim_t, outer_in, inner_in, output, token):
    size = outer_in.shape[0] // 2
    incoming = jnp.concatenate([outer_in[size:], inner_in[size : 2 * size]], axis=0)
    output[...] = (base[...] + t_mm(rim_t[...], incoming)).astype(BF)
    token[...] = jnp.zeros(token.shape, F32)


def halo_tables(lists, slope, table, slope_rows):
    size = lists.shape[2]
    for k, wanted in enumerate(pair_order(lists, lax.axis_index("dom"))):
        table[:, k * size : (k + 1) * size] = pick(table.shape[0], wanted)
    slope_rows[...] = t_mm(table[...], slope[...])


def grid_local(own_t, grad, slope, weight, cotangent, base, mesh_grad):
    mesh_grad[...] = grad[...]

    @pl.when(lax.axis_index("dom") % 2 == 1)
    def _():
        grid_base(own_t, grad, slope, weight, cotangent, base)


def grid_back(even_base, odd_base, table, slope_rows, weight, even_in, odd_in, inner_in, output, staging, sems):
    even = lax.axis_index("dom") % 2 == 0
    outer_in = jnp.where(even, even_in[...], odd_in[...])
    returned = jnp.concatenate([outer_in, inner_in[...]], axis=0).astype(F32)
    change = mm_t((returned * slope_rows[...]).astype(BF), weight[...]).astype(BF)
    copies = []
    for i, part in enumerate(row_chunks(table.shape[0])):
        base = jnp.where(even, even_base[part], odd_base[part])
        staging[part] = (base + mm(table[part], change)).astype(BF)
        copies.append(pltpu.make_async_copy(staging.at[part], output.at[part], sems.at[i]))
        copies[-1].start()
    for copy in copies:
        copy.wait()


def touch(_, token):
    token[...] = jnp.zeros(token.shape, F32)


def toggle(value, bits):
    peers = lax.axis_size("dom")
    return lax.ppermute(value, "dom", [(i, i ^ bits) for i in range(peers)])


def across(value):
    peers = lax.axis_size("dom")
    pairs = [(i, (i + 1) % peers if i % 2 else (i - 1) % peers) for i in range(peers)]
    return lax.ppermute(value, "dom", pairs)


def across_one_way(value, parity):
    peers = lax.axis_size("dom")
    step = 1 if parity else -1
    return lax.ppermute(value, "dom", [(i, (i + step) % peers) for i in range(peers) if i % 2 == parity])


def exchange(outs, cap):
    width = outs[0].shape[1]
    if len(outs) == 3:
        outer, inner, far = outs
        peers = lax.axis_size("dom")
        blocks = far.reshape(peers, cap, width)
        blocks = lax.all_to_all(blocks, "dom", split_axis=0, concat_axis=0, tiled=True)
        return [across(outer), toggle(inner, 1), blocks.reshape(-1, width)]
    outer, inner, own, *rest = outs
    columns = STAGED // PLANE
    moved = [toggle(rest[m - 1], m * PLANE) for m in reversed(range(1, columns))]
    outer_in = across(outer)
    block = columns * cap
    blocks = call(
        shuffle,
        [((block, width), BF), ((inner.shape[0] + block, width), BF), ((block, width), BF), ((block, width), BF)],
        2 * (STAGED * cap) ** 2 * width,
        inner, own, *moved,
    )
    return [outer_in, toggle(blocks[1], 1), toggle(blocks[3], 3), toggle(blocks[2], 2), blocks[0]]


def on_device(
    grid_latent,
    mesh_latent,
    encoder_weight,
    processor_weights,
    decoder_weight,
    cotangent,
    grid_halo_rows,
    encoder_neighbours,
    halo_rows,
    far_sources,
    mesh_neighbours,
    decoder_neighbours,
):
    devices = lax.axis_size("dom")
    grid_rows, width = grid_latent.shape
    mesh_rows = mesh_latent.shape[0]
    ghalo = grid_halo_rows.shape[2]
    halo = halo_rows.shape[2]
    cap = far_sources.shape[2]
    slots = devices * cap
    listed = 2 * halo + slots
    scale = 1.0 / mesh_neighbours.shape[1]

    def square(rows, depth):
        return 2 * rows * depth * width

    def sends(per_side):
        stages = STAGED // PLANE if devices == STAGED else 1
        return [((per_side, width), BF)] * 2 + [((slots // stages, width), BF)] * stages

    state = ((mesh_rows, width), BF)
    total = ((mesh_rows, width), F32)
    rim = ((halo, width), BF)
    grid_rim = ((ghalo, width), BF)
    step = 3 * square(mesh_rows, width)

    outer, inner = call(
        grid_send,
        [grid_rim, grid_rim],
        64 * square(grid_rows, width),
        grid_latent, grid_halo_rows,
        hbm=2, hbm_out=2, limit=FIRST_LIMIT,
        scratch=copies_of([grid_latent, grid_halo_rows])
        + [pltpu.VMEM((2 * ghalo, width), BF), pltpu.SemaphoreType.DMA((CHUNKS + 1,))],
    )
    outer_in, inner_in = across(outer), toggle(inner, 1)

    own_t, forth_t, back_t, send, receive = call(
        functools.partial(tables, size=halo, devices=devices),
        [((mesh_rows, mesh_rows), BF)] + [((listed, mesh_rows), BF)] * 2 + [((mesh_rows, listed), BF)] * 2,
        64 * square(mesh_rows, mesh_rows),
        mesh_neighbours.T, halo_rows, far_sources[0].T,
    )
    _, latent, weight, mesh = lax.optimization_barrier((inner, grid_latent, encoder_weight, mesh_latent))
    near, grid_own_t, grid_rim_t, grid_slope = call(
        functools.partial(encoder_local, size=ghalo),
        [total, ((grid_rows, mesh_rows), BF), ((2 * ghalo, mesh_rows), BF), ((grid_rows, width), BF)],
        4 * square(grid_rows, width),
        encoder_neighbours.T, weight, latent, mesh,
    )

    hidden, *outs = call(
        functools.partial(first_hidden, size=halo),
        [state] + sends(halo),
        step,
        near, grid_rim_t, outer_in, inner_in, encoder_weight, processor_weights, send,
    )
    ins = exchange(outs, cap)
    near, slope_0 = call(
        functools.partial(layer_local, layer=0, scale=scale),
        [total, total],
        6 * square(mesh_rows, mesh_rows),
        hidden, own_t, processor_weights, ins[-1],
        free=1,
    )
    decoder_own_t, decoder_rim_t, decoder_near, outer_extra, inner_extra = call(
        decoder_back,
        [((mesh_rows, grid_rows), BF), ((2 * halo, grid_rows), BF), total, rim, rim],
        square(grid_rows, mesh_rows),
        decoder_neighbours.T, cotangent, ins[-1],
        free=1,
    )

    hidden, *outs = call(
        functools.partial(next_hidden, ins=len(ins), layer=1, scale=scale, size=halo),
        [state] + sends(2 * halo),
        step,
        near, forth_t, processor_weights, send, outer_extra, inner_extra, *ins,
    )
    ins = exchange(outs, cap)
    near, slope_1 = call(
        functools.partial(layer_local, layer=1, scale=scale),
        [total, total],
        6 * square(mesh_rows, mesh_rows),
        hidden, own_t, processor_weights, ins[-1],
        free=1,
    )

    message, grad, *outs = call(
        functools.partial(turn, ins=len(ins), scale=scale, size=halo),
        [state, state] + sends(2 * halo),
        2 * step,
        near, forth_t, decoder_weight, send, receive, back_t, decoder_near, *ins,
    )
    ins = exchange(outs, cap)
    (near,) = call(back_local, [total], 6 * square(mesh_rows, mesh_rows), own_t, grad)

    outer_decoder, inner_decoder = ins[:2]
    (near,) = call(back_local, [total], 6 * square(mesh_rows, mesh_rows), own_t, grad, ins[-1], free=1)
    (base,) = call(
        decode_own,
        [((grid_rows, width), F32)],
        square(grid_rows, mesh_rows),
        grid_latent, decoder_own_t, message, ins[-1],
        free=1,
    )

    table, slope_rows = call(
        halo_tables,
        [((grid_rows, 2 * ghalo), BF), ((2 * ghalo, width), F32)],
        square(grid_rows, 2 * ghalo),
        grid_halo_rows, grid_slope, ins[-1],
        free=1,
    )

    grad, *outs = call(
        functools.partial(middle_back, ins=len(ins), layer=1, scale=scale, size=halo),
        [state] + sends(halo),
        step,
        near, receive, slope_1, processor_weights, grad, back_t, *ins, base, slope_rows,
        free=2,
    )
    ins = exchange(outs, cap)
    (near,) = call(back_local, [total], 6 * square(mesh_rows, mesh_rows), own_t, grad, ins[-1], free=1)
    output, token = call(
        decode_rim,
        [((grid_rows, width), BF), ((8, 128), F32)],
        square(grid_rows, 2 * halo),
        base, decoder_rim_t, outer_decoder, inner_decoder, ins[-1],
        free=1,
    )

    sides = [state, grid_rim, grid_rim]
    last = functools.partial(last_back, ins=len(ins), scale=scale)
    operands = (near, receive, slope_0, processor_weights, grad, grid_rim_t, *ins)
    odd_grad, outer, odd_inner = call(
        functools.partial(last, parity=1), sides, step, *operands, token, free=1
    )
    even_in = across_one_way(outer, 1)
    grid_shape = ((grid_rows, width), F32)
    grid_operands = (grid_slope, encoder_weight, cotangent)
    grad, outer, inner, even_base = call(
        functools.partial(last_even, ins=len(ins), scale=scale),
        sides + [grid_shape],
        step + 2 * square(grid_rows, width),
        *operands[:6], grid_own_t, *grid_operands, *ins, odd_grad, odd_inner,
    )
    odd_in, inner_in = across_one_way(outer, 0), toggle(inner, 1)
    odd_base, mesh_grad = call(
        grid_local,
        [grid_shape, state],
        square(grid_rows, width),
        grid_own_t, grad, *grid_operands,
    )
    (token,) = call(touch, [((8, 128), F32)], 1 * step, even_in)
    (grid_grad,) = call(
        grid_back,
        [((grid_rows, width), BF)],
        square(grid_rows, 4 * ghalo),
        even_base, odd_base, table, slope_rows, encoder_weight, even_in, odd_in, inner_in, token,
        free=1, hbm_out=1,
        scratch=[pltpu.VMEM((grid_rows, width), BF), pltpu.SemaphoreType.DMA((CHUNKS,))],
    )
    return (output, grid_grad, mesh_grad)


def solution(mesh):
    in_specs = (
        P(("groups", "dom"), None),
        P(("groups", "dom"), None),
        P(),
        P(),
        P(),
        P(("groups", "dom"), None),
        P("dom", None, None),
        P("dom", None),
        P("dom", None, None),
        P("dom", None, None),
        P("dom", None),
        P("dom", None),
    )
    out_specs = (P(("groups", "dom"), None), P(("groups", "dom"), None), P(("groups", "dom"), None))
    return jax.shard_map(
        on_device, mesh=mesh, in_specs=in_specs, out_specs=out_specs, check_vma=False
    )
```

```python
import functools

import jax
import jax.numpy as jnp
from jax import lax
from jax.experimental import pallas as pl
from jax.experimental.pallas import tpu as pltpu
from jax.sharding import PartitionSpec as P

BF = jnp.bfloat16
F32 = jnp.float32
VMEM_LIMIT = 24 * 1024 * 1024
FIRST_LIMIT = 60 * 1024 * 1024
PLANE = 4
STAGED = 16
CHUNKS = 4


def mm(a, b):
    return jnp.dot(a, b, preferred_element_type=F32)


def mm_t(a, b):
    return lax.dot_general(a, b, (((1,), (1,)), ((), ())), preferred_element_type=F32)


def t_mm(a, b):
    return lax.dot_general(a, b, (((0,), (0,)), ((), ())), preferred_element_type=F32)


def silu_pair(value):
    sigma = 0.5 + 0.5 * jnp.tanh(0.5 * value)
    message = value * sigma
    return message, sigma + message * (1.0 - sigma)


def match(places, wanted):
    shape = places.shape
    wanted = jnp.broadcast_to(wanted, shape).astype(jnp.int16)
    return jnp.where(places == wanted, jnp.ones(shape, BF), jnp.zeros(shape, BF))


def pick(rows, wanted):
    places = lax.broadcasted_iota(jnp.int32, (rows, wanted.shape[1]), 0).astype(jnp.int16)
    return match(places, wanted)


def counts_t(columns, first, entries):
    degree, rows = entries.shape
    places = (lax.broadcasted_iota(jnp.int32, (columns, rows), 0) + first).astype(jnp.int16)
    total = match(places, entries[0:1])
    for k in range(1, degree):
        total = total + match(places, entries[k : k + 1])
    return total


def side_swap(entries, rows, size, me):
    swapped = jnp.where(entries < rows + size, entries + size, entries - size)
    rim = (entries >= rows) & (entries < rows + 2 * size)
    return jnp.where(rim & (me % 2 == 1), swapped, entries)


def pair_order(lists, me):
    left, right = lists[0, 0:1], lists[0, 1:2]
    odd = me % 2
    return left + odd * (right - left), right + odd * (left - right)


def by_stage(x, devices):
    return (x % PLANE) * (devices // PLANE) + x // PLANE


def call(body, out_shapes, flops, *args, hbm=0, free=0, hbm_out=0, scratch=(), limit=VMEM_LIMIT):
    shapes = [jax.ShapeDtypeStruct(s, t) for s, t in out_shapes]
    size = sum(a.size * a.dtype.itemsize for a in args)
    size += sum(s.size * s.dtype.itemsize for s in shapes)
    size *= hbm == 0
    places = [pltpu.HBM] * hbm + [pltpu.VMEM] * (len(args) - hbm - free)
    places += [pl.ANY] * free
    out_places = [pltpu.HBM] * hbm_out + [pltpu.VMEM] * (len(shapes) - hbm_out)
    kept = len(args) - free
    inner = body if free == 0 else lambda *refs: body(*refs[:kept], *refs[len(args) :])
    return pl.pallas_call(
        inner,
        out_shape=shapes,
        in_specs=[pl.BlockSpec(memory_space=place) for place in places],
        out_specs=[pl.BlockSpec(memory_space=place) for place in out_places],
        scratch_shapes=list(scratch),
        compiler_params=pltpu.CompilerParams(vmem_limit_bytes=limit),
        cost_estimate=pl.CostEstimate(flops=flops, bytes_accessed=size, transcendentals=0),
    )(*args)


def copies_of(arrays):
    return [pltpu.VMEM(a.shape, a.dtype) for a in arrays]


def fetch(sources, targets, sems):
    copies = [pltpu.make_async_copy(s, t, sems.at[i]) for i, (s, t) in enumerate(zip(sources, targets))]
    for copy in copies:
        copy.start()
    return copies


def row_chunks(rows):
    step = rows // CHUNKS
    return [pl.ds(i * step, step) for i in range(CHUNKS)]


def grid_send(latent, lists, outer, inner, values, wanted, rows, sems):
    parts = row_chunks(latent.shape[0])
    copies = fetch([lists] + [latent.at[part] for part in parts], [wanted] + [values.at[part] for part in parts], sems)
    size = outer.shape[0]
    step = latent.shape[0] // CHUNKS
    copies[0].wait()
    listed = jnp.concatenate(pair_order(wanted, lax.axis_index("dom")), axis=1)
    chosen = pick(latent.shape[0], listed)
    total = 0.0
    for i, part in enumerate(parts):
        copies[i + 1].wait()
        total += t_mm(chosen[i * step : (i + 1) * step], values[part])
    rows[...] = total.astype(BF)
    sides = [rows.at[pl.ds(0, size)], rows.at[pl.ds(size, size)]]
    for copy in fetch(sides, [outer, inner], sems):
        copy.wait()


def encoder_local(entries, weight, latent, mesh, near, grid_own_t, grid_rim_t, slope, *, size):
    me = lax.axis_index("dom")
    rows = latent.shape[0]
    columns = side_swap(entries[...], rows, size, me)
    own = counts_t(rows, 0, columns)
    grid_own_t[...] = own
    grid_rim_t[...] = counts_t(2 * size, rows, columns)
    message, gradient = silu_pair(mm(latent[...], weight[...]))
    slope[...] = gradient.astype(BF)
    near[...] = mesh[...].astype(F32) + t_mm(own, message.astype(BF))


def list_tables(me, lists, far_lists, send, receive):
    rows = send.shape[0]
    size = lists.shape[2]
    cap, devices = far_lists.shape
    outer, inner = pair_order(lists, me)
    rim = [pick(rows, outer), pick(rows, inner)]
    for k in range(2):
        send[:, k * size : (k + 1) * size] = rim[k]
        receive[:, k * size : (k + 1) * size] = rim[k]
    partner = lax.broadcasted_iota(jnp.int32, (devices, devices * cap), 0)
    place = lax.broadcasted_iota(jnp.int32, (devices, devices * cap), 1)
    if devices == STAGED:
        x = partner ^ me
        send_place, receive_place = x * cap, by_stage(x, devices) * cap
    else:
        send_place, receive_place = partner * cap, partner * cap
    send_far = jnp.zeros((rows, devices * cap), F32)
    receive_far = jnp.zeros((rows, devices * cap), F32)
    for j in range(cap):
        chosen = pick(rows, far_lists[j : j + 1])
        send_far += mm(chosen, (place == send_place + j).astype(F32).astype(BF))
        receive_far += mm(chosen, (place == receive_place + j).astype(F32).astype(BF))
    send[:, 2 * size :] = send_far.astype(BF)
    receive[:, 2 * size :] = receive_far.astype(BF)


def mesh_tables(me, entries, own_t, forth_t, back_t, size, devices):
    rows = own_t.shape[0]
    slots = forth_t.shape[0] - 2 * size
    cap = slots // devices
    columns = side_swap(entries[...], rows, size, me)
    own_t[...] = counts_t(rows, 0, columns)
    rim = counts_t(2 * size, rows, columns)
    forth_t[: 2 * size] = rim
    back_t[: 2 * size] = rim
    far = jnp.maximum(columns - rows - 2 * size, 0)
    partner, slot = far // cap, far % cap
    if devices == STAGED:
        partner = partner ^ me
        send_place, receive_place = partner * cap + slot, by_stage(partner, devices) * cap + slot
    else:
        send_place, receive_place = far, far
    is_far = columns >= rows + 2 * size
    forth_t[2 * size :] = counts_t(slots, 0, jnp.where(is_far, receive_place, -1))
    back_t[2 * size :] = counts_t(slots, 0, jnp.where(is_far, send_place, -1))


def decoder_back(entries, cotangent, own_t, rim_t, near, outer, inner):
    me = lax.axis_index("dom")
    rows = near.shape[0]
    size = outer.shape[0]
    columns = side_swap(entries[...], rows, size, me)
    own = counts_t(rows, 0, columns)
    side = counts_t(2 * size, rows, columns)
    own_t[...] = own
    rim_t[...] = side
    grads = cotangent[...]
    near[...] = mm(own, grads)
    back = mm(side, grads).astype(BF)
    outer[...] = back[:size]
    inner[...] = back[size:]


def emit(outs, rows, size, extra=None):
    rows = rows.astype(BF)
    for k in range(2):
        outs[k][:size] = rows[k * size : (k + 1) * size]
        if extra is not None:
            outs[k][size:] = extra[k]
    far = rows[2 * size :]
    block = far.shape[0] // (len(outs) - 2)
    for m, out in enumerate(outs[2:]):
        out[...] = far[m * block : (m + 1) * block]


def arrived(ins, size):
    outer, inner = ins[:2]
    parts = [outer[:size], inner[:size]]
    if len(ins) > 3:
        third, second, own = ins[2:]
        parts += [own[...], inner[inner.shape[0] - own.shape[0] :], second[...], third[...]]
    else:
        parts += [ref[...] for ref in ins[2:]]
    return jnp.concatenate(parts, axis=0)


def shuffle(inner, own, *refs):
    columns = STAGED // PLANE
    parts = [own[...]] + [ref[...] for ref in refs[: columns - 1][::-1]]
    rows = jnp.concatenate(parts, axis=0)
    outs = refs[columns - 1 :]
    count = rows.shape[0]
    cap = count // STAGED
    target = lax.broadcasted_iota(jnp.int32, (count, count), 0)
    source = lax.broadcasted_iota(jnp.int32, (count, count), 1)
    place, slot = target // cap, target % cap
    wanted = ((place % columns) * PLANE + place // columns) * cap + slot
    moved = mm((source == wanted).astype(F32).astype(BF), rows).astype(BF)
    block = columns * cap
    used = inner.shape[0]
    outs[1][:used] = inner[...]
    outs[1][used:] = moved[block : 2 * block]
    for k in (0, 2, 3):
        outs[k][...] = moved[k * block : (k + 1) * block]


def tables(entries, lists, far_lists, own_t, forth_t, back_t, send, receive, *, size, devices):
    me = lax.axis_index("dom")
    mesh_tables(me, entries, own_t, forth_t, back_t, size, devices)
    list_tables(me, lists, far_lists, send, receive)


def layer_local(hidden, own_t, weight, near, slope, *, layer, scale):
    state = hidden[...]
    value, gradient = silu_pair(mm(state, weight[layer]))
    slope[...] = gradient
    near[...] = state.astype(F32) + scale * t_mm(own_t[...], value.astype(BF))


def chosen_messages(send, state, weight):
    return silu_pair(mm(t_mm(send[...], state).astype(BF), weight))[0]


def first_hidden(near, rim_t, outer_in, inner_in, encoder, weight, send, hidden, *outs, size):
    incoming = silu_pair(mm(arrived([outer_in, inner_in], outer_in.shape[0]), encoder[...]))[0].astype(BF)
    state = (near[...] + t_mm(rim_t[...], incoming)).astype(BF)
    hidden[...] = state
    emit(outs, chosen_messages(send, state, weight[0]), size)


def next_hidden(near, forth_t, weight, send, outer_extra, inner_extra, *refs, ins, layer, scale, size):
    rows = arrived(refs[:ins], size)
    state = (near[...] + scale * t_mm(forth_t[...], rows)).astype(BF)
    refs[ins][...] = state
    emit(refs[ins + 1 :], chosen_messages(send, state, weight[layer]), size, (outer_extra[...], inner_extra[...]))


def turn(near, forth_t, weight, send, receive, back_t, back_near, *refs, ins, scale, size):
    rows = arrived(refs[:ins], size)
    message, grad = refs[ins : ins + 2]
    state = (near[...] + scale * t_mm(forth_t[...], rows)).astype(BF)
    value, gradient = silu_pair(mm(state, weight[...]))
    value = value.astype(BF)
    message[...] = value
    returned = jnp.concatenate([refs[0][size : 2 * size], refs[1][size : 2 * size]], axis=0)
    back = back_near[...] + mm(receive[:, : 2 * size], returned)
    change = (back * gradient).astype(BF)
    grad[...] = change
    rim = t_mm(send[:, : 2 * size], value).astype(BF)
    rows = mm_t(mm(back_t[...], change).astype(BF), weight[...])
    emit(refs[ins + 2 :], rows, size, (rim[:size], rim[size:]))


def turn_local(own_t, change, weight, near, grad):
    whole = mm_t(change[...], weight[...]).astype(BF)
    grad[...] = whole
    near[...] = mm(own_t[...], whole)


def layer_change(near, receive, rows, slope, scale):
    total = near[...] + mm(receive[...], rows)
    return (total * scale * slope[...]).astype(BF)


def middle_back(near, receive, slope, weight, grad, back_t, *refs, ins, layer, scale, size):
    rows = arrived(refs[:ins], size)
    change = mm_t(layer_change(near, receive, rows, slope, scale), weight[layer])
    change = (grad[...].astype(F32) + change).astype(BF)
    refs[ins][...] = change
    emit(refs[ins + 1 :], mm(back_t[...], change), size)


def last_local(own_t, grad, grid_rim_t, near, rim_near):
    near[...] = mm(own_t[...], grad[...])
    rim_near[...] = mm(grid_rim_t[...], grad[...])


def last_back(near, rim_near, receive, slope, weight, grid_rim_t, *refs, ins, scale):
    kept, outer, inner = refs[ins:]
    rows = arrived(refs[:ins], refs[0].shape[0])
    change = layer_change(near, receive, rows, slope, scale)
    kept[...] = change
    back = rim_near[...] + mm_t(mm(grid_rim_t[...], change).astype(BF), weight[0])
    back = back.astype(BF)
    outer[...] = back[: outer.shape[0]]
    inner[...] = back[outer.shape[0] :]


def decode_own(latent, own_t, message, base):
    base[...] = latent[...].astype(F32) + t_mm(own_t[...], message[...])


def decode_rim(base, rim_t, outer_in, inner_in, output, token):
    size = outer_in.shape[0] // 2
    incoming = jnp.concatenate([outer_in[size:], inner_in[size : 2 * size]], axis=0)
    output[...] = (base[...] + t_mm(rim_t[...], incoming)).astype(BF)
    token[...] = jnp.zeros(token.shape, F32)


def halo_tables(lists, slope, table, slope_rows):
    size = lists.shape[2]
    for k, wanted in enumerate(pair_order(lists, lax.axis_index("dom"))):
        table[:, k * size : (k + 1) * size] = pick(table.shape[0], wanted)
    slope_rows[...] = t_mm(table[...], slope[...])


def grid_local(own_t, grad, change, mesh_weight, slope, weight, cotangent, base, mesh_grad):
    whole = (grad[...].astype(F32) + mm_t(change[...], mesh_weight[0])).astype(BF)
    mesh_grad[...] = whole
    spread = (mm(own_t[...], whole) * slope[...].astype(F32)).astype(BF)
    base[...] = cotangent[...].astype(F32) + mm_t(spread, weight[...])


def grid_back(base, table, slope_rows, weight, outer_in, inner_in, output, staging, sems):
    returned = jnp.concatenate([outer_in[...], inner_in[...]], axis=0).astype(F32)
    returned = (returned * slope_rows[...]).astype(BF)
    half = weight.shape[0] // 2
    copies = []
    for columns in (pl.ds(0, half), pl.ds(half, half)):
        change = mm_t(returned, weight[columns]).astype(BF)
        for rows in row_chunks(base.shape[0])[:: CHUNKS // 2]:
            rows = pl.ds(rows.start, base.shape[0] // 2)
            staging[rows, columns] = (base[rows, columns] + mm(table[rows], change)).astype(BF)
            place = (rows, columns)
            copies.append(pltpu.make_async_copy(staging.at[place], output.at[place], sems.at[len(copies)]))
            copies[-1].start()
    for copy in copies:
        copy.wait()


def toggle(value, bits):
    peers = lax.axis_size("dom")
    return lax.ppermute(value, "dom", [(i, i ^ bits) for i in range(peers)])


def across(value):
    peers = lax.axis_size("dom")
    pairs = [(i, (i + 1) % peers if i % 2 else (i - 1) % peers) for i in range(peers)]
    return lax.ppermute(value, "dom", pairs)


def exchange(outs, cap):
    width = outs[0].shape[1]
    if len(outs) == 3:
        outer, inner, far = outs
        peers = lax.axis_size("dom")
        blocks = far.reshape(peers, cap, width)
        blocks = lax.all_to_all(blocks, "dom", split_axis=0, concat_axis=0, tiled=True)
        return [across(outer), toggle(inner, 1), blocks.reshape(-1, width)]
    outer, inner, own, *rest = outs
    columns = STAGED // PLANE
    moved = [toggle(rest[m - 1], m * PLANE) for m in reversed(range(1, columns))]
    outer_in = across(outer)
    block = columns * cap
    blocks = call(
        shuffle,
        [((block, width), BF), ((inner.shape[0] + block, width), BF), ((block, width), BF), ((block, width), BF)],
        2 * (STAGED * cap) ** 2 * width,
        inner, own, *moved,
    )
    return [outer_in, toggle(blocks[1], 1), toggle(blocks[3], 3), toggle(blocks[2], 2), blocks[0]]


def on_device(
    grid_latent,
    mesh_latent,
    encoder_weight,
    processor_weights,
    decoder_weight,
    cotangent,
    grid_halo_rows,
    encoder_neighbours,
    halo_rows,
    far_sources,
    mesh_neighbours,
    decoder_neighbours,
):
    devices = lax.axis_size("dom")
    grid_rows, width = grid_latent.shape
    mesh_rows = mesh_latent.shape[0]
    ghalo = grid_halo_rows.shape[2]
    halo = halo_rows.shape[2]
    cap = far_sources.shape[2]
    slots = devices * cap
    listed = 2 * halo + slots
    scale = 1.0 / mesh_neighbours.shape[1]

    def square(rows, depth):
        return 2 * rows * depth * width

    def sends(per_side):
        stages = STAGED // PLANE if devices == STAGED else 1
        return [((per_side, width), BF)] * 2 + [((slots // stages, width), BF)] * stages

    state = ((mesh_rows, width), BF)
    total = ((mesh_rows, width), F32)
    rim = ((halo, width), BF)
    grid_rim = ((ghalo, width), BF)
    step = 3 * square(mesh_rows, width)

    outer, inner = call(
        grid_send,
        [grid_rim, grid_rim],
        64 * square(grid_rows, width),
        grid_latent, grid_halo_rows,
        hbm=2, hbm_out=2, limit=FIRST_LIMIT,
        scratch=copies_of([grid_latent, grid_halo_rows])
        + [pltpu.VMEM((2 * ghalo, width), BF), pltpu.SemaphoreType.DMA((CHUNKS + 1,))],
    )
    outer_in, inner_in = across(outer), toggle(inner, 1)

    own_t, forth_t, back_t, send, receive = call(
        functools.partial(tables, size=halo, devices=devices),
        [((mesh_rows, mesh_rows), BF)] + [((listed, mesh_rows), BF)] * 2 + [((mesh_rows, listed), BF)] * 2,
        64 * square(mesh_rows, mesh_rows),
        mesh_neighbours.T, halo_rows, far_sources[0].T,
    )
    _, latent, weight, mesh = lax.optimization_barrier((inner, grid_latent, encoder_weight, mesh_latent))
    near, grid_own_t, grid_rim_t, grid_slope = call(
        functools.partial(encoder_local, size=ghalo),
        [total, ((grid_rows, mesh_rows), BF), ((2 * ghalo, mesh_rows), BF), ((grid_rows, width), BF)],
        4 * square(grid_rows, width),
        encoder_neighbours.T, weight, latent, mesh,
    )

    hidden, *outs = call(
        functools.partial(first_hidden, size=halo),
        [state] + sends(halo),
        step,
        near, grid_rim_t, outer_in, inner_in, encoder_weight, processor_weights, send,
    )
    ins = exchange(outs, cap)
    near, slope_0 = call(
        functools.partial(layer_local, layer=0, scale=scale),
        [total, total],
        6 * square(mesh_rows, mesh_rows),
        hidden, own_t, processor_weights, ins[-1],
        free=1,
    )
    decoder_own_t, decoder_rim_t, decoder_near, outer_extra, inner_extra = call(
        decoder_back,
        [((mesh_rows, grid_rows), BF), ((2 * halo, grid_rows), BF), total, rim, rim],
        square(grid_rows, mesh_rows),
        decoder_neighbours.T, cotangent, ins[-1],
        free=1,
    )

    hidden, *outs = call(
        functools.partial(next_hidden, ins=len(ins), layer=1, scale=scale, size=halo),
        [state] + sends(2 * halo),
        step,
        near, forth_t, processor_weights, send, outer_extra, inner_extra, *ins,
    )
    ins = exchange(outs, cap)
    near, slope_1 = call(
        functools.partial(layer_local, layer=1, scale=scale),
        [total, total],
        6 * square(mesh_rows, mesh_rows),
        hidden, own_t, processor_weights, ins[-1],
        free=1,
    )

    message, change, *outs = call(
        functools.partial(turn, ins=len(ins), scale=scale, size=halo),
        [state, state] + sends(2 * halo),
        2 * step,
        near, forth_t, decoder_weight, send, receive, back_t, decoder_near, *ins,
    )
    ins = exchange(outs, cap)
    outer_decoder, inner_decoder = ins[:2]
    near, grad = call(
        turn_local,
        [total, state],
        6 * square(mesh_rows, mesh_rows),
        own_t, change, decoder_weight, ins[-1],
        free=1,
    )
    table, slope_rows = call(
        halo_tables,
        [((grid_rows, 2 * ghalo), BF), ((2 * ghalo, width), F32)],
        square(grid_rows, 2 * ghalo),
        grid_halo_rows, grid_slope, ins[-1],
        free=1,
    )
    (base,) = call(
        decode_own,
        [((grid_rows, width), F32)],
        square(grid_rows, mesh_rows),
        grid_latent, decoder_own_t, message, ins[-1],
        free=1,
    )

    grad, *outs = call(
        functools.partial(middle_back, ins=len(ins), layer=1, scale=scale, size=halo),
        [state] + sends(halo),
        step,
        near, receive, slope_1, processor_weights, grad, back_t, *ins, base, slope_rows,
        free=2,
    )
    ins = exchange(outs, cap)
    near, rim_near = call(
        last_local,
        [total, ((2 * ghalo, width), F32)],
        6 * square(mesh_rows, mesh_rows),
        own_t, grad, grid_rim_t, ins[-1],
        free=1,
    )
    output, token = call(
        decode_rim,
        [((grid_rows, width), BF), ((8, 128), F32)],
        square(grid_rows, 2 * halo),
        base, decoder_rim_t, outer_decoder, inner_decoder, ins[-1],
        free=1,
    )

    change, outer, inner = call(
        functools.partial(last_back, ins=len(ins), scale=scale),
        [state, grid_rim, grid_rim],
        step,
        near, rim_near, receive, slope_0, processor_weights, grid_rim_t, *ins, token,
        free=1,
    )
    outer_in, inner_in = across(outer), toggle(inner, 1)
    base, mesh_grad = call(
        grid_local,
        [((grid_rows, width), F32), state],
        square(mesh_rows, grid_rows) + square(grid_rows, width),
        grid_own_t, grad, change, processor_weights, grid_slope, encoder_weight, cotangent,
    )
    (grid_grad,) = call(
        grid_back,
        [((grid_rows, width), BF)],
        square(grid_rows, 4 * ghalo),
        base, table, slope_rows, encoder_weight, outer_in, inner_in,
        hbm_out=1,
        scratch=[pltpu.VMEM((grid_rows, width), BF), pltpu.SemaphoreType.DMA((CHUNKS,))],
    )
    return (output, grid_grad, mesh_grad)


def solution(mesh):
    in_specs = (
        P(("groups", "dom"), None),
        P(("groups", "dom"), None),
        P(),
        P(),
        P(),
        P(("groups", "dom"), None),
        P("dom", None, None),
        P("dom", None),
        P("dom", None, None),
        P("dom", None, None),
        P("dom", None),
        P("dom", None),
    )
    out_specs = (P(("groups", "dom"), None), P(("groups", "dom"), None), P(("groups", "dom"), None))
    return jax.shard_map(
        on_device, mesh=mesh, in_specs=in_specs, out_specs=out_specs, check_vma=False
    )
```

```python
import functools

import jax
import jax.numpy as jnp
from jax import lax
from jax.experimental import pallas as pl
from jax.experimental.pallas import tpu as pltpu
from jax.sharding import PartitionSpec as P

BF = jnp.bfloat16
F32 = jnp.float32
VMEM_LIMIT = 24 * 1024 * 1024
FIRST_LIMIT = 60 * 1024 * 1024
PLANE = 4
STAGED = 16
CHUNKS = 4
Z_ORDER = (2, 3, 1)


def mm(a, b):
    return jnp.dot(a, b, preferred_element_type=F32)


def mm_t(a, b):
    return lax.dot_general(a, b, (((1,), (1,)), ((), ())), preferred_element_type=F32)


def t_mm(a, b):
    return lax.dot_general(a, b, (((0,), (0,)), ((), ())), preferred_element_type=F32)


def silu_pair(value):
    sigma = 0.5 + 0.5 * jnp.tanh(0.5 * value)
    message = value * sigma
    return message, sigma + message * (1.0 - sigma)


def match(places, wanted):
    shape = places.shape
    wanted = jnp.broadcast_to(wanted, shape).astype(jnp.int16)
    return jnp.where(places == wanted, jnp.ones(shape, BF), jnp.zeros(shape, BF))


def pick(rows, wanted):
    places = lax.broadcasted_iota(jnp.int32, (rows, wanted.shape[1]), 0).astype(jnp.int16)
    return match(places, wanted)


def counts_t(columns, first, entries):
    degree, rows = entries.shape
    places = (lax.broadcasted_iota(jnp.int32, (columns, rows), 0) + first).astype(jnp.int16)
    total = match(places, entries[0:1])
    for k in range(1, degree):
        total = total + match(places, entries[k : k + 1])
    return total


def side_swap(entries, rows, size, me):
    swapped = jnp.where(entries < rows + size, entries + size, entries - size)
    rim = (entries >= rows) & (entries < rows + 2 * size)
    return jnp.where(rim & (me % 2 == 1), swapped, entries)


def pair_order(lists, me):
    left, right = lists[0, 0:1], lists[0, 1:2]
    odd = me % 2
    return left + odd * (right - left), right + odd * (left - right)


def by_stage(x, devices):
    return (x % PLANE) * (devices // PLANE) + x // PLANE


def call(body, out_shapes, flops, *args, hbm=0, free=0, hbm_out=0, scratch=(), limit=VMEM_LIMIT):
    shapes = [jax.ShapeDtypeStruct(s, t) for s, t in out_shapes]
    size = sum(a.size * a.dtype.itemsize for a in args)
    size += sum(s.size * s.dtype.itemsize for s in shapes)
    size *= hbm == 0
    places = [pltpu.HBM] * hbm + [pltpu.VMEM] * (len(args) - hbm - free)
    places += [pl.ANY] * free
    out_places = [pltpu.HBM] * hbm_out + [pltpu.VMEM] * (len(shapes) - hbm_out)
    kept = len(args) - free
    inner = body if free == 0 else lambda *refs: body(*refs[:kept], *refs[len(args) :])
    return pl.pallas_call(
        inner,
        out_shape=shapes,
        in_specs=[pl.BlockSpec(memory_space=place) for place in places],
        out_specs=[pl.BlockSpec(memory_space=place) for place in out_places],
        scratch_shapes=list(scratch),
        compiler_params=pltpu.CompilerParams(vmem_limit_bytes=limit),
        cost_estimate=pl.CostEstimate(flops=flops, bytes_accessed=size, transcendentals=0),
    )(*args)


def copies_of(arrays):
    return [pltpu.VMEM(a.shape, a.dtype) for a in arrays]


def fetch(sources, targets, sems):
    copies = [pltpu.make_async_copy(s, t, sems.at[i]) for i, (s, t) in enumerate(zip(sources, targets))]
    for copy in copies:
        copy.start()
    return copies


def row_chunks(rows):
    step = rows // CHUNKS
    return [pl.ds(i * step, step) for i in range(CHUNKS)]


def grid_send(latent, lists, outer, inner, values, wanted, rows, sems):
    parts = row_chunks(latent.shape[0])
    copies = fetch([lists] + [latent.at[part] for part in parts], [wanted] + [values.at[part] for part in parts], sems)
    size = outer.shape[0]
    step = latent.shape[0] // CHUNKS
    copies[0].wait()
    listed = jnp.concatenate(pair_order(wanted, lax.axis_index("dom")), axis=1)
    chosen = pick(latent.shape[0], listed)
    total = 0.0
    for i, part in enumerate(parts):
        copies[i + 1].wait()
        total += t_mm(chosen[i * step : (i + 1) * step], values[part])
    rows[...] = total.astype(BF)
    sides = [rows.at[pl.ds(0, size)], rows.at[pl.ds(size, size)]]
    for copy in fetch(sides, [outer, inner], sems):
        copy.wait()


def encoder_local(entries, weight, latent, mesh, near, grid_own_t, grid_rim_t, slope, *, size):
    me = lax.axis_index("dom")
    rows = latent.shape[0]
    columns = side_swap(entries[...], rows, size, me)
    own = counts_t(rows, 0, columns)
    grid_own_t[...] = own
    grid_rim_t[...] = counts_t(2 * size, rows, columns)
    message, gradient = silu_pair(mm(latent[...], weight[...]))
    slope[...] = gradient.astype(BF)
    near[...] = mesh[...].astype(F32) + t_mm(own, message.astype(BF))


def list_tables(me, lists, far_lists, send, receive):
    rows = send.shape[0]
    size = lists.shape[2]
    cap, devices = far_lists.shape
    outer, inner = pair_order(lists, me)
    rim = [pick(rows, outer), pick(rows, inner)]
    for k in range(2):
        send[:, k * size : (k + 1) * size] = rim[k]
        receive[:, k * size : (k + 1) * size] = rim[k]
    partner = lax.broadcasted_iota(jnp.int32, (devices, devices * cap), 0)
    place = lax.broadcasted_iota(jnp.int32, (devices, devices * cap), 1)
    if devices == STAGED:
        x = partner ^ me
        send_place, receive_place = x * cap, by_stage(x, devices) * cap
    else:
        send_place, receive_place = partner * cap, partner * cap
    send_far = jnp.zeros((rows, devices * cap), F32)
    receive_far = jnp.zeros((rows, devices * cap), F32)
    for j in range(cap):
        chosen = pick(rows, far_lists[j : j + 1])
        send_far += mm(chosen, (place == send_place + j).astype(F32).astype(BF))
        receive_far += mm(chosen, (place == receive_place + j).astype(F32).astype(BF))
    send[:, 2 * size :] = send_far.astype(BF)
    receive[:, 2 * size :] = receive_far.astype(BF)


def mesh_tables(me, entries, own_t, forth_t, back_t, size, devices):
    rows = own_t.shape[0]
    slots = forth_t.shape[0] - 2 * size
    cap = slots // devices
    columns = side_swap(entries[...], rows, size, me)
    own_t[...] = counts_t(rows, 0, columns)
    rim = counts_t(2 * size, rows, columns)
    forth_t[: 2 * size] = rim
    back_t[: 2 * size] = rim
    far = jnp.maximum(columns - rows - 2 * size, 0)
    partner, slot = far // cap, far % cap
    if devices == STAGED:
        partner = partner ^ me
        send_place, receive_place = partner * cap + slot, by_stage(partner, devices) * cap + slot
    else:
        send_place, receive_place = far, far
    is_far = columns >= rows + 2 * size
    forth_t[2 * size :] = counts_t(slots, 0, jnp.where(is_far, receive_place, -1))
    back_t[2 * size :] = counts_t(slots, 0, jnp.where(is_far, send_place, -1))


def decoder_back(entries, cotangent, own_t, rim_t, near, outer, inner):
    me = lax.axis_index("dom")
    rows = near.shape[0]
    size = outer.shape[0]
    columns = side_swap(entries[...], rows, size, me)
    own = counts_t(rows, 0, columns)
    side = counts_t(2 * size, rows, columns)
    own_t[...] = own
    rim_t[...] = side
    grads = cotangent[...]
    near[...] = mm(own, grads)
    back = mm(side, grads).astype(BF)
    outer[...] = back[:size]
    inner[...] = back[size:]


def emit(outs, rows, size, extra=None):
    rows = rows.astype(BF)
    for k in range(2):
        outs[k][:size] = rows[k * size : (k + 1) * size]
        if extra is not None:
            outs[k][size:] = extra[k]
    far = rows[2 * size :]
    block = far.shape[0] // (len(outs) - 2)
    for m, out in enumerate(outs[2:]):
        out[...] = far[m * block : (m + 1) * block]


def arrived(ins, size):
    outer, inner = ins[:2]
    parts = [outer[:size], inner[:size]]
    if len(ins) > 3:
        third, second, own = ins[2:]
        parts += [own[...], inner[inner.shape[0] - own.shape[0] :], second[...], third[...]]
    else:
        parts += [ref[...] for ref in ins[2:]]
    return jnp.concatenate(parts, axis=0)


def shuffle(inner, own, *refs):
    columns = STAGED // PLANE
    parts = [own[...]] + [refs[Z_ORDER.index(m)][...] for m in range(1, columns)]
    rows = jnp.concatenate(parts, axis=0)
    outs = refs[columns - 1 :]
    count = rows.shape[0]
    cap = count // STAGED
    target = lax.broadcasted_iota(jnp.int32, (count, count), 0)
    source = lax.broadcasted_iota(jnp.int32, (count, count), 1)
    place, slot = target // cap, target % cap
    wanted = ((place % columns) * PLANE + place // columns) * cap + slot
    moved = mm((source == wanted).astype(F32).astype(BF), rows).astype(BF)
    block = columns * cap
    used = inner.shape[0]
    outs[1][:used] = inner[...]
    outs[1][used:] = moved[block : 2 * block]
    for k in (0, 2, 3):
        outs[k][...] = moved[k * block : (k + 1) * block]


def tables(entries, lists, far_lists, own_t, forth_t, back_t, send, receive, *, size, devices):
    me = lax.axis_index("dom")
    mesh_tables(me, entries, own_t, forth_t, back_t, size, devices)
    list_tables(me, lists, far_lists, send, receive)


def layer_local(hidden, own_t, weight, near, slope, *, layer, scale):
    state = hidden[...]
    value, gradient = silu_pair(mm(state, weight[layer]))
    slope[...] = gradient
    near[...] = state.astype(F32) + scale * t_mm(own_t[...], value.astype(BF))


def back_local(own_t, grad, near):
    near[...] = mm(own_t[...], grad[...])


def chosen_messages(send, state, weight):
    return silu_pair(mm(t_mm(send[...], state).astype(BF), weight))[0]


def first_hidden(near, rim_t, outer_in, inner_in, encoder, weight, send, hidden, *outs, size):
    incoming = silu_pair(mm(arrived([outer_in, inner_in], outer_in.shape[0]), encoder[...]))[0].astype(BF)
    state = (near[...] + t_mm(rim_t[...], incoming)).astype(BF)
    hidden[...] = state
    emit(outs, chosen_messages(send, state, weight[0]), size)


def next_hidden(near, forth_t, weight, send, outer_extra, inner_extra, *refs, ins, layer, scale, size):
    rows = arrived(refs[:ins], size)
    state = (near[...] + scale * t_mm(forth_t[...], rows)).astype(BF)
    refs[ins][...] = state
    emit(refs[ins + 1 :], chosen_messages(send, state, weight[layer]), size, (outer_extra[...], inner_extra[...]))


def turn(near, forth_t, weight, send, receive, back_t, back_near, *refs, ins, scale, size):
    rows = arrived(refs[:ins], size)
    message, grad = refs[ins : ins + 2]
    state = (near[...] + scale * t_mm(forth_t[...], rows)).astype(BF)
    value, gradient = silu_pair(mm(state, weight[...]))
    value = value.astype(BF)
    message[...] = value
    returned = jnp.concatenate([refs[0][size : 2 * size], refs[1][size : 2 * size]], axis=0)
    back = back_near[...] + mm(receive[:, : 2 * size], returned)
    change = mm_t((back * gradient).astype(BF), weight[...]).astype(BF)
    grad[...] = change
    rim = t_mm(send[:, : 2 * size], value).astype(BF)
    emit(refs[ins + 2 :], mm(back_t[...], change), size, (rim[:size], rim[size:]))


def layer_back(near, receive, rows, slope, weight, grad, scale):
    total = near[...] + mm(receive[...], rows)
    change = (total * scale * slope[...]).astype(BF)
    return (grad[...].astype(F32) + mm_t(change, weight)).astype(BF)


def middle_back(near, receive, slope, weight, grad, back_t, *refs, ins, layer, scale, size):
    rows = arrived(refs[:ins], size)
    change = layer_back(near, receive, rows, slope, weight[layer], grad, scale)
    refs[ins][...] = change
    emit(refs[ins + 1 :], mm(back_t[...], change), size)


def last_back(near, receive, slope, weight, grad, grid_rim_t, *refs, ins, scale):
    new_grad, outer, inner = refs[ins:]
    rows = arrived(refs[:ins], refs[0].shape[0])
    change = layer_back(near, receive, rows, slope, weight[0], grad, scale)
    new_grad[...] = change
    back = mm(grid_rim_t[...], change).astype(BF)
    outer[...] = back[: outer.shape[0]]
    inner[...] = back[outer.shape[0] :]


def decode_own(latent, own_t, message, base):
    base[...] = latent[...].astype(F32) + t_mm(own_t[...], message[...])


def decode_rim(base, rim_t, outer_in, inner_in, output, token):
    size = outer_in.shape[0] // 2
    incoming = jnp.concatenate([outer_in[size:], inner_in[size : 2 * size]], axis=0)
    output[...] = (base[...] + t_mm(rim_t[...], incoming)).astype(BF)
    token[...] = jnp.zeros(token.shape, F32)


def grid_local(own_t, grad, lists, slope, weight, cotangent, base, table, slope_rows, mesh_grad):
    me = lax.axis_index("dom")
    mesh_grad[...] = grad[...]
    rows = own_t.shape[0]
    size = lists.shape[2]
    for k, wanted in enumerate(pair_order(lists, me)):
        table[:, k * size : (k + 1) * size] = pick(rows, wanted)
    slope_rows[...] = t_mm(table[...], slope[...])
    change = (mm(own_t[...], grad[...]) * slope[...].astype(F32)).astype(BF)
    base[...] = cotangent[...].astype(F32) + mm_t(change, weight[...])


def grid_back(base, table, slope_rows, weight, outer_in, inner_in, output, staging, sems):
    returned = jnp.concatenate([outer_in[...], inner_in[...]], axis=0).astype(F32)
    change = mm_t((returned * slope_rows[...]).astype(BF), weight[...]).astype(BF)
    copies = []
    for i, part in enumerate(row_chunks(base.shape[0])):
        staging[part] = (base[part] + mm(table[part], change)).astype(BF)
        copies.append(pltpu.make_async_copy(staging.at[part], output.at[part], sems.at[i]))
        copies[-1].start()
    for copy in copies:
        copy.wait()


def toggle(value, bits):
    peers = lax.axis_size("dom")
    return lax.ppermute(value, "dom", [(i, i ^ bits) for i in range(peers)])


def across(value):
    peers = lax.axis_size("dom")
    pairs = [(i, (i + 1) % peers if i % 2 else (i - 1) % peers) for i in range(peers)]
    return lax.ppermute(value, "dom", pairs)


def exchange(outs, cap):
    width = outs[0].shape[1]
    if len(outs) == 3:
        outer, inner, far = outs
        peers = lax.axis_size("dom")
        blocks = far.reshape(peers, cap, width)
        blocks = lax.all_to_all(blocks, "dom", split_axis=0, concat_axis=0, tiled=True)
        return [across(outer), toggle(inner, 1), blocks.reshape(-1, width)]
    outer, inner, own, *rest = outs
    columns = STAGED // PLANE
    moved = [toggle(rest[m - 1], m * PLANE) for m in Z_ORDER]
    outer_in = across(outer)
    block = columns * cap
    blocks = call(
        shuffle,
        [((block, width), BF), ((inner.shape[0] + block, width), BF), ((block, width), BF), ((block, width), BF)],
        2 * (STAGED * cap) ** 2 * width,
        inner, own, *moved,
    )
    return [outer_in, toggle(blocks[1], 1), toggle(blocks[3], 3), toggle(blocks[2], 2), blocks[0]]


def on_device(
    grid_latent,
    mesh_latent,
    encoder_weight,
    processor_weights,
    decoder_weight,
    cotangent,
    grid_halo_rows,
    encoder_neighbours,
    halo_rows,
    far_sources,
    mesh_neighbours,
    decoder_neighbours,
):
    devices = lax.axis_size("dom")
    grid_rows, width = grid_latent.shape
    mesh_rows = mesh_latent.shape[0]
    ghalo = grid_halo_rows.shape[2]
    halo = halo_rows.shape[2]
    cap = far_sources.shape[2]
    slots = devices * cap
    listed = 2 * halo + slots
    scale = 1.0 / mesh_neighbours.shape[1]

    def square(rows, depth):
        return 2 * rows * depth * width

    def sends(per_side):
        stages = STAGED // PLANE if devices == STAGED else 1
        return [((per_side, width), BF)] * 2 + [((slots // stages, width), BF)] * stages

    state = ((mesh_rows, width), BF)
    total = ((mesh_rows, width), F32)
    rim = ((halo, width), BF)
    grid_rim = ((ghalo, width), BF)
    step = 3 * square(mesh_rows, width)

    outer, inner = call(
        grid_send,
        [grid_rim, grid_rim],
        64 * square(grid_rows, width),
        grid_latent, grid_halo_rows,
        hbm=2, hbm_out=2, limit=FIRST_LIMIT,
        scratch=copies_of([grid_latent, grid_halo_rows])
        + [pltpu.VMEM((2 * ghalo, width), BF), pltpu.SemaphoreType.DMA((CHUNKS + 1,))],
    )
    outer_in, inner_in = across(outer), toggle(inner, 1)

    own_t, forth_t, back_t, send, receive = call(
        functools.partial(tables, size=halo, devices=devices),
        [((mesh_rows, mesh_rows), BF)] + [((listed, mesh_rows), BF)] * 2 + [((mesh_rows, listed), BF)] * 2,
        64 * square(mesh_rows, mesh_rows),
        mesh_neighbours.T, halo_rows, far_sources[0].T,
    )
    _, latent, weight, mesh = lax.optimization_barrier((inner, grid_latent, encoder_weight, mesh_latent))
    near, grid_own_t, grid_rim_t, grid_slope = call(
        functools.partial(encoder_local, size=ghalo),
        [total, ((grid_rows, mesh_rows), BF), ((2 * ghalo, mesh_rows), BF), ((grid_rows, width), BF)],
        4 * square(grid_rows, width),
        encoder_neighbours.T, weight, latent, mesh,
    )

    hidden, *outs = call(
        functools.partial(first_hidden, size=halo),
        [state] + sends(halo),
        step,
        near, grid_rim_t, outer_in, inner_in, encoder_weight, processor_weights, send,
    )
    ins = exchange(outs, cap)
    near, slope_0 = call(
        functools.partial(layer_local, layer=0, scale=scale),
        [total, total],
        6 * square(mesh_rows, mesh_rows),
        hidden, own_t, processor_weights, ins[-1],
        free=1,
    )
    decoder_own_t, decoder_rim_t, decoder_near, outer_extra, inner_extra = call(
        decoder_back,
        [((mesh_rows, grid_rows), BF), ((2 * halo, grid_rows), BF), total, rim, rim],
        square(grid_rows, mesh_rows),
        decoder_neighbours.T, cotangent, ins[-1],
        free=1,
    )

    hidden, *outs = call(
        functools.partial(next_hidden, ins=len(ins), layer=1, scale=scale, size=halo),
        [state] + sends(2 * halo),
        step,
        near, forth_t, processor_weights, send, outer_extra, inner_extra, *ins,
    )
    ins = exchange(outs, cap)
    near, slope_1 = call(
        functools.partial(layer_local, layer=1, scale=scale),
        [total, total],
        6 * square(mesh_rows, mesh_rows),
        hidden, own_t, processor_weights, ins[-1],
        free=1,
    )

    message, grad, *outs = call(
        functools.partial(turn, ins=len(ins), scale=scale, size=halo),
        [state, state] + sends(2 * halo),
        2 * step,
        near, forth_t, decoder_weight, send, receive, back_t, decoder_near, *ins,
    )
    ins = exchange(outs, cap)
    (near,) = call(back_local, [total], 6 * square(mesh_rows, mesh_rows), own_t, grad)

    outer_decoder, inner_decoder = ins[:2]
    (near,) = call(back_local, [total], 6 * square(mesh_rows, mesh_rows), own_t, grad, ins[-1], free=1)
    (base,) = call(
        decode_own,
        [((grid_rows, width), F32)],
        square(grid_rows, mesh_rows),
        grid_latent, decoder_own_t, message, ins[-1],
        free=1,
    )

    grad, *outs = call(
        functools.partial(middle_back, ins=len(ins), layer=1, scale=scale, size=halo),
        [state] + sends(halo),
        step,
        near, receive, slope_1, processor_weights, grad, back_t, *ins, base,
        free=1,
    )
    ins = exchange(outs, cap)
    (near,) = call(back_local, [total], 6 * square(mesh_rows, mesh_rows), own_t, grad, ins[-1], free=1)
    output, token = call(
        decode_rim,
        [((grid_rows, width), BF), ((8, 128), F32)],
        square(grid_rows, 2 * halo),
        base, decoder_rim_t, outer_decoder, inner_decoder, ins[-1],
        free=1,
    )

    grad, outer, inner = call(
        functools.partial(last_back, ins=len(ins), scale=scale),
        [state, grid_rim, grid_rim],
        step,
        near, receive, slope_0, processor_weights, grad, grid_rim_t, *ins, token,
        free=1,
    )
    outer_in, inner_in = across(outer), toggle(inner, 1)
    base, table, slope_rows, mesh_grad = call(
        grid_local,
        [((grid_rows, width), F32), ((grid_rows, 2 * ghalo), BF), ((2 * ghalo, width), F32), state],
        square(mesh_rows, grid_rows) + square(grid_rows, width),
        grid_own_t, grad, grid_halo_rows, grid_slope, encoder_weight, cotangent,
    )
    (grid_grad,) = call(
        grid_back,
        [((grid_rows, width), BF)],
        square(grid_rows, 4 * ghalo),
        base, table, slope_rows, encoder_weight, outer_in, inner_in,
        hbm_out=1,
        scratch=[pltpu.VMEM((grid_rows, width), BF), pltpu.SemaphoreType.DMA((CHUNKS,))],
    )
    return (output, grid_grad, mesh_grad)


def solution(mesh):
    in_specs = (
        P(("groups", "dom"), None),
        P(("groups", "dom"), None),
        P(),
        P(),
        P(),
        P(("groups", "dom"), None),
        P("dom", None, None),
        P("dom", None),
        P("dom", None, None),
        P("dom", None, None),
        P("dom", None),
        P("dom", None),
    )
    out_specs = (P(("groups", "dom"), None), P(("groups", "dom"), None), P(("groups", "dom"), None))
    return jax.shard_map(
        on_device, mesh=mesh, in_specs=in_specs, out_specs=out_specs, check_vma=False
    )
```

```python
import functools

import jax
import jax.numpy as jnp
from jax import lax
from jax.experimental import pallas as pl
from jax.experimental.pallas import tpu as pltpu
from jax.sharding import PartitionSpec as P

BF = jnp.bfloat16
F32 = jnp.float32
VMEM_LIMIT = 24 * 1024 * 1024
FIRST_LIMIT = 107 * 512 * 1024
PLANE = 4
STAGED = 16
CHUNKS = 4
Z_ORDER = (2, 3, 1)


def mm(a, b):
    return jnp.dot(a, b, preferred_element_type=F32)


def mm_t(a, b):
    return lax.dot_general(a, b, (((1,), (1,)), ((), ())), preferred_element_type=F32)


def t_mm(a, b):
    return lax.dot_general(a, b, (((0,), (0,)), ((), ())), preferred_element_type=F32)


def silu_pair(value):
    sigma = 0.5 + 0.5 * jnp.tanh(0.5 * value)
    message = value * sigma
    return message, sigma + message * (1.0 - sigma)


def match(places, wanted):
    shape = places.shape
    wanted = jnp.broadcast_to(wanted, shape).astype(jnp.int16)
    return jnp.where(places == wanted, jnp.ones(shape, BF), jnp.zeros(shape, BF))


def pick(rows, wanted):
    places = lax.broadcasted_iota(jnp.int32, (rows, wanted.shape[1]), 0).astype(jnp.int16)
    return match(places, wanted)


def counts_t(columns, first, entries):
    degree, rows = entries.shape
    places = (lax.broadcasted_iota(jnp.int32, (columns, rows), 0) + first).astype(jnp.int16)
    total = match(places, entries[0:1])
    for k in range(1, degree):
        total = total + match(places, entries[k : k + 1])
    return total


def side_swap(entries, rows, size, me):
    swapped = jnp.where(entries < rows + size, entries + size, entries - size)
    rim = (entries >= rows) & (entries < rows + 2 * size)
    return jnp.where(rim & (me % 2 == 1), swapped, entries)


def pair_order(lists, me):
    left, right = lists[0, 0:1], lists[0, 1:2]
    odd = me % 2
    return left + odd * (right - left), right + odd * (left - right)


def by_stage(x, devices):
    return (x % PLANE) * (devices // PLANE) + x // PLANE


def call(body, out_shapes, flops, *args, hbm=0, free=0, hbm_out=0, scratch=(), limit=VMEM_LIMIT):
    shapes = [jax.ShapeDtypeStruct(s, t) for s, t in out_shapes]
    size = sum(a.size * a.dtype.itemsize for a in args)
    size += sum(s.size * s.dtype.itemsize for s in shapes)
    size *= hbm == 0
    places = [pltpu.HBM] * hbm + [pltpu.VMEM] * (len(args) - hbm - free)
    places += [pl.ANY] * free
    out_places = [pltpu.HBM] * hbm_out + [pltpu.VMEM] * (len(shapes) - hbm_out)
    kept = len(args) - free
    inner = body if free == 0 else lambda *refs: body(*refs[:kept], *refs[len(args) :])
    return pl.pallas_call(
        inner,
        out_shape=shapes,
        in_specs=[pl.BlockSpec(memory_space=place) for place in places],
        out_specs=[pl.BlockSpec(memory_space=place) for place in out_places],
        scratch_shapes=list(scratch),
        compiler_params=pltpu.CompilerParams(vmem_limit_bytes=limit),
        cost_estimate=pl.CostEstimate(flops=flops, bytes_accessed=size, transcendentals=0),
    )(*args)


def copies_of(arrays):
    return [pltpu.VMEM(a.shape, a.dtype) for a in arrays]


def fetch(sources, targets, sems):
    copies = [pltpu.make_async_copy(s, t, sems.at[i]) for i, (s, t) in enumerate(zip(sources, targets))]
    for copy in copies:
        copy.start()
    return copies


def row_chunks(rows):
    step = rows // CHUNKS
    return [pl.ds(i * step, step) for i in range(CHUNKS)]


def grid_send(latent, lists, outer, inner, values, sems):
    parts = row_chunks(latent.shape[0])
    copies = fetch([latent.at[part] for part in parts], [values.at[part] for part in parts], sems)
    size = outer.shape[0]
    step = latent.shape[0] // CHUNKS
    listed = jnp.concatenate(pair_order(lists, lax.axis_index("dom")), axis=1)
    chosen = pick(latent.shape[0], listed)
    rows = 0.0
    for i, part in enumerate(parts):
        copies[i].wait()
        rows += t_mm(chosen[i * step : (i + 1) * step], values[part])
    outer[...] = rows[:size].astype(BF)
    inner[...] = rows[size:].astype(BF)


def encoder_local(entries, weight, latent, mesh, near, grid_own_t, grid_rim_t, slope, *, size):
    me = lax.axis_index("dom")
    rows = latent.shape[0]
    columns = side_swap(entries[...], rows, size, me)
    own = counts_t(rows, 0, columns)
    grid_own_t[...] = own
    grid_rim_t[...] = counts_t(2 * size, rows, columns)
    message, gradient = silu_pair(mm(latent[...], weight[...]))
    slope[...] = gradient.astype(BF)
    near[...] = mesh[...].astype(F32) + t_mm(own, message.astype(BF))


def list_tables(me, lists, far_lists, send, receive):
    rows = send.shape[0]
    size = lists.shape[2]
    cap, devices = far_lists.shape
    outer, inner = pair_order(lists, me)
    rim = [pick(rows, outer), pick(rows, inner)]
    for k in range(2):
        send[:, k * size : (k + 1) * size] = rim[k]
        receive[:, k * size : (k + 1) * size] = rim[k]
    partner = lax.broadcasted_iota(jnp.int32, (devices, devices * cap), 0)
    place = lax.broadcasted_iota(jnp.int32, (devices, devices * cap), 1)
    if devices == STAGED:
        x = partner ^ me
        send_place, receive_place = x * cap, by_stage(x, devices) * cap
    else:
        send_place, receive_place = partner * cap, partner * cap
    send_far = jnp.zeros((rows, devices * cap), F32)
    receive_far = jnp.zeros((rows, devices * cap), F32)
    for j in range(cap):
        chosen = pick(rows, far_lists[j : j + 1])
        send_far += mm(chosen, (place == send_place + j).astype(F32).astype(BF))
        receive_far += mm(chosen, (place == receive_place + j).astype(F32).astype(BF))
    send[:, 2 * size :] = send_far.astype(BF)
    receive[:, 2 * size :] = receive_far.astype(BF)


def mesh_tables(me, entries, own_t, forth_t, back_t, size, devices):
    rows = own_t.shape[0]
    slots = forth_t.shape[0] - 2 * size
    cap = slots // devices
    columns = side_swap(entries[...], rows, size, me)
    own_t[...] = counts_t(rows, 0, columns)
    rim = counts_t(2 * size, rows, columns)
    forth_t[: 2 * size] = rim
    back_t[: 2 * size] = rim
    far = jnp.maximum(columns - rows - 2 * size, 0)
    partner, slot = far // cap, far % cap
    if devices == STAGED:
        partner = partner ^ me
        send_place, receive_place = partner * cap + slot, by_stage(partner, devices) * cap + slot
    else:
        send_place, receive_place = far, far
    is_far = columns >= rows + 2 * size
    forth_t[2 * size :] = counts_t(slots, 0, jnp.where(is_far, receive_place, -1))
    back_t[2 * size :] = counts_t(slots, 0, jnp.where(is_far, send_place, -1))


def decoder_back(entries, cotangent, own_t, rim_t, near, outer, inner):
    me = lax.axis_index("dom")
    rows = near.shape[0]
    size = outer.shape[0]
    columns = side_swap(entries[...], rows, size, me)
    own = counts_t(rows, 0, columns)
    side = counts_t(2 * size, rows, columns)
    own_t[...] = own
    rim_t[...] = side
    grads = cotangent[...]
    near[...] = mm(own, grads)
    back = mm(side, grads).astype(BF)
    outer[...] = back[:size]
    inner[...] = back[size:]


def emit(outs, rows, size, extra=None):
    rows = rows.astype(BF)
    for k in range(2):
        outs[k][:size] = rows[k * size : (k + 1) * size]
        if extra is not None:
            outs[k][size:] = extra[k]
    far = rows[2 * size :]
    block = far.shape[0] // (len(outs) - 2)
    for m, out in enumerate(outs[2:]):
        out[...] = far[m * block : (m + 1) * block]


def arrived(ins, size):
    outer, inner = ins[:2]
    parts = [outer[:size], inner[:size]]
    if len(ins) > 3:
        third, second, own = ins[2:]
        parts += [own[...], inner[inner.shape[0] - own.shape[0] :], second[...], third[...]]
    else:
        parts += [ref[...] for ref in ins[2:]]
    return jnp.concatenate(parts, axis=0)


def shuffle(inner, own, *refs):
    columns = STAGED // PLANE
    parts = [own[...]] + [refs[Z_ORDER.index(m)][...] for m in range(1, columns)]
    rows = jnp.concatenate(parts, axis=0)
    outs = refs[columns - 1 :]
    count = rows.shape[0]
    cap = count // STAGED
    target = lax.broadcasted_iota(jnp.int32, (count, count), 0)
    source = lax.broadcasted_iota(jnp.int32, (count, count), 1)
    place, slot = target // cap, target % cap
    wanted = ((place % columns) * PLANE + place // columns) * cap + slot
    moved = mm((source == wanted).astype(F32).astype(BF), rows).astype(BF)
    block = columns * cap
    used = inner.shape[0]
    outs[1][:used] = inner[...]
    outs[1][used:] = moved[block : 2 * block]
    for k in (0, 2, 3):
        outs[k][...] = moved[k * block : (k + 1) * block]


def tables(entries, lists, far_lists, own_t, forth_t, back_t, send, receive, *, size, devices):
    me = lax.axis_index("dom")
    mesh_tables(me, entries, own_t, forth_t, back_t, size, devices)
    list_tables(me, lists, far_lists, send, receive)


def layer_local(hidden, own_t, weight, near, slope, *, layer, scale):
    state = hidden[...]
    value, gradient = silu_pair(mm(state, weight[layer]))
    slope[...] = gradient
    near[...] = state.astype(F32) + scale * t_mm(own_t[...], value.astype(BF))


def back_local(own_t, grad, near):
    near[...] = mm(own_t[...], grad[...])


def chosen_messages(send, state, weight):
    return silu_pair(mm(t_mm(send[...], state).astype(BF), weight))[0]


def first_hidden(near, rim_t, outer_in, inner_in, encoder, weight, send, hidden, *outs, size):
    incoming = silu_pair(mm(arrived([outer_in, inner_in], outer_in.shape[0]), encoder[...]))[0].astype(BF)
    state = (near[...] + t_mm(rim_t[...], incoming)).astype(BF)
    hidden[...] = state
    emit(outs, chosen_messages(send, state, weight[0]), size)


def next_hidden(near, forth_t, weight, send, outer_extra, inner_extra, *refs, ins, layer, scale, size):
    rows = arrived(refs[:ins], size)
    state = (near[...] + scale * t_mm(forth_t[...], rows)).astype(BF)
    refs[ins][...] = state
    emit(refs[ins + 1 :], chosen_messages(send, state, weight[layer]), size, (outer_extra[...], inner_extra[...]))


def turn(near, forth_t, weight, send, receive, back_t, back_near, *refs, ins, scale, size):
    rows = arrived(refs[:ins], size)
    message, grad = refs[ins : ins + 2]
    state = (near[...] + scale * t_mm(forth_t[...], rows)).astype(BF)
    value, gradient = silu_pair(mm(state, weight[...]))
    value = value.astype(BF)
    message[...] = value
    returned = jnp.concatenate([refs[0][size : 2 * size], refs[1][size : 2 * size]], axis=0)
    back = back_near[...] + mm(receive[:, : 2 * size], returned)
    change = mm_t((back * gradient).astype(BF), weight[...]).astype(BF)
    grad[...] = change
    rim = t_mm(send[:, : 2 * size], value).astype(BF)
    emit(refs[ins + 2 :], mm(back_t[...], change), size, (rim[:size], rim[size:]))


def layer_back(near, receive, rows, slope, weight, grad, scale):
    total = near[...] + mm(receive[...], rows)
    change = (total * scale * slope[...]).astype(BF)
    return (grad[...].astype(F32) + mm_t(change, weight)).astype(BF)


def middle_back(near, receive, slope, weight, grad, back_t, *refs, ins, layer, scale, size):
    rows = arrived(refs[:ins], size)
    change = layer_back(near, receive, rows, slope, weight[layer], grad, scale)
    refs[ins][...] = change
    emit(refs[ins + 1 :], mm(back_t[...], change), size)


def last_back(near, receive, slope, weight, grad, grid_rim_t, *refs, ins, scale):
    new_grad, outer, inner = refs[ins:]
    rows = arrived(refs[:ins], refs[0].shape[0])
    change = layer_back(near, receive, rows, slope, weight[0], grad, scale)
    new_grad[...] = change
    back = mm(grid_rim_t[...], change).astype(BF)
    outer[...] = back[: outer.shape[0]]
    inner[...] = back[outer.shape[0] :]


def decode_own(latent, own_t, message, base):
    base[...] = latent[...].astype(F32) + t_mm(own_t[...], message[...])


def decode_rim(base, rim_t, outer_in, inner_in, output, token):
    size = outer_in.shape[0] // 2
    incoming = jnp.concatenate([outer_in[size:], inner_in[size : 2 * size]], axis=0)
    output[...] = (base[...] + t_mm(rim_t[...], incoming)).astype(BF)
    token[...] = jnp.zeros(token.shape, F32)


def grid_local(own_t, grad, lists, slope, weight, cotangent, base, table, slope_rows, mesh_grad):
    me = lax.axis_index("dom")
    mesh_grad[...] = grad[...]
    rows = own_t.shape[0]
    size = lists.shape[2]
    for k, wanted in enumerate(pair_order(lists, me)):
        table[:, k * size : (k + 1) * size] = pick(rows, wanted)
    slope_rows[...] = t_mm(table[...], slope[...])
    change = (mm(own_t[...], grad[...]) * slope[...].astype(F32)).astype(BF)
    base[...] = cotangent[...].astype(F32) + mm_t(change, weight[...])


def grid_back(base, table, slope_rows, weight, outer_in, inner_in, output, staging, sems):
    returned = jnp.concatenate([outer_in[...], inner_in[...]], axis=0).astype(F32)
    change = mm_t((returned * slope_rows[...]).astype(BF), weight[...]).astype(BF)
    copies = []
    for i, part in enumerate(row_chunks(base.shape[0])):
        staging[part] = (base[part] + mm(table[part], change)).astype(BF)
        copies.append(pltpu.make_async_copy(staging.at[part], output.at[part], sems.at[i]))
        copies[-1].start()
    for copy in copies:
        copy.wait()


def toggle(value, bits):
    peers = lax.axis_size("dom")
    return lax.ppermute(value, "dom", [(i, i ^ bits) for i in range(peers)])


def across(value):
    peers = lax.axis_size("dom")
    pairs = [(i, (i + 1) % peers if i % 2 else (i - 1) % peers) for i in range(peers)]
    return lax.ppermute(value, "dom", pairs)


def exchange(outs, cap):
    width = outs[0].shape[1]
    if len(outs) == 3:
        outer, inner, far = outs
        peers = lax.axis_size("dom")
        blocks = far.reshape(peers, cap, width)
        blocks = lax.all_to_all(blocks, "dom", split_axis=0, concat_axis=0, tiled=True)
        return [across(outer), toggle(inner, 1), blocks.reshape(-1, width)]
    outer, inner, own, *rest = outs
    columns = STAGED // PLANE
    moved = [toggle(rest[m - 1], m * PLANE) for m in Z_ORDER]
    outer_in = across(outer)
    block = columns * cap
    blocks = call(
        shuffle,
        [((block, width), BF), ((inner.shape[0] + block, width), BF), ((block, width), BF), ((block, width), BF)],
        2 * (STAGED * cap) ** 2 * width,
        inner, own, *moved,
    )
    return [outer_in, toggle(blocks[1], 1), toggle(blocks[3], 3), toggle(blocks[2], 2), blocks[0]]


def on_device(
    grid_latent,
    mesh_latent,
    encoder_weight,
    processor_weights,
    decoder_weight,
    cotangent,
    grid_halo_rows,
    encoder_neighbours,
    halo_rows,
    far_sources,
    mesh_neighbours,
    decoder_neighbours,
):
    devices = lax.axis_size("dom")
    grid_rows, width = grid_latent.shape
    mesh_rows = mesh_latent.shape[0]
    ghalo = grid_halo_rows.shape[2]
    halo = halo_rows.shape[2]
    cap = far_sources.shape[2]
    slots = devices * cap
    listed = 2 * halo + slots
    scale = 1.0 / mesh_neighbours.shape[1]

    def square(rows, depth):
        return 2 * rows * depth * width

    def sends(per_side):
        stages = STAGED // PLANE if devices == STAGED else 1
        return [((per_side, width), BF)] * 2 + [((slots // stages, width), BF)] * stages

    state = ((mesh_rows, width), BF)
    total = ((mesh_rows, width), F32)
    rim = ((halo, width), BF)
    grid_rim = ((ghalo, width), BF)
    step = 3 * square(mesh_rows, width)

    outer, inner = call(
        grid_send,
        [grid_rim, grid_rim],
        64 * square(grid_rows, width),
        grid_latent, grid_halo_rows,
        hbm=1, limit=FIRST_LIMIT,
        scratch=copies_of([grid_latent]) + [pltpu.SemaphoreType.DMA((CHUNKS,))],
    )
    outer_in, inner_in = across(outer), toggle(inner, 1)

    own_t, forth_t, back_t, send, receive = call(
        functools.partial(tables, size=halo, devices=devices),
        [((mesh_rows, mesh_rows), BF)] + [((listed, mesh_rows), BF)] * 2 + [((mesh_rows, listed), BF)] * 2,
        64 * square(mesh_rows, mesh_rows),
        mesh_neighbours.T, halo_rows, far_sources[0].T,
    )
    _, latent, weight, mesh = lax.optimization_barrier((inner, grid_latent, encoder_weight, mesh_latent))
    near, grid_own_t, grid_rim_t, grid_slope = call(
        functools.partial(encoder_local, size=ghalo),
        [total, ((grid_rows, mesh_rows), BF), ((2 * ghalo, mesh_rows), BF), ((grid_rows, width), BF)],
        4 * square(grid_rows, width),
        encoder_neighbours.T, weight, latent, mesh,
    )

    hidden, *outs = call(
        functools.partial(first_hidden, size=halo),
        [state] + sends(halo),
        step,
        near, grid_rim_t, outer_in, inner_in, encoder_weight, processor_weights, send,
    )
    ins = exchange(outs, cap)
    near, slope_0 = call(
        functools.partial(layer_local, layer=0, scale=scale),
        [total, total],
        6 * square(mesh_rows, mesh_rows),
        hidden, own_t, processor_weights, ins[-1],
        free=1,
    )
    decoder_own_t, decoder_rim_t, decoder_near, outer_extra, inner_extra = call(
        decoder_back,
        [((mesh_rows, grid_rows), BF), ((2 * halo, grid_rows), BF), total, rim, rim],
        square(grid_rows, mesh_rows),
        decoder_neighbours.T, cotangent, ins[-1],
        free=1,
    )

    hidden, *outs = call(
        functools.partial(next_hidden, ins=len(ins), layer=1, scale=scale, size=halo),
        [state] + sends(2 * halo),
        step,
        near, forth_t, processor_weights, send, outer_extra, inner_extra, *ins,
    )
    ins = exchange(outs, cap)
    near, slope_1 = call(
        functools.partial(layer_local, layer=1, scale=scale),
        [total, total],
        6 * square(mesh_rows, mesh_rows),
        hidden, own_t, processor_weights, ins[-1],
        free=1,
    )

    message, grad, *outs = call(
        functools.partial(turn, ins=len(ins), scale=scale, size=halo),
        [state, state] + sends(2 * halo),
        2 * step,
        near, forth_t, decoder_weight, send, receive, back_t, decoder_near, *ins,
    )
    ins = exchange(outs, cap)
    (near,) = call(back_local, [total], 6 * square(mesh_rows, mesh_rows), own_t, grad)

    outer_decoder, inner_decoder = ins[:2]
    (near,) = call(back_local, [total], 6 * square(mesh_rows, mesh_rows), own_t, grad, ins[-1], free=1)
    (base,) = call(
        decode_own,
        [((grid_rows, width), F32)],
        square(grid_rows, mesh_rows),
        grid_latent, decoder_own_t, message, ins[-1],
        free=1,
    )

    grad, *outs = call(
        functools.partial(middle_back, ins=len(ins), layer=1, scale=scale, size=halo),
        [state] + sends(halo),
        step,
        near, receive, slope_1, processor_weights, grad, back_t, *ins, base,
        free=1,
    )
    ins = exchange(outs, cap)
    (near,) = call(back_local, [total], 6 * square(mesh_rows, mesh_rows), own_t, grad, ins[-1], free=1)
    output, token = call(
        decode_rim,
        [((grid_rows, width), BF), ((8, 128), F32)],
        square(grid_rows, 2 * halo),
        base, decoder_rim_t, outer_decoder, inner_decoder, ins[-1],
        free=1,
    )

    grad, outer, inner = call(
        functools.partial(last_back, ins=len(ins), scale=scale),
        [state, grid_rim, grid_rim],
        step,
        near, receive, slope_0, processor_weights, grad, grid_rim_t, *ins, token,
        free=1,
    )
    outer_in, inner_in = across(outer), toggle(inner, 1)
    base, table, slope_rows, mesh_grad = call(
        grid_local,
        [((grid_rows, width), F32), ((grid_rows, 2 * ghalo), BF), ((2 * ghalo, width), F32), state],
        square(mesh_rows, grid_rows) + square(grid_rows, width),
        grid_own_t, grad, grid_halo_rows, grid_slope, encoder_weight, cotangent,
    )
    (grid_grad,) = call(
        grid_back,
        [((grid_rows, width), BF)],
        square(grid_rows, 4 * ghalo),
        base, table, slope_rows, encoder_weight, outer_in, inner_in,
        hbm_out=1,
        scratch=[pltpu.VMEM((grid_rows, width), BF), pltpu.SemaphoreType.DMA((CHUNKS,))],
    )
    return (output, grid_grad, mesh_grad)


def solution(mesh):
    in_specs = (
        P(("groups", "dom"), None),
        P(("groups", "dom"), None),
        P(),
        P(),
        P(),
        P(("groups", "dom"), None),
        P("dom", None, None),
        P("dom", None),
        P("dom", None, None),
        P("dom", None, None),
        P("dom", None),
        P("dom", None),
    )
    out_specs = (P(("groups", "dom"), None), P(("groups", "dom"), None), P(("groups", "dom"), None))
    return jax.shard_map(
        on_device, mesh=mesh, in_specs=in_specs, out_specs=out_specs, check_vma=False
    )
```

```python
import functools

import jax
import jax.numpy as jnp
from jax import lax
from jax.experimental import pallas as pl
from jax.experimental.pallas import tpu as pltpu
from jax.sharding import PartitionSpec as P

BF = jnp.bfloat16
F32 = jnp.float32
VMEM_LIMIT = 24 * 1024 * 1024
FIRST_LIMIT = 107 * 512 * 1024
PLANE = 4
STAGED = 16
CHUNKS = 4
Z_ORDER = (2, 3, 1)


def mm(a, b):
    return jnp.dot(a, b, preferred_element_type=F32)


def mm_t(a, b):
    return lax.dot_general(a, b, (((1,), (1,)), ((), ())), preferred_element_type=F32)


def t_mm(a, b):
    return lax.dot_general(a, b, (((0,), (0,)), ((), ())), preferred_element_type=F32)


def silu_pair(value):
    sigma = 0.5 + 0.5 * jnp.tanh(0.5 * value)
    message = value * sigma
    return message, sigma + message * (1.0 - sigma)


def match(places, wanted):
    shape = places.shape
    wanted = jnp.broadcast_to(wanted, shape).astype(jnp.int16)
    return jnp.where(places == wanted, jnp.ones(shape, BF), jnp.zeros(shape, BF))


def pick(rows, wanted):
    places = lax.broadcasted_iota(jnp.int32, (rows, wanted.shape[1]), 0).astype(jnp.int16)
    return match(places, wanted)


def counts_t(columns, first, entries):
    degree, rows = entries.shape
    places = (lax.broadcasted_iota(jnp.int32, (columns, rows), 0) + first).astype(jnp.int16)
    total = match(places, entries[0:1])
    for k in range(1, degree):
        total = total + match(places, entries[k : k + 1])
    return total


def side_swap(entries, rows, size, me):
    swapped = jnp.where(entries < rows + size, entries + size, entries - size)
    rim = (entries >= rows) & (entries < rows + 2 * size)
    return jnp.where(rim & (me % 2 == 1), swapped, entries)


def pair_order(lists, me):
    left, right = lists[0, 0:1], lists[0, 1:2]
    odd = me % 2
    return left + odd * (right - left), right + odd * (left - right)


def by_stage(x, devices):
    return (x % PLANE) * (devices // PLANE) + x // PLANE


def call(body, out_shapes, flops, *args, hbm=0, free=0, hbm_out=0, scratch=(), limit=VMEM_LIMIT):
    shapes = [jax.ShapeDtypeStruct(s, t) for s, t in out_shapes]
    size = sum(a.size * a.dtype.itemsize for a in args)
    size += sum(s.size * s.dtype.itemsize for s in shapes)
    size *= hbm == 0
    places = [pltpu.HBM] * hbm + [pltpu.VMEM] * (len(args) - hbm - free)
    places += [pl.ANY] * free
    out_places = [pltpu.HBM] * hbm_out + [pltpu.VMEM] * (len(shapes) - hbm_out)
    kept = len(args) - free
    inner = body if free == 0 else lambda *refs: body(*refs[:kept], *refs[len(args) :])
    return pl.pallas_call(
        inner,
        out_shape=shapes,
        in_specs=[pl.BlockSpec(memory_space=place) for place in places],
        out_specs=[pl.BlockSpec(memory_space=place) for place in out_places],
        scratch_shapes=list(scratch),
        compiler_params=pltpu.CompilerParams(vmem_limit_bytes=limit),
        cost_estimate=pl.CostEstimate(flops=flops, bytes_accessed=size, transcendentals=0),
    )(*args)


def copies_of(arrays):
    return [pltpu.VMEM(a.shape, a.dtype) for a in arrays]


def fetch(sources, targets, sems):
    copies = [pltpu.make_async_copy(s, t, sems.at[i]) for i, (s, t) in enumerate(zip(sources, targets))]
    for copy in copies:
        copy.start()
    return copies


def row_chunks(rows):
    step = rows // CHUNKS
    return [pl.ds(i * step, step) for i in range(CHUNKS)]


def grid_send(latent, lists, outer, inner, values, sems):
    parts = row_chunks(latent.shape[0])
    copies = fetch([latent.at[part] for part in parts], [values.at[part] for part in parts], sems)
    size = outer.shape[0]
    step = latent.shape[0] // CHUNKS
    listed = jnp.concatenate(pair_order(lists, lax.axis_index("dom")), axis=1)
    chosen = pick(latent.shape[0], listed)
    rows = 0.0
    for i, part in enumerate(parts):
        copies[i].wait()
        rows += t_mm(chosen[i * step : (i + 1) * step], values[part])
    outer[...] = rows[:size].astype(BF)
    inner[...] = rows[size:].astype(BF)


def encoder_local(entries, weight, latent, mesh, near, grid_own_t, grid_rim_t, slope, *, size):
    me = lax.axis_index("dom")
    rows = latent.shape[0]
    columns = side_swap(entries[...], rows, size, me)
    own = counts_t(rows, 0, columns)
    grid_own_t[...] = own
    grid_rim_t[...] = counts_t(2 * size, rows, columns)
    message, gradient = silu_pair(mm(latent[...], weight[...]))
    slope[...] = gradient.astype(BF)
    near[...] = mesh[...].astype(F32) + t_mm(own, message.astype(BF))


def list_tables(me, lists, far_lists, send, receive):
    rows = send.shape[0]
    size = lists.shape[2]
    cap, devices = far_lists.shape
    outer, inner = pair_order(lists, me)
    rim = [pick(rows, outer), pick(rows, inner)]
    for k in range(2):
        send[:, k * size : (k + 1) * size] = rim[k]
        receive[:, k * size : (k + 1) * size] = rim[k]
    partner = lax.broadcasted_iota(jnp.int32, (devices, devices * cap), 0)
    place = lax.broadcasted_iota(jnp.int32, (devices, devices * cap), 1)
    if devices == STAGED:
        x = partner ^ me
        send_place, receive_place = x * cap, by_stage(x, devices) * cap
    else:
        send_place, receive_place = partner * cap, partner * cap
    send_far = jnp.zeros((rows, devices * cap), F32)
    receive_far = jnp.zeros((rows, devices * cap), F32)
    for j in range(cap):
        chosen = pick(rows, far_lists[j : j + 1])
        send_far += mm(chosen, (place == send_place + j).astype(F32).astype(BF))
        receive_far += mm(chosen, (place == receive_place + j).astype(F32).astype(BF))
    send[:, 2 * size :] = send_far.astype(BF)
    receive[:, 2 * size :] = receive_far.astype(BF)


def mesh_tables(me, entries, own_t, forth_t, back_t, size, devices):
    rows = own_t.shape[0]
    slots = forth_t.shape[0] - 2 * size
    cap = slots // devices
    columns = side_swap(entries[...], rows, size, me)
    own_t[...] = counts_t(rows, 0, columns)
    rim = counts_t(2 * size, rows, columns)
    forth_t[: 2 * size] = rim
    back_t[: 2 * size] = rim
    far = jnp.maximum(columns - rows - 2 * size, 0)
    partner, slot = far // cap, far % cap
    if devices == STAGED:
        partner = partner ^ me
        send_place, receive_place = partner * cap + slot, by_stage(partner, devices) * cap + slot
    else:
        send_place, receive_place = far, far
    is_far = columns >= rows + 2 * size
    forth_t[2 * size :] = counts_t(slots, 0, jnp.where(is_far, receive_place, -1))
    back_t[2 * size :] = counts_t(slots, 0, jnp.where(is_far, send_place, -1))


def decoder_back(entries, cotangent, own_t, rim_t, near, outer, inner):
    me = lax.axis_index("dom")
    rows = near.shape[0]
    size = outer.shape[0]
    columns = side_swap(entries[...], rows, size, me)
    own = counts_t(rows, 0, columns)
    side = counts_t(2 * size, rows, columns)
    own_t[...] = own
    rim_t[...] = side
    grads = cotangent[...]
    near[...] = mm(own, grads)
    back = mm(side, grads).astype(BF)
    outer[...] = back[:size]
    inner[...] = back[size:]


def emit(outs, rows, size, extra=None):
    rows = rows.astype(BF)
    for k in range(2):
        outs[k][:size] = rows[k * size : (k + 1) * size]
        if extra is not None:
            outs[k][size:] = extra[k]
    far = rows[2 * size :]
    block = far.shape[0] // (len(outs) - 2)
    for m, out in enumerate(outs[2:]):
        out[...] = far[m * block : (m + 1) * block]


def arrived(ins, size):
    outer, inner = ins[:2]
    parts = [outer[:size], inner[:size]]
    if len(ins) > 3:
        third, second, own = ins[2:]
        parts += [own[...], inner[inner.shape[0] - own.shape[0] :], second[...], third[...]]
    else:
        parts += [ref[...] for ref in ins[2:]]
    return jnp.concatenate(parts, axis=0)


def shuffle(inner, own, *refs):
    columns = STAGED // PLANE
    parts = [own[...]] + [refs[Z_ORDER.index(m)][...] for m in range(1, columns)]
    rows = jnp.concatenate(parts, axis=0)
    outs = refs[columns - 1 :]
    count = rows.shape[0]
    cap = count // STAGED
    target = lax.broadcasted_iota(jnp.int32, (count, count), 0)
    source = lax.broadcasted_iota(jnp.int32, (count, count), 1)
    place, slot = target // cap, target % cap
    wanted = ((place % columns) * PLANE + place // columns) * cap + slot
    moved = mm((source == wanted).astype(F32).astype(BF), rows).astype(BF)
    block = columns * cap
    used = inner.shape[0]
    outs[1][:used] = inner[...]
    outs[1][used:] = moved[block : 2 * block]
    for k in (0, 2, 3):
        outs[k][...] = moved[k * block : (k + 1) * block]


def tables(entries, lists, far_lists, own_t, forth_t, back_t, send, receive, *, size, devices):
    me = lax.axis_index("dom")
    mesh_tables(me, entries, own_t, forth_t, back_t, size, devices)
    list_tables(me, lists, far_lists, send, receive)


def layer_local(hidden, own_t, weight, near, slope, *, layer, scale):
    state = hidden[...]
    value, gradient = silu_pair(mm(state, weight[layer]))
    slope[...] = gradient
    near[...] = state.astype(F32) + scale * t_mm(own_t[...], value.astype(BF))


def back_local(own_t, grad, near):
    near[...] = mm(own_t[...], grad[...])


def chosen_messages(send, state, weight):
    return silu_pair(mm(t_mm(send[...], state).astype(BF), weight))[0]


def first_hidden(near, rim_t, outer_in, inner_in, encoder, weight, send, hidden, *outs, size):
    incoming = silu_pair(mm(arrived([outer_in, inner_in], outer_in.shape[0]), encoder[...]))[0].astype(BF)
    state = (near[...] + t_mm(rim_t[...], incoming)).astype(BF)
    hidden[...] = state
    emit(outs, chosen_messages(send, state, weight[0]), size)


def next_hidden(near, forth_t, weight, send, outer_extra, inner_extra, *refs, ins, layer, scale, size):
    rows = arrived(refs[:ins], size)
    state = (near[...] + scale * t_mm(forth_t[...], rows)).astype(BF)
    refs[ins][...] = state
    emit(refs[ins + 1 :], chosen_messages(send, state, weight[layer]), size, (outer_extra[...], inner_extra[...]))


def turn(near, forth_t, weight, send, receive, back_t, back_near, *refs, ins, scale, size):
    rows = arrived(refs[:ins], size)
    message, grad = refs[ins : ins + 2]
    state = (near[...] + scale * t_mm(forth_t[...], rows)).astype(BF)
    value, gradient = silu_pair(mm(state, weight[...]))
    value = value.astype(BF)
    message[...] = value
    returned = jnp.concatenate([refs[0][size : 2 * size], refs[1][size : 2 * size]], axis=0)
    back = back_near[...] + mm(receive[:, : 2 * size], returned)
    change = mm_t((back * gradient).astype(BF), weight[...]).astype(BF)
    grad[...] = change
    rim = t_mm(send[:, : 2 * size], value).astype(BF)
    emit(refs[ins + 2 :], mm(back_t[...], change), size, (rim[:size], rim[size:]))


def layer_back(near, receive, rows, slope, weight, grad, scale):
    total = near[...] + mm(receive[...], rows)
    change = (total * scale * slope[...]).astype(BF)
    return (grad[...].astype(F32) + mm_t(change, weight)).astype(BF)


def middle_back(near, receive, slope, weight, grad, back_t, *refs, ins, layer, scale, size):
    rows = arrived(refs[:ins], size)
    change = layer_back(near, receive, rows, slope, weight[layer], grad, scale)
    refs[ins][...] = change
    emit(refs[ins + 1 :], mm(back_t[...], change), size)


def last_back(near, receive, slope, weight, grad, grid_rim_t, *refs, ins, scale):
    new_grad, outer, inner = refs[ins:]
    rows = arrived(refs[:ins], refs[0].shape[0])
    change = layer_back(near, receive, rows, slope, weight[0], grad, scale)
    new_grad[...] = change
    back = mm(grid_rim_t[...], change).astype(BF)
    outer[...] = back[: outer.shape[0]]
    inner[...] = back[outer.shape[0] :]


def decode_own(latent, own_t, message, base):
    base[...] = latent[...].astype(F32) + t_mm(own_t[...], message[...])


def decode_rim(base, rim_t, outer_in, inner_in, output, token):
    size = outer_in.shape[0] // 2
    incoming = jnp.concatenate([outer_in[size:], inner_in[size : 2 * size]], axis=0)
    output[...] = (base[...] + t_mm(rim_t[...], incoming)).astype(BF)
    token[...] = jnp.zeros(token.shape, F32)


def grid_local(own_t, grad, lists, slope, weight, cotangent, base, table, slope_rows, mesh_grad):
    me = lax.axis_index("dom")
    mesh_grad[...] = grad[...]
    rows = own_t.shape[0]
    size = lists.shape[2]
    for k, wanted in enumerate(pair_order(lists, me)):
        table[:, k * size : (k + 1) * size] = pick(rows, wanted)
    slope_rows[...] = t_mm(table[...], slope[...])
    change = (mm(own_t[...], grad[...]) * slope[...].astype(F32)).astype(BF)
    base[...] = cotangent[...].astype(F32) + mm_t(change, weight[...])


def grid_back(base, table, slope_rows, weight, outer_in, inner_in, output, staging, sems):
    returned = jnp.concatenate([outer_in[...], inner_in[...]], axis=0).astype(F32)
    change = mm_t((returned * slope_rows[...]).astype(BF), weight[...]).astype(BF)
    copies = []
    for i, part in enumerate(row_chunks(base.shape[0])):
        staging[part] = (base[part] + mm(table[part], change)).astype(BF)
        copies.append(pltpu.make_async_copy(staging.at[part], output.at[part], sems.at[i]))
        copies[-1].start()
    for copy in copies:
        copy.wait()


def toggle(value, bits):
    peers = lax.axis_size("dom")
    return lax.ppermute(value, "dom", [(i, i ^ bits) for i in range(peers)])


def across(value):
    peers = lax.axis_size("dom")
    pairs = [(i, (i + 1) % peers if i % 2 else (i - 1) % peers) for i in range(peers)]
    return lax.ppermute(value, "dom", pairs)


def exchange(outs, cap):
    width = outs[0].shape[1]
    if len(outs) == 3:
        outer, inner, far = outs
        peers = lax.axis_size("dom")
        blocks = far.reshape(peers, cap, width)
        blocks = lax.all_to_all(blocks, "dom", split_axis=0, concat_axis=0, tiled=True)
        return [across(outer), toggle(inner, 1), blocks.reshape(-1, width)]
    outer, inner, own, *rest = outs
    columns = STAGED // PLANE
    moved = [toggle(rest[m - 1], m * PLANE) for m in Z_ORDER]
    outer_in = across(outer)
    block = columns * cap
    blocks = call(
        shuffle,
        [((block, width), BF), ((inner.shape[0] + block, width), BF), ((block, width), BF), ((block, width), BF)],
        2 * (STAGED * cap) ** 2 * width,
        inner, own, *moved,
    )
    return [outer_in, toggle(blocks[1], 1), toggle(blocks[3], 3), toggle(blocks[2], 2), blocks[0]]


def on_device(
    grid_latent,
    mesh_latent,
    encoder_weight,
    processor_weights,
    decoder_weight,
    cotangent,
    grid_halo_rows,
    encoder_neighbours,
    halo_rows,
    far_sources,
    mesh_neighbours,
    decoder_neighbours,
):
    devices = lax.axis_size("dom")
    grid_rows, width = grid_latent.shape
    mesh_rows = mesh_latent.shape[0]
    ghalo = grid_halo_rows.shape[2]
    halo = halo_rows.shape[2]
    cap = far_sources.shape[2]
    slots = devices * cap
    listed = 2 * halo + slots
    scale = 1.0 / mesh_neighbours.shape[1]

    def square(rows, depth):
        return 2 * rows * depth * width

    def sends(per_side):
        stages = STAGED // PLANE if devices == STAGED else 1
        return [((per_side, width), BF)] * 2 + [((slots // stages, width), BF)] * stages

    state = ((mesh_rows, width), BF)
    total = ((mesh_rows, width), F32)
    rim = ((halo, width), BF)
    grid_rim = ((ghalo, width), BF)
    step = 3 * square(mesh_rows, width)

    outer, inner = call(
        grid_send,
        [grid_rim, grid_rim],
        64 * square(grid_rows, width),
        grid_latent, grid_halo_rows,
        hbm=1, limit=FIRST_LIMIT,
        scratch=copies_of([grid_latent]) + [pltpu.SemaphoreType.DMA((CHUNKS,))],
    )
    outer_in, inner_in = across(outer), toggle(inner, 1)

    own_t, forth_t, back_t, send, receive = call(
        functools.partial(tables, size=halo, devices=devices),
        [((mesh_rows, mesh_rows), BF)] + [((listed, mesh_rows), BF)] * 2 + [((mesh_rows, listed), BF)] * 2,
        64 * square(mesh_rows, mesh_rows),
        mesh_neighbours.T, halo_rows, far_sources[0].T,
    )
    _, latent, weight, mesh = lax.optimization_barrier((inner, grid_latent, encoder_weight, mesh_latent))
    near, grid_own_t, grid_rim_t, grid_slope = call(
        functools.partial(encoder_local, size=ghalo),
        [total, ((grid_rows, mesh_rows), BF), ((2 * ghalo, mesh_rows), BF), ((grid_rows, width), BF)],
        4 * square(grid_rows, width),
        encoder_neighbours.T, weight, latent, mesh,
    )

    hidden, *outs = call(
        functools.partial(first_hidden, size=halo),
        [state] + sends(halo),
        step,
        near, grid_rim_t, outer_in, inner_in, encoder_weight, processor_weights, send,
    )
    ins = exchange(outs, cap)
    near, slope_0 = call(
        functools.partial(layer_local, layer=0, scale=scale),
        [total, total],
        4 * square(mesh_rows, mesh_rows),
        hidden, own_t, processor_weights, ins[-1],
        free=1,
    )
    decoder_own_t, decoder_rim_t, decoder_near, outer_extra, inner_extra = call(
        decoder_back,
        [((mesh_rows, grid_rows), BF), ((2 * halo, grid_rows), BF), total, rim, rim],
        square(grid_rows, mesh_rows),
        decoder_neighbours.T, cotangent, ins[-1],
        free=1,
    )

    hidden, *outs = call(
        functools.partial(next_hidden, ins=len(ins), layer=1, scale=scale, size=halo),
        [state] + sends(2 * halo),
        step,
        near, forth_t, processor_weights, send, outer_extra, inner_extra, *ins,
    )
    ins = exchange(outs, cap)
    near, slope_1 = call(
        functools.partial(layer_local, layer=1, scale=scale),
        [total, total],
        6 * square(mesh_rows, mesh_rows),
        hidden, own_t, processor_weights, ins[-1],
        free=1,
    )

    message, grad, *outs = call(
        functools.partial(turn, ins=len(ins), scale=scale, size=halo),
        [state, state] + sends(2 * halo),
        2 * step,
        near, forth_t, decoder_weight, send, receive, back_t, decoder_near, *ins,
    )
    ins = exchange(outs, cap)
    (near,) = call(back_local, [total], 6 * square(mesh_rows, mesh_rows), own_t, grad)

    outer_decoder, inner_decoder = ins[:2]
    (near,) = call(back_local, [total], 6 * square(mesh_rows, mesh_rows), own_t, grad, ins[-1], free=1)
    (base,) = call(
        decode_own,
        [((grid_rows, width), F32)],
        square(grid_rows, mesh_rows),
        grid_latent, decoder_own_t, message, ins[-1],
        free=1,
    )

    grad, *outs = call(
        functools.partial(middle_back, ins=len(ins), layer=1, scale=scale, size=halo),
        [state] + sends(halo),
        step,
        near, receive, slope_1, processor_weights, grad, back_t, *ins, base,
        free=1,
    )
    ins = exchange(outs, cap)
    (near,) = call(back_local, [total], 6 * square(mesh_rows, mesh_rows), own_t, grad, ins[-1], free=1)
    output, token = call(
        decode_rim,
        [((grid_rows, width), BF), ((8, 128), F32)],
        square(grid_rows, 2 * halo),
        base, decoder_rim_t, outer_decoder, inner_decoder, ins[-1],
        free=1,
    )

    grad, outer, inner = call(
        functools.partial(last_back, ins=len(ins), scale=scale),
        [state, grid_rim, grid_rim],
        step,
        near, receive, slope_0, processor_weights, grad, grid_rim_t, *ins, token,
        free=1,
    )
    outer_in, inner_in = across(outer), toggle(inner, 1)
    base, table, slope_rows, mesh_grad = call(
        grid_local,
        [((grid_rows, width), F32), ((grid_rows, 2 * ghalo), BF), ((2 * ghalo, width), F32), state],
        square(mesh_rows, grid_rows) + square(grid_rows, width),
        grid_own_t, grad, grid_halo_rows, grid_slope, encoder_weight, cotangent,
    )
    (grid_grad,) = call(
        grid_back,
        [((grid_rows, width), BF)],
        square(grid_rows, 4 * ghalo),
        base, table, slope_rows, encoder_weight, outer_in, inner_in,
        hbm_out=1,
        scratch=[pltpu.VMEM((grid_rows, width), BF), pltpu.SemaphoreType.DMA((CHUNKS,))],
    )
    return (output, grid_grad, mesh_grad)


def solution(mesh):
    in_specs = (
        P(("groups", "dom"), None),
        P(("groups", "dom"), None),
        P(),
        P(),
        P(),
        P(("groups", "dom"), None),
        P("dom", None, None),
        P("dom", None),
        P("dom", None, None),
        P("dom", None, None),
        P("dom", None),
        P("dom", None),
    )
    out_specs = (P(("groups", "dom"), None), P(("groups", "dom"), None), P(("groups", "dom"), None))
    return jax.shard_map(
        on_device, mesh=mesh, in_specs=in_specs, out_specs=out_specs, check_vma=False
    )
```

```python
import functools

import jax
import jax.numpy as jnp
from jax import lax
from jax.experimental import pallas as pl
from jax.experimental.pallas import tpu as pltpu
from jax.sharding import PartitionSpec as P

BF = jnp.bfloat16
F32 = jnp.float32
VMEM_LIMIT = 24 * 1024 * 1024
FIRST_LIMIT = 107 * 512 * 1024
PLANE = 4
STAGED = 16
CHUNKS = 8
Z_ORDER = (2, 3, 1)


def mm(a, b):
    return jnp.dot(a, b, preferred_element_type=F32)


def mm_t(a, b):
    return lax.dot_general(a, b, (((1,), (1,)), ((), ())), preferred_element_type=F32)


def t_mm(a, b):
    return lax.dot_general(a, b, (((0,), (0,)), ((), ())), preferred_element_type=F32)


def silu_pair(value):
    sigma = 0.5 + 0.5 * jnp.tanh(0.5 * value)
    message = value * sigma
    return message, sigma + message * (1.0 - sigma)


def match(places, wanted):
    shape = places.shape
    wanted = jnp.broadcast_to(wanted, shape).astype(jnp.int16)
    return jnp.where(places == wanted, jnp.ones(shape, BF), jnp.zeros(shape, BF))


def pick(rows, wanted):
    places = lax.broadcasted_iota(jnp.int32, (rows, wanted.shape[1]), 0).astype(jnp.int16)
    return match(places, wanted)


def counts_t(columns, first, entries):
    degree, rows = entries.shape
    places = (lax.broadcasted_iota(jnp.int32, (columns, rows), 0) + first).astype(jnp.int16)
    total = match(places, entries[0:1])
    for k in range(1, degree):
        total = total + match(places, entries[k : k + 1])
    return total


def side_swap(entries, rows, size, me):
    swapped = jnp.where(entries < rows + size, entries + size, entries - size)
    rim = (entries >= rows) & (entries < rows + 2 * size)
    return jnp.where(rim & (me % 2 == 1), swapped, entries)


def pair_order(lists, me):
    left, right = lists[0, 0:1], lists[0, 1:2]
    odd = me % 2
    return left + odd * (right - left), right + odd * (left - right)


def by_stage(x, devices):
    return (x % PLANE) * (devices // PLANE) + x // PLANE


def call(body, out_shapes, flops, *args, hbm=0, free=0, hbm_out=0, scratch=(), limit=VMEM_LIMIT):
    shapes = [jax.ShapeDtypeStruct(s, t) for s, t in out_shapes]
    size = sum(a.size * a.dtype.itemsize for a in args)
    size += sum(s.size * s.dtype.itemsize for s in shapes)
    size *= hbm == 0
    places = [pltpu.HBM] * hbm + [pltpu.VMEM] * (len(args) - hbm - free)
    places += [pl.ANY] * free
    out_places = [pltpu.HBM] * hbm_out + [pltpu.VMEM] * (len(shapes) - hbm_out)
    kept = len(args) - free
    inner = body if free == 0 else lambda *refs: body(*refs[:kept], *refs[len(args) :])
    return pl.pallas_call(
        inner,
        out_shape=shapes,
        in_specs=[pl.BlockSpec(memory_space=place) for place in places],
        out_specs=[pl.BlockSpec(memory_space=place) for place in out_places],
        scratch_shapes=list(scratch),
        compiler_params=pltpu.CompilerParams(vmem_limit_bytes=limit),
        cost_estimate=pl.CostEstimate(flops=flops, bytes_accessed=size, transcendentals=0),
    )(*args)


def copies_of(arrays):
    return [pltpu.VMEM(a.shape, a.dtype) for a in arrays]


def fetch(sources, targets, sems):
    copies = [pltpu.make_async_copy(s, t, sems.at[i]) for i, (s, t) in enumerate(zip(sources, targets))]
    for copy in copies:
        copy.start()
    return copies


def row_chunks(rows):
    step = rows // CHUNKS
    return [pl.ds(i * step, step) for i in range(CHUNKS)]


def grid_send(latent, lists, outer, inner, values, sems):
    parts = row_chunks(latent.shape[0])
    copies = fetch([latent.at[part] for part in parts], [values.at[part] for part in parts], sems)
    size = outer.shape[0]
    step = latent.shape[0] // CHUNKS
    listed = jnp.concatenate(pair_order(lists, lax.axis_index("dom")), axis=1)
    chosen = pick(latent.shape[0], listed)
    rows = 0.0
    for i, part in enumerate(parts):
        copies[i].wait()
        rows += t_mm(chosen[i * step : (i + 1) * step], values[part])
    outer[...] = rows[:size].astype(BF)
    inner[...] = rows[size:].astype(BF)


def encoder_local(entries, weight, latent, mesh, near, grid_own_t, grid_rim_t, slope, *, size):
    me = lax.axis_index("dom")
    rows = latent.shape[0]
    columns = side_swap(entries[...], rows, size, me)
    own = counts_t(rows, 0, columns)
    grid_own_t[...] = own
    grid_rim_t[...] = counts_t(2 * size, rows, columns)
    message, gradient = silu_pair(mm(latent[...], weight[...]))
    slope[...] = gradient.astype(BF)
    near[...] = mesh[...].astype(F32) + t_mm(own, message.astype(BF))


def list_tables(me, lists, far_lists, send, receive):
    rows = send.shape[0]
    size = lists.shape[2]
    cap, devices = far_lists.shape
    outer, inner = pair_order(lists, me)
    rim = [pick(rows, outer), pick(rows, inner)]
    for k in range(2):
        send[:, k * size : (k + 1) * size] = rim[k]
        receive[:, k * size : (k + 1) * size] = rim[k]
    partner = lax.broadcasted_iota(jnp.int32, (devices, devices * cap), 0)
    place = lax.broadcasted_iota(jnp.int32, (devices, devices * cap), 1)
    if devices == STAGED:
        x = partner ^ me
        send_place, receive_place = x * cap, by_stage(x, devices) * cap
    else:
        send_place, receive_place = partner * cap, partner * cap
    send_far = jnp.zeros((rows, devices * cap), F32)
    receive_far = jnp.zeros((rows, devices * cap), F32)
    for j in range(cap):
        chosen = pick(rows, far_lists[j : j + 1])
        send_far += mm(chosen, (place == send_place + j).astype(F32).astype(BF))
        receive_far += mm(chosen, (place == receive_place + j).astype(F32).astype(BF))
    send[:, 2 * size :] = send_far.astype(BF)
    receive[:, 2 * size :] = receive_far.astype(BF)


def mesh_tables(me, entries, own_t, forth_t, back_t, size, devices):
    rows = own_t.shape[0]
    slots = forth_t.shape[0] - 2 * size
    cap = slots // devices
    columns = side_swap(entries[...], rows, size, me)
    own_t[...] = counts_t(rows, 0, columns)
    rim = counts_t(2 * size, rows, columns)
    forth_t[: 2 * size] = rim
    back_t[: 2 * size] = rim
    far = jnp.maximum(columns - rows - 2 * size, 0)
    partner, slot = far // cap, far % cap
    if devices == STAGED:
        partner = partner ^ me
        send_place, receive_place = partner * cap + slot, by_stage(partner, devices) * cap + slot
    else:
        send_place, receive_place = far, far
    is_far = columns >= rows + 2 * size
    forth_t[2 * size :] = counts_t(slots, 0, jnp.where(is_far, receive_place, -1))
    back_t[2 * size :] = counts_t(slots, 0, jnp.where(is_far, send_place, -1))


def decoder_back(entries, cotangent, own_t, rim_t, near, outer, inner):
    me = lax.axis_index("dom")
    rows = near.shape[0]
    size = outer.shape[0]
    columns = side_swap(entries[...], rows, size, me)
    own = counts_t(rows, 0, columns)
    side = counts_t(2 * size, rows, columns)
    own_t[...] = own
    rim_t[...] = side
    grads = cotangent[...]
    near[...] = mm(own, grads)
    back = mm(side, grads).astype(BF)
    outer[...] = back[:size]
    inner[...] = back[size:]


def emit(outs, rows, size, extra=None):
    rows = rows.astype(BF)
    for k in range(2):
        outs[k][:size] = rows[k * size : (k + 1) * size]
        if extra is not None:
            outs[k][size:] = extra[k]
    far = rows[2 * size :]
    block = far.shape[0] // (len(outs) - 2)
    for m, out in enumerate(outs[2:]):
        out[...] = far[m * block : (m + 1) * block]


def arrived(ins, size):
    outer, inner = ins[:2]
    parts = [outer[:size], inner[:size]]
    if len(ins) > 3:
        third, second, own = ins[2:]
        parts += [own[...], inner[inner.shape[0] - own.shape[0] :], second[...], third[...]]
    else:
        parts += [ref[...] for ref in ins[2:]]
    return jnp.concatenate(parts, axis=0)


def shuffle(inner, own, *refs):
    columns = STAGED // PLANE
    parts = [own[...]] + [refs[Z_ORDER.index(m)][...] for m in range(1, columns)]
    rows = jnp.concatenate(parts, axis=0)
    outs = refs[columns - 1 :]
    count = rows.shape[0]
    cap = count // STAGED
    target = lax.broadcasted_iota(jnp.int32, (count, count), 0)
    source = lax.broadcasted_iota(jnp.int32, (count, count), 1)
    place, slot = target // cap, target % cap
    wanted = ((place % columns) * PLANE + place // columns) * cap + slot
    moved = mm((source == wanted).astype(F32).astype(BF), rows).astype(BF)
    block = columns * cap
    used = inner.shape[0]
    outs[1][:used] = inner[...]
    outs[1][used:] = moved[block : 2 * block]
    for k in (0, 2, 3):
        outs[k][...] = moved[k * block : (k + 1) * block]


def tables(entries, lists, far_lists, own_t, forth_t, back_t, send, receive, *, size, devices):
    me = lax.axis_index("dom")
    mesh_tables(me, entries, own_t, forth_t, back_t, size, devices)
    list_tables(me, lists, far_lists, send, receive)


def layer_local(hidden, own_t, weight, near, slope, *, layer, scale):
    state = hidden[...]
    value, gradient = silu_pair(mm(state, weight[layer]))
    slope[...] = gradient
    near[...] = state.astype(F32) + scale * t_mm(own_t[...], value.astype(BF))


def back_local(own_t, grad, near):
    near[...] = mm(own_t[...], grad[...])


def chosen_messages(send, state, weight):
    return silu_pair(mm(t_mm(send[...], state).astype(BF), weight))[0]


def first_hidden(near, rim_t, outer_in, inner_in, encoder, weight, send, hidden, *outs, size):
    incoming = silu_pair(mm(arrived([outer_in, inner_in], outer_in.shape[0]), encoder[...]))[0].astype(BF)
    state = (near[...] + t_mm(rim_t[...], incoming)).astype(BF)
    hidden[...] = state
    emit(outs, chosen_messages(send, state, weight[0]), size)


def next_hidden(near, forth_t, weight, send, outer_extra, inner_extra, *refs, ins, layer, scale, size):
    rows = arrived(refs[:ins], size)
    state = (near[...] + scale * t_mm(forth_t[...], rows)).astype(BF)
    refs[ins][...] = state
    emit(refs[ins + 1 :], chosen_messages(send, state, weight[layer]), size, (outer_extra[...], inner_extra[...]))


def turn(near, forth_t, weight, send, receive, back_t, back_near, *refs, ins, scale, size):
    rows = arrived(refs[:ins], size)
    message, grad = refs[ins : ins + 2]
    state = (near[...] + scale * t_mm(forth_t[...], rows)).astype(BF)
    value, gradient = silu_pair(mm(state, weight[...]))
    value = value.astype(BF)
    message[...] = value
    returned = jnp.concatenate([refs[0][size : 2 * size], refs[1][size : 2 * size]], axis=0)
    back = back_near[...] + mm(receive[:, : 2 * size], returned)
    change = mm_t((back * gradient).astype(BF), weight[...]).astype(BF)
    grad[...] = change
    rim = t_mm(send[:, : 2 * size], value).astype(BF)
    emit(refs[ins + 2 :], mm(back_t[...], change), size, (rim[:size], rim[size:]))


def layer_back(near, receive, rows, slope, weight, grad, scale):
    total = near[...] + mm(receive[...], rows)
    change = (total * scale * slope[...]).astype(BF)
    return (grad[...].astype(F32) + mm_t(change, weight)).astype(BF)


def middle_back(near, receive, slope, weight, grad, back_t, *refs, ins, layer, scale, size):
    rows = arrived(refs[:ins], size)
    change = layer_back(near, receive, rows, slope, weight[layer], grad, scale)
    refs[ins][...] = change
    emit(refs[ins + 1 :], mm(back_t[...], change), size)


def last_back(near, receive, slope, weight, grad, grid_rim_t, *refs, ins, scale):
    new_grad, outer, inner = refs[ins:]
    rows = arrived(refs[:ins], refs[0].shape[0])
    change = layer_back(near, receive, rows, slope, weight[0], grad, scale)
    new_grad[...] = change
    back = mm(grid_rim_t[...], change).astype(BF)
    outer[...] = back[: outer.shape[0]]
    inner[...] = back[outer.shape[0] :]


def decode_own(latent, own_t, message, base):
    base[...] = latent[...].astype(F32) + t_mm(own_t[...], message[...])


def decode_rim(base, rim_t, outer_in, inner_in, output, token):
    size = outer_in.shape[0] // 2
    incoming = jnp.concatenate([outer_in[size:], inner_in[size : 2 * size]], axis=0)
    output[...] = (base[...] + t_mm(rim_t[...], incoming)).astype(BF)
    token[...] = jnp.zeros(token.shape, F32)


def grid_local(own_t, grad, lists, slope, weight, cotangent, base, table, slope_rows, mesh_grad):
    me = lax.axis_index("dom")
    mesh_grad[...] = grad[...]
    rows = own_t.shape[0]
    size = lists.shape[2]
    for k, wanted in enumerate(pair_order(lists, me)):
        table[:, k * size : (k + 1) * size] = pick(rows, wanted)
    slope_rows[...] = t_mm(table[...], slope[...])
    change = (mm(own_t[...], grad[...]) * slope[...].astype(F32)).astype(BF)
    base[...] = cotangent[...].astype(F32) + mm_t(change, weight[...])


def grid_back(base, table, slope_rows, weight, outer_in, inner_in, output, staging, sems):
    returned = jnp.concatenate([outer_in[...], inner_in[...]], axis=0).astype(F32)
    change = mm_t((returned * slope_rows[...]).astype(BF), weight[...]).astype(BF)
    copies = []
    for i, part in enumerate(row_chunks(base.shape[0])):
        staging[part] = (base[part] + mm(table[part], change)).astype(BF)
        copies.append(pltpu.make_async_copy(staging.at[part], output.at[part], sems.at[i]))
        copies[-1].start()
    for copy in copies:
        copy.wait()


def toggle(value, bits):
    peers = lax.axis_size("dom")
    return lax.ppermute(value, "dom", [(i, i ^ bits) for i in range(peers)])


def across(value):
    peers = lax.axis_size("dom")
    pairs = [(i, (i + 1) % peers if i % 2 else (i - 1) % peers) for i in range(peers)]
    return lax.ppermute(value, "dom", pairs)


def exchange(outs, cap):
    width = outs[0].shape[1]
    if len(outs) == 3:
        outer, inner, far = outs
        peers = lax.axis_size("dom")
        blocks = far.reshape(peers, cap, width)
        blocks = lax.all_to_all(blocks, "dom", split_axis=0, concat_axis=0, tiled=True)
        return [across(outer), toggle(inner, 1), blocks.reshape(-1, width)]
    outer, inner, own, *rest = outs
    columns = STAGED // PLANE
    moved = [toggle(rest[m - 1], m * PLANE) for m in Z_ORDER]
    outer_in = across(outer)
    block = columns * cap
    blocks = call(
        shuffle,
        [((block, width), BF), ((inner.shape[0] + block, width), BF), ((block, width), BF), ((block, width), BF)],
        2 * (STAGED * cap) ** 2 * width,
        inner, own, *moved,
    )
    return [outer_in, toggle(blocks[1], 1), toggle(blocks[3], 3), toggle(blocks[2], 2), blocks[0]]


def on_device(
    grid_latent,
    mesh_latent,
    encoder_weight,
    processor_weights,
    decoder_weight,
    cotangent,
    grid_halo_rows,
    encoder_neighbours,
    halo_rows,
    far_sources,
    mesh_neighbours,
    decoder_neighbours,
):
    devices = lax.axis_size("dom")
    grid_rows, width = grid_latent.shape
    mesh_rows = mesh_latent.shape[0]
    ghalo = grid_halo_rows.shape[2]
    halo = halo_rows.shape[2]
    cap = far_sources.shape[2]
    slots = devices * cap
    listed = 2 * halo + slots
    scale = 1.0 / mesh_neighbours.shape[1]

    def square(rows, depth):
        return 2 * rows * depth * width

    def sends(per_side):
        stages = STAGED // PLANE if devices == STAGED else 1
        return [((per_side, width), BF)] * 2 + [((slots // stages, width), BF)] * stages

    state = ((mesh_rows, width), BF)
    total = ((mesh_rows, width), F32)
    rim = ((halo, width), BF)
    grid_rim = ((ghalo, width), BF)
    step = 3 * square(mesh_rows, width)

    outer, inner = call(
        grid_send,
        [grid_rim, grid_rim],
        64 * square(grid_rows, width),
        grid_latent, grid_halo_rows,
        hbm=1, limit=FIRST_LIMIT,
        scratch=copies_of([grid_latent]) + [pltpu.SemaphoreType.DMA((CHUNKS,))],
    )
    outer_in, inner_in = across(outer), toggle(inner, 1)

    own_t, forth_t, back_t, send, receive = call(
        functools.partial(tables, size=halo, devices=devices),
        [((mesh_rows, mesh_rows), BF)] + [((listed, mesh_rows), BF)] * 2 + [((mesh_rows, listed), BF)] * 2,
        64 * square(mesh_rows, mesh_rows),
        mesh_neighbours.T, halo_rows, far_sources[0].T,
    )
    _, latent, weight, mesh = lax.optimization_barrier((inner, grid_latent, encoder_weight, mesh_latent))
    near, grid_own_t, grid_rim_t, grid_slope = call(
        functools.partial(encoder_local, size=ghalo),
        [total, ((grid_rows, mesh_rows), BF), ((2 * ghalo, mesh_rows), BF), ((grid_rows, width), BF)],
        4 * square(grid_rows, width),
        encoder_neighbours.T, weight, latent, mesh,
    )

    hidden, *outs = call(
        functools.partial(first_hidden, size=halo),
        [state] + sends(halo),
        step,
        near, grid_rim_t, outer_in, inner_in, encoder_weight, processor_weights, send,
    )
    ins = exchange(outs, cap)
    near, slope_0 = call(
        functools.partial(layer_local, layer=0, scale=scale),
        [total, total],
        4 * square(mesh_rows, mesh_rows),
        hidden, own_t, processor_weights, ins[-1],
        free=1,
    )
    decoder_own_t, decoder_rim_t, decoder_near, outer_extra, inner_extra = call(
        decoder_back,
        [((mesh_rows, grid_rows), BF), ((2 * halo, grid_rows), BF), total, rim, rim],
        square(grid_rows, mesh_rows),
        decoder_neighbours.T, cotangent, ins[-1],
        free=1,
    )

    hidden, *outs = call(
        functools.partial(next_hidden, ins=len(ins), layer=1, scale=scale, size=halo),
        [state] + sends(2 * halo),
        step,
        near, forth_t, processor_weights, send, outer_extra, inner_extra, *ins,
    )
    ins = exchange(outs, cap)
    near, slope_1 = call(
        functools.partial(layer_local, layer=1, scale=scale),
        [total, total],
        6 * square(mesh_rows, mesh_rows),
        hidden, own_t, processor_weights, ins[-1],
        free=1,
    )

    message, grad, *outs = call(
        functools.partial(turn, ins=len(ins), scale=scale, size=halo),
        [state, state] + sends(2 * halo),
        2 * step,
        near, forth_t, decoder_weight, send, receive, back_t, decoder_near, *ins,
    )
    ins = exchange(outs, cap)
    (near,) = call(back_local, [total], 6 * square(mesh_rows, mesh_rows), own_t, grad)

    outer_decoder, inner_decoder = ins[:2]
    (near,) = call(back_local, [total], 6 * square(mesh_rows, mesh_rows), own_t, grad, ins[-1], free=1)
    (base,) = call(
        decode_own,
        [((grid_rows, width), F32)],
        square(grid_rows, mesh_rows),
        grid_latent, decoder_own_t, message, ins[-1],
        free=1,
    )

    grad, *outs = call(
        functools.partial(middle_back, ins=len(ins), layer=1, scale=scale, size=halo),
        [state] + sends(halo),
        step,
        near, receive, slope_1, processor_weights, grad, back_t, *ins, base,
        free=1,
    )
    ins = exchange(outs, cap)
    (near,) = call(back_local, [total], 6 * square(mesh_rows, mesh_rows), own_t, grad, ins[-1], free=1)
    output, token = call(
        decode_rim,
        [((grid_rows, width), BF), ((8, 128), F32)],
        square(grid_rows, 2 * halo),
        base, decoder_rim_t, outer_decoder, inner_decoder, ins[-1],
        free=1,
    )

    grad, outer, inner = call(
        functools.partial(last_back, ins=len(ins), scale=scale),
        [state, grid_rim, grid_rim],
        step,
        near, receive, slope_0, processor_weights, grad, grid_rim_t, *ins, token,
        free=1,
    )
    outer_in, inner_in = across(outer), toggle(inner, 1)
    base, table, slope_rows, mesh_grad = call(
        grid_local,
        [((grid_rows, width), F32), ((grid_rows, 2 * ghalo), BF), ((2 * ghalo, width), F32), state],
        square(mesh_rows, grid_rows) + square(grid_rows, width),
        grid_own_t, grad, grid_halo_rows, grid_slope, encoder_weight, cotangent,
    )
    (grid_grad,) = call(
        grid_back,
        [((grid_rows, width), BF)],
        square(grid_rows, 4 * ghalo),
        base, table, slope_rows, encoder_weight, outer_in, inner_in,
        hbm_out=1,
        scratch=[pltpu.VMEM((grid_rows, width), BF), pltpu.SemaphoreType.DMA((CHUNKS,))],
    )
    return (output, grid_grad, mesh_grad)


def solution(mesh):
    in_specs = (
        P(("groups", "dom"), None),
        P(("groups", "dom"), None),
        P(),
        P(),
        P(),
        P(("groups", "dom"), None),
        P("dom", None, None),
        P("dom", None),
        P("dom", None, None),
        P("dom", None, None),
        P("dom", None),
        P("dom", None),
    )
    out_specs = (P(("groups", "dom"), None), P(("groups", "dom"), None), P(("groups", "dom"), None))
    return jax.shard_map(
        on_device, mesh=mesh, in_specs=in_specs, out_specs=out_specs, check_vma=False
    )
```
